32 devices in a mesh: section: 2 (over core), ctx: 4 (over z), tensor: 4 (over y, x).
Axes of the slice: x: 2, y: 2, z: 4, core: 2. Of those that a mesh axis runs over, the one named last changes fastest.
Arguments:
- tokens: bfloat16 [4, 1024, 1536], P(None, 'ctx'), may hold values from -6 to 6
- cotangent: bfloat16 [4, 1024, 1536], P(None, 'ctx'), may hold values from -6 to 6
- seg_ids: int32 [4, 1024], replicated, may hold values from 0 to 1, as said below
- norm_gain: bfloat16 [2, 1536], P('section'), may hold values from 0.099609375 to 1.8984375
- in_zx: bfloat16 [2, 1536, 2, 3072], P('section', 'ctx', None, 'tensor'), may hold values from -0.15625 to 0.15625
- in_bc: bfloat16 [2, 1536, 256], P('section', 'ctx'), may hold values from -0.15625 to 0.15625
- in_dt: bfloat16 [2, 1536, 48], P('section', 'ctx', 'tensor'), may hold values from -0.15625 to 0.15625
- conv_x: bfloat16 [2, 4, 3072], P('section', None, 'tensor'), may hold values from -3 to 3
- conv_xb: bfloat16 [2, 3072], P('section', 'tensor'), may hold values from -3 to 3
- conv_bc: bfloat16 [2, 4, 256], P('section'), may hold values from -3 to 3
- conv_bcb: bfloat16 [2, 256], P('section'), may hold values from -3 to 3
- dt_bias: float32 [2, 48], P('section', 'tensor'), may hold values from -3 to 0
- a_log: float32 [2, 48], P('section', 'tensor'), may hold values from -12 to -1
- skip_gain: float32 [2, 48], P('section', 'tensor'), may hold values from 0.5 to 1.5
- gate_gain: bfloat16 [2, 3072], P('section', 'tensor'), may hold values from 0.099609375 to 1.8984375
- out_w: bfloat16 [2, 3072, 1536], P('section', 'tensor', 'ctx'), may hold values from -0.109375 to 0.109375
Outputs:
- section_outputs: bfloat16 [2, 4, 1024, 1536], P('section', None, 'ctx')
- input_grads: float32 [2, 4, 1024, 1536], P('section', None, 'ctx')
- grad_norm_gain: float32 [2, 1536], P('section')
- grad_in_zx: float32 [2, 1536, 2, 3072], P('section', 'ctx', None, 'tensor')
- grad_in_bc: float32 [2, 1536, 256], P('section', 'ctx')
- grad_in_dt: float32 [2, 1536, 48], P('section', 'ctx', 'tensor')
- grad_conv_x: float32 [2, 4, 3072], P('section', None, 'tensor')
- grad_conv_xb: float32 [2, 3072], P('section', 'tensor')
- grad_conv_bc: float32 [2, 4, 256], P('section')
- grad_conv_bcb: float32 [2, 256], P('section')
- grad_dt_bias: float32 [2, 48], P('section', 'tensor')
- grad_a_log: float32 [2, 48], P('section', 'tensor')
- grad_skip_gain: float32 [2, 48], P('section', 'tensor')
- grad_gate_gain: float32 [2, 3072], P('section', 'tensor')
- grad_out_w: float32 [2, 3072, 1536], P('section', 'tensor', 'ctx')
The draws below stay inside these ranges and needn't reach their ends.
Inputs may be any that keep to these rules, and one draw needn't show every extreme that they name: `seg_ids`: ids never fall along each micro-batch's 1024 tokens and start at 0 in each; equal ids mark one document. One micro-batch is a single document; in each other one, every aligned block of 512 tokens but the first holds exactly one document start, so its ids run from 0 to 1.
All inputs are finite; a program needn't handle non-finite values.
Results may differ from the reference program's by a relative error of at most 0.0131.
The reference program's roundings to bfloat16 on the way count: a program that leaves them out, or rounds other values in their place, can miss the bound.
Values may be sent and summed in bfloat16 or wider, within the bound.
No kernel may reach another device: no remote copies, remote signals or barrier semaphores. Data moves between devices by JAX's collectives and lax.ppermute only.
A program may use at most 256 MiB of HBM per device.

```python
from functools import partial
import jax
import jax.numpy as jnp
from jax import lax

D = 1536
H = 48
P_SIZE = 64
N = 128
KC = 4
CH = 256
MICRO = 4
DI = 3072
MB_TOK = 1024
DOCS = 2
BLK = 512
N_SECTION = 2


def draw_seg_ids(key, part):
    key = jax.random.fold_in(key, 11)
    key_offsets, key_whole = jax.random.split(key)
    offsets = jax.random.randint(key_offsets, (MICRO, DOCS), 0, BLK)
    block_first = lax.broadcasted_iota(jnp.int32, (MICRO, DOCS), 1) * BLK
    start_pos = (block_first + offsets)[:, 1:]
    positions = lax.broadcasted_iota(jnp.int32, (MICRO, MB_TOK), 1)
    counted = (positions[:, :, None] >= start_pos[:, None, :]).astype(jnp.int32)
    ids = jnp.sum(counted, axis=2).astype(jnp.int32)
    whole_batch = jax.random.randint(key_whole, (), 0, MICRO)
    batch_rows = lax.broadcasted_iota(jnp.int32, (MICRO, MB_TOK), 0)
    return jnp.where(batch_rows == whole_batch, 0, ids).astype(jnp.int32)


def draw_a_log(key, part):
    key = jax.random.fold_in(key, 23)
    upper = -1.0
    return jax.random.uniform(key, (N_SECTION, H), jnp.float32, -12.0, upper)


def levels(own_key, dims, shards, least, largest):
    def one(dim, shards_of):
        heights = jax.random.uniform(jax.random.fold_in(jax.random.fold_in(own_key, 6), dim), (shards_of,), jnp.float32, least / len(shards), largest / len(shards))
        return jnp.repeat(jnp.exp(heights), dims[dim] // shards_of).reshape((-1,) + (1,) * (len(dims) - dim - 1))

    gain = one(*shards[0])
    for cut in shards[1:]:
        gain = gain * one(*cut)
    return gain


def scatter_about(key, extent, deviation, most, shards=(), dtype=jnp.bfloat16):
    values = deviation * jax.random.normal(key, extent, jnp.float32)
    if shards:
        values = values * levels(key, extent, shards, -0.22, 0.18)
    return jnp.clip(values, -most, most).astype(dtype)


def setup_inputs(seed: int = 0) -> dict:
    key_of = jax.random.split(jax.random.key(seed), 17)
    return {
        "tokens": scatter_about(key_of[0], (MICRO, MB_TOK, D), 1.0, 6.0, ((1, 4),)),
        "cotangent": scatter_about(key_of[1], (MICRO, MB_TOK, D), 1.0, 6.0, ((1, 4),)),
        "seg_ids": draw_seg_ids(jax.random.fold_in(key_of[16], 71), 0),
        "norm_gain": jnp.clip(1.0 + 0.18 * jax.random.normal(key_of[3], (N_SECTION, D), jnp.float32), 0.099609375, 1.8984375).astype(jnp.bfloat16),
        "in_zx": scatter_about(key_of[4], (N_SECTION, D, 2, DI), D ** -0.5, 0.15625, ((0, 2), (1, 4), (3, 4))),
        "in_bc": scatter_about(key_of[5], (N_SECTION, D, 2 * N), D ** -0.5, 0.15625, ((0, 2), (1, 4))),
        "in_dt": scatter_about(key_of[6], (N_SECTION, D, H), D ** -0.5, 0.15625, ((0, 2), (1, 4), (2, 4))),
        "conv_x": scatter_about(key_of[7], (N_SECTION, KC, DI), 0.5, 3.0, ((0, 2), (2, 4))),
        "conv_xb": scatter_about(key_of[8], (N_SECTION, DI), 0.5, 3.0, ((0, 2), (1, 4))),
        "conv_bc": scatter_about(key_of[9], (N_SECTION, KC, 2 * N), 0.5, 3.0, ((0, 2),)),
        "conv_bcb": scatter_about(key_of[10], (N_SECTION, 2 * N), 0.5, 3.0, ((0, 2),)),
        "dt_bias": jnp.clip(-3.0 + 3.0 * jax.random.uniform(key_of[11], (N_SECTION, H), jnp.float32) ** levels(key_of[11], (N_SECTION, H), ((0, 2), (1, 4)), -0.2, 0.2), -3.0, 0.0),
        "a_log": draw_a_log(jax.random.fold_in(key_of[16], 71), 0),
        "skip_gain": jnp.clip(0.5 + 1.0 * jax.random.uniform(key_of[13], (N_SECTION, H), jnp.float32) ** levels(key_of[13], (N_SECTION, H), ((0, 2), (1, 4)), -0.2, 0.2), 0.5, 1.5),
        "gate_gain": jnp.clip(1.0 + 0.18 * jax.random.normal(key_of[14], (N_SECTION, DI), jnp.float32), 0.099609375, 1.8984375).astype(jnp.bfloat16),
        "out_w": scatter_about(key_of[15], (N_SECTION, DI, D), DI ** -0.5, 0.109375, ((0, 2), (1, 4), (2, 4))),
    }


epsilon = 1e-05
precise = lax.Precision.HIGHEST

@jax.custom_vjp
def low(v):
    return lax.optimization_barrier(v.astype(jnp.bfloat16)).astype(jnp.float32)

@jax.custom_vjp
def low_back(v):
    return v

def low_keep(v):
    return (low(v), None)

def low_pass(kept, grad):
    return (grad,)

def back_keep(v):
    return (v, None)

def back_low(kept, grad):
    return (low(grad),)
low.defvjp(low_keep, low_pass)
low_back.defvjp(back_keep, back_low)

def block_step(decay_rate, carried, inputs):
    state_now, seg_before = carried
    x_block, rate_block, b_block, c_block, seg_block = inputs
    cumulative = jnp.cumsum(rate_block * decay_rate[None, :], axis=0)
    width_block = seg_block.shape[0]
    row_index = lax.broadcasted_iota(jnp.int32, (width_block, width_block), 0)
    col_index = lax.broadcasted_iota(jnp.int32, (width_block, width_block), 1)
    within = (row_index >= col_index) & (seg_block[:, None] == seg_block[None, :])
    within_heads = within[:, :, None]
    spread = cumulative[:, None, :] - cumulative[None, :, :]
    decay = jnp.where(within_heads, jnp.exp(jnp.where(within_heads, spread, 0.0)), 0.0)
    scores = jnp.dot(c_block, b_block.T, precision=precise)
    weights = scores[:, :, None] * decay * rate_block[None, :, :]
    output = jnp.einsum('tsh,shp->thp', weights, x_block, precision=precise)
    entering = jnp.exp(cumulative) * (seg_block == seg_before)[:, None].astype(jnp.float32)
    output = output + entering[:, :, None] * jnp.einsum('tn,hpn->thp', c_block, state_now, precision=precise)
    leaving = jnp.exp(cumulative[-1][None, :] - cumulative) * (seg_block == seg_block[-1])[:, None].astype(jnp.float32) * rate_block
    state_next = entering[-1][:, None, None] * state_now + jnp.einsum('sh,shp,sn->hpn', leaving, x_block, b_block, precision=precise)
    return ((state_next, seg_block[-1]), output)

def scan_blocks(x_heads, step_rate, b_part, c_part, seg_own, decay_rate, state_start, seg_start):
    blocks = x_heads.shape[0] // CH

    def to_blocks(value):
        return value.reshape((blocks, CH) + value.shape[1:])
    stepper = jax.checkpoint(partial(block_step, decay_rate))
    final_carry, output = lax.scan(stepper, (state_start, seg_start), (to_blocks(x_heads), to_blocks(step_rate), to_blocks(b_part), to_blocks(c_part), to_blocks(seg_own)))
    return (output.reshape(x_heads.shape), final_carry[0])

def causal_conv(padded_in, kernel, offset, seg_padded):
    own_rows = padded_in.shape[0] - (KC - 1)
    current = seg_padded[KC - 1:]
    summed = jnp.zeros((own_rows, padded_in.shape[1]), jnp.float32) + offset[None, :]
    for tap_index in range(KC):
        shifted = padded_in[tap_index:tap_index + own_rows]
        same_doc = (seg_padded[tap_index:tap_index + own_rows] == current).astype(jnp.float32)
        summed = summed + kernel[tap_index][None, :] * shifted * same_doc[:, None]
    return summed

def layer_forward(section_in, seg_row, params):
    norm_gain, in_zx, in_bc, in_dt, conv_x, conv_xb, conv_bc, conv_bcb, dt_bias, a_log, skip_gain, gate_gain, out_w = params
    own_rows = section_in.shape[0]
    in_scale = lax.rsqrt(lax.optimization_barrier(jnp.mean(section_in * section_in, axis=1)) + epsilon)
    normed = low(section_in * in_scale[:, None] * norm_gain[None, :])
    joined = jnp.dot(normed, in_zx.reshape(D, 2 * DI), precision=precise)
    gate_pre = low_back(joined[:, :DI])
    x_pre = low_back(low(joined[:, DI:]))
    bc_pre = low(jnp.dot(normed, in_bc, precision=precise))
    step_pre = low_back(jnp.dot(normed, in_dt, precision=precise))
    seg_padded = jnp.concatenate([jnp.full((KC - 1,), -1, jnp.int32), seg_row])
    mixed_pre = jnp.concatenate([x_pre, bc_pre], axis=1)
    padded_in = jnp.concatenate([jnp.zeros((KC - 1, DI + 2 * N), jnp.float32), mixed_pre], axis=0)
    kernel = jnp.concatenate([conv_x, conv_bc], axis=1)
    offset = jnp.concatenate([conv_xb, conv_bcb])
    conv_out = jax.nn.silu(causal_conv(padded_in, kernel, offset, seg_padded))
    x_heads = conv_out[:, :DI].reshape(own_rows, H, P_SIZE)
    b_part = conv_out[:, DI:DI + N]
    c_part = conv_out[:, DI + N:]
    step_rate = jax.nn.softplus(step_pre + dt_bias[None, :])
    decay_rate = -jnp.exp(a_log)
    ssm_out = scan_blocks(x_heads, step_rate, b_part, c_part, seg_row, decay_rate, jnp.zeros((H, P_SIZE, N), jnp.float32), jnp.array(-1, jnp.int32))[0]
    ssm_out = ssm_out + skip_gain[None, :, None] * x_heads
    gated = ssm_out.reshape(own_rows, DI) * jax.nn.silu(gate_pre)
    gate_scale = lax.rsqrt(lax.optimization_barrier(jnp.mean(gated * gated, axis=1)) + epsilon)
    gate_normed = low(gated * gate_scale[:, None] * gate_gain[None, :])
    return section_in + jnp.dot(gate_normed, out_w, precision=precise)

def reference(tokens, cotangent, seg_ids, norm_gain, in_zx, in_bc, in_dt, conv_x, conv_xb, conv_bc, conv_bcb, dt_bias, a_log, skip_gain, gate_gain, out_w):
    weights_all = tuple((array_in.astype(jnp.float32) for array_in in (norm_gain, in_zx, in_bc, in_dt, conv_x, conv_xb, conv_bc, conv_bcb, dt_bias, a_log, skip_gain, gate_gain, out_w)))
    first_section = tuple((array_in[0] for array_in in weights_all))
    second_section = tuple((array_in[1] for array_in in weights_all))

    def one_batch(running_totals, batch_items):
        batch_tokens, batch_cot, batch_seg = batch_items

        def section_first(section_in, params):
            return low(layer_forward(section_in, batch_seg, params))

        def section_second(section_in, params):
            return layer_forward(section_in, batch_seg, params)
        sent_value, pull_first = jax.vjp(section_first, batch_tokens.astype(jnp.float32), first_section)
        result, pull_second = jax.vjp(section_second, sent_value, second_section)
        middle_grad, grads_second = pull_second(batch_cot.astype(jnp.float32))
        sent_grad = low(middle_grad)
        input_grad, grads_first = pull_first(sent_grad)
        running_totals = tuple((running + jnp.stack([grad_one, grad_two]) for running, grad_one, grad_two in zip(running_totals, grads_first, grads_second)))
        return (running_totals, (sent_value.astype(jnp.bfloat16), result.astype(jnp.bfloat16), input_grad, sent_grad))
    starting = tuple((jnp.zeros_like(array_in) for array_in in weights_all))
    totals, stacked = lax.scan(one_batch, starting, (tokens, cotangent, seg_ids))
    section_outputs = jnp.stack([stacked[0], stacked[1]])
    input_grads = jnp.stack([stacked[2], stacked[3]])
    return (section_outputs, input_grads, totals[0], totals[1], totals[2], totals[3], totals[4], totals[5], totals[6], totals[7], totals[8], totals[9], totals[10], totals[11], totals[12])
```

```python
from functools import partial

import jax
import jax.numpy as jnp
from jax import lax
from jax.experimental import pallas as pl
from jax.experimental.pallas import tpu as pltpu
from jax.sharding import PartitionSpec as P

bf16 = jnp.bfloat16
f32 = jnp.float32
precise = lax.Precision.HIGHEST
epsilon = 1e-05
N = 128
KC = 4
CH = 256
DI = 3072
HALO = 16
LANES = 128
VMEM_BYTES = 48 * 1024 * 1024

M_FWD, M_BWD, M_ENTER, M_LEAVE, M_SEG = 0, 4, 8, 9, 10


def mm(a, b):
    return lax.dot_general(a, b, (((1,), (0,)), ((), ())), preferred_element_type=f32)


def mm_nt(a, b, precision=None):
    return lax.dot_general(a, b, (((1,), (1,)), ((), ())), preferred_element_type=f32, precision=precision)


def mm_tn(a, b):
    return lax.dot_general(a, b, (((0,), (0,)), ((), ())), preferred_element_type=f32)


def split(v):
    high = v.astype(bf16)
    return high, (v - high.astype(f32)).astype(bf16)


def rows_of(selector, values):
    high, low = split(values)
    return mm_nt(selector, high) + mm_nt(selector, low)


def times_mask(rows, mask):
    high, low = split(rows)
    return mm(high, mask) + mm(low, mask)


def left_parts(a):
    high, low = split(a)
    return jnp.concatenate([high, low, high], axis=1)


def right_parts(b, axis):
    high, low = split(b)
    return jnp.concatenate([high, high, low], axis=axis)


def precise_nt(a, b):
    return mm_nt(left_parts(a), right_parts(b, 1))


def precise_mm(a, b):
    return mm(left_parts(a), right_parts(b, 0))


def head_selector(head_size):
    row = lax.broadcasted_iota(jnp.int32, (8, LANES), 0)
    lane = lax.broadcasted_iota(jnp.int32, (8, LANES), 1)
    return (row == lane // head_size).astype(bf16)


def iota2(shape):
    return lax.broadcasted_iota(jnp.int32, shape, 0), lax.broadcasted_iota(jnp.int32, shape, 1)


def sigmoid(v):
    return 1.0 / (1.0 + jnp.exp(-v))


def softplus(v):
    return jnp.maximum(v, 0.0) + jnp.log1p(jnp.exp(-jnp.abs(v)))


def fill_padded(padded, halo_ref, pre_ref, rows):
    padded[pl.ds(0, HALO), :] = halo_ref[...].astype(f32)
    padded[pl.ds(HALO, rows), :] = pre_ref[...].astype(f32)


def conv_tile(padded, taps_ref, marks, start, count):
    total = jnp.zeros((count, LANES), f32) + taps_ref[KC : KC + 1, :]
    for k in range(KC):
        shifted = padded[pl.ds(start + HALO - KC + 1 + k, count), :]
        if k == KC - 1:
            total = total + taps_ref[k : k + 1, :] * shifted
        else:
            total = total + taps_ref[k : k + 1, :] * (shifted * marks[start : start + count, M_FWD + k : M_FWD + k + 1])
    return total


TILE = 128


def scan_forward_kernel(
    head_size, rows, pre_ref, halo_ref, taps_ref, marks_ref, seg_ref, step_ref, bias_ref, decay_ref,
    conv_ref, y_ref, own_state_ref, last_state_ref, cum_ref, rate_ref, cum_rows_ref, step_rows_ref,
    padded, b_all, b_turned, scores, cum_all, rate_all, step_all,
):
    i = pl.program_id(0)
    chunks = rows // CH
    fill_padded(padded, halo_ref, pre_ref, rows)
    for start in range(0, rows, TILE):
        value = conv_tile(padded, taps_ref, marks_ref, start, TILE)
        conv_ref[pl.ds(start, TILE), :] = value / (1.0 + jnp.exp(-value))

    @pl.when(i == 0)
    def _():
        b_all[...] = conv_ref[...]
        b_turned[...] = conv_ref[...].T
        shifted = step_ref[...] + bias_ref[...]
        rate = softplus(shifted)
        step_all[...] = shifted
        rate_all[...] = rate
        r, c = iota2((CH, CH))
        tri = (r >= c).astype(f32)
        for n in range(chunks):
            part = rate[n * CH : (n + 1) * CH, :] * decay_ref[...]
            cum_all[pl.ds(n * CH, CH), :] = lax.dot_general(
                tri, part, (((1,), (0,)), ((), ())), preferred_element_type=f32, precision=precise
            )

    @pl.when(i == 1)
    def _():
        r, c = iota2((CH, CH))
        for n in range(chunks):
            here = pl.ds(n * CH, CH)
            same = marks_ref[here, M_SEG : M_SEG + 1] == seg_ref[0:1, here]
            value = precise_nt(conv_ref[here, :], b_all[here, :])
            scores[n] = jnp.where((r >= c) & same, value, 0.0)

    @pl.when(i >= 2)
    def _():
        j = i - 2
        per = LANES // head_size
        row, lane = iota2((LANES, LANES))
        widen = (row == per * j + lane // head_size).astype(f32)
        cum = lax.dot_general(cum_all[...], widen, (((1,), (0,)), ((), ())), preferred_element_type=f32, precision=precise)
        rate = lax.dot_general(rate_all[...], widen, (((1,), (0,)), ((), ())), preferred_element_type=f32, precision=precise)
        row8, lane8 = iota2((8, LANES))
        pick = ((lane8 == per * j + row8) & (row8 < per)).astype(f32)
        cum_rows = mm_nt(pick, cum_all[...], precise)
        cum_rows_ref[0] = cum_rows
        step_rows_ref[0] = mm_nt(pick, step_all[...], precise)
        cum_ref[...] = cum
        rate_ref[...] = rate
        lane_c = lax.broadcasted_iota(jnp.int32, (CH, LANES), 1)
        states = []
        for n in range(chunks):
            here = pl.ds(n * CH, CH)
            span = slice(n * CH, (n + 1) * CH)
            scaled = rate[span] * conv_ref[here, :]
            scaled_parts = right_parts(scaled, 0)
            out = jnp.zeros((CH, LANES), f32)
            for h in range(per):
                spread = cum[span, h * head_size : h * head_size + 1] - cum_rows[h : h + 1, span]
                value = mm(left_parts(scores[n] * jnp.exp(jnp.minimum(spread, 0.0))), scaled_parts)
                out = value if per == 1 else jnp.where(lane_c // head_size == h, value, out)
            y_ref[here, :] = out
            leave = jnp.exp(cum[(n + 1) * CH - 1 : (n + 1) * CH, :] - cum[span]) * marks_ref[here, M_LEAVE : M_LEAVE + 1]
            state = precise_mm(b_turned[:, here], scaled * leave)
            own_state_ref[n] = state
            states.append(state)
        total = states[0]
        for n in range(1, chunks):
            last = (n + 1) * CH - 1
            kept = jnp.exp(cum[last : last + 1, :]) * marks_ref[last : last + 1, M_ENTER : M_ENTER + 1]
            total = kept * total + states[n]
        last_state_ref[...] = total


def call(kernel, held, in_specs, **rest):
    count = len(held)

    def run(*refs):
        kernel(*refs[count:])

    made = pl.pallas_call(run, in_specs=[pl.BlockSpec(memory_space=pl.ANY)] * count + in_specs, **rest)
    return lambda *args: made(*held, *args)


def ordered(value, *others):
    anywhere = pl.BlockSpec(memory_space=pl.ANY)
    return pl.pallas_call(
        lambda *refs: None,
        in_specs=[anywhere] * (1 + len(others)),
        out_specs=anywhere,
        out_shape=jax.ShapeDtypeStruct(value.shape, value.dtype),
        input_output_aliases={0: 0},
        cost_estimate=cost(0),
        name="ordered",
    )(value, *others)


def whole(shape):
    return pl.BlockSpec(shape, lambda i: (0,) * len(shape))


def params(limit=VMEM_BYTES):
    return pltpu.CompilerParams(vmem_limit_bytes=limit, dimension_semantics=("arbitrary",))


def cost(microseconds):
    return pl.CostEstimate(flops=0, bytes_accessed=int(microseconds * 3e6), transcendentals=0)


def scan_forward(pre, halo, taps, marks, seg_row, step, bias, decay, head_size, held=()):
    rows, mixed = pre.shape
    inner = mixed - 2 * N
    pairs = inner // LANES
    chunks = rows // CH
    steps = pairs + 2
    column = lambda i: (0, (i + pairs) % steps)
    pair = lambda i: (0, jnp.maximum(i - 2, 0))
    return call(
        partial(scan_forward_kernel, head_size, rows),
        held,
        grid=(steps,),
        in_specs=[
            pl.BlockSpec((rows, LANES), column),
            pl.BlockSpec((HALO, LANES), column),
            pl.BlockSpec((8, LANES), column),
            whole((rows, LANES)),
            whole((8, rows)),
            whole((rows, LANES)),
            whole((1, LANES)),
            whole((1, LANES)),
        ],
        out_specs=[
            pl.BlockSpec((rows, LANES), column),
            pl.BlockSpec((rows, LANES), pair),
            pl.BlockSpec((chunks, N, LANES), lambda i: (0, 0, jnp.maximum(i - 2, 0))),
            pl.BlockSpec((N, LANES), pair),
            pl.BlockSpec((rows, LANES), pair),
            pl.BlockSpec((rows, LANES), pair),
            pl.BlockSpec((1, 8, rows), lambda i: (jnp.maximum(i - 2, 0), 0, 0)),
            pl.BlockSpec((1, 8, rows), lambda i: (jnp.maximum(i - 2, 0), 0, 0)),
        ],
        out_shape=[
            jax.ShapeDtypeStruct((rows, mixed), f32),
            jax.ShapeDtypeStruct((rows, inner), f32),
            jax.ShapeDtypeStruct((chunks, N, inner), f32),
            jax.ShapeDtypeStruct((N, inner), f32),
            jax.ShapeDtypeStruct((rows, inner), f32),
            jax.ShapeDtypeStruct((rows, inner), f32),
            jax.ShapeDtypeStruct((pairs, 8, rows), f32),
            jax.ShapeDtypeStruct((pairs, 8, rows), f32),
        ],
        scratch_shapes=[
            pltpu.VMEM((rows + HALO, LANES), f32),
            pltpu.VMEM((rows, LANES), f32),
            pltpu.VMEM((N, rows), f32),
            pltpu.VMEM((chunks, CH, CH), f32),
            pltpu.VMEM((rows, LANES), f32),
            pltpu.VMEM((rows, LANES), f32),
            pltpu.VMEM((rows, LANES), f32),
        ],
        compiler_params=params(),
        cost_estimate=cost(15),
        name="scan_forward",
    )(pre, halo, taps, marks, seg_row, step, bias, decay)


def gate_kernel(
    chunks, with_grad, y_ref, conv_ref, c_ref, cum_ref, marks_ref, own_state_ref, state_ref, gate_ref, skip_ref, gain_ref,
    *rest,
):
    if with_grad:
        grad_ref, ssm_ref, gated_ref, entering_ref, sums_ref = rest
    else:
        ssm_ref, gated_ref, entering_ref, sums_ref = rest
    i = pl.program_id(0)
    state = state_ref[...]
    for n in range(chunks):
        here = pl.ds(n * CH, CH)
        entering_ref[n] = state
        enter = jnp.exp(cum_ref[here, :]) * marks_ref[here, M_ENTER : M_ENTER + 1]
        ssm_ref[here, :] = (
            y_ref[here, :]
            + enter * precise_mm(c_ref[here, :], state)
            + skip_ref[...] * conv_ref[here, :]
        )
        state = enter[CH - 1 : CH, :] * state + own_state_ref[n]
    gate = gate_ref[...]
    gated = ssm_ref[...] * (gate * sigmoid(gate))
    scaled = gated * gain_ref[...]
    gated_ref[...] = scaled
    row = lax.broadcasted_iota(jnp.int32, (8, LANES), 0)
    sums = rows_of((row == 0).astype(bf16), gated * gated)
    if with_grad:
        sums = sums + rows_of((row == 1).astype(bf16), scaled * grad_ref[...])

    @pl.when(i == 0)
    def _():
        sums_ref[...] = sums

    @pl.when(i > 0)
    def _():
        sums_ref[...] += sums


def gate_forward(y, conv, cum, marks, own_state, state_in, gate, skip, gain, grad=None, held=()):
    rows, inner = y.shape
    pairs = inner // LANES
    chunks = rows // CH
    block = pl.BlockSpec((rows, LANES), lambda i: (0, i))
    line = pl.BlockSpec((1, LANES), lambda i: (0, i))
    states = pl.BlockSpec((chunks, N, LANES), lambda i: (0, 0, i))
    last = conv.shape[1] // LANES - 1
    in_specs = [
        block, block, pl.BlockSpec((rows, LANES), lambda i: (0, last)), block, whole((rows, LANES)), states,
        pl.BlockSpec((N, LANES), lambda i: (0, i)), block, line, line,
    ]
    args = [y, conv, conv, cum, marks, own_state, state_in, gate, skip, gain]
    if grad is not None:
        in_specs.append(block)
        args.append(grad)
    return call(
        partial(gate_kernel, chunks, grad is not None),
        held,
        grid=(pairs,),
        in_specs=in_specs,
        out_specs=[block, block, states, whole((8, rows))],
        out_shape=[
            jax.ShapeDtypeStruct((rows, inner), f32),
            jax.ShapeDtypeStruct((rows, inner), f32),
            jax.ShapeDtypeStruct((chunks, N, inner), f32),
            jax.ShapeDtypeStruct((8, rows), f32),
        ],
        compiler_params=params(),
        cost_estimate=cost(6),
        name="gate_forward",
    )(*args)


def gate_backward_kernel(
    chunks, channels, grad_ref, gate_ref, ssm_ref, conv_ref, c_ref, cum_ref, marks_ref, sums_ref, gain_ref,
    out_grad_ref, gate_grad_ref, pulled_ref, first_ref, gain_grad_ref, skip_grad_ref, dots_ref,
    scale_all, shift_all, c_turned,
):
    i = pl.program_id(0)

    @pl.when(i == 0)
    def _():
        scale = lax.rsqrt(sums_ref[0:1, :] / channels + epsilon)
        shift = scale * scale * scale * sums_ref[1:2, :] / channels
        rows = scale.shape[1]
        scale_all[...] = jnp.broadcast_to(scale, (LANES, rows)).T
        shift_all[...] = jnp.broadcast_to(shift, (LANES, rows)).T
        c_turned[...] = c_ref[...].T

    gate = gate_ref[...]
    sig = sigmoid(gate)
    act = gate * sig
    ssm = ssm_ref[...]
    gated = ssm * act
    grad = grad_ref[...]
    scale = scale_all[...]
    gated_grad = scale * gain_ref[...] * grad - gated * shift_all[...]
    gain_grad_ref[...] = jnp.sum(grad * gated * scale, axis=0, keepdims=True)
    out_grad = gated_grad * act
    out_grad_ref[...] = out_grad
    skip_grad_ref[...] = jnp.sum(out_grad * conv_ref[...], axis=0, keepdims=True)
    gate_grad = gated_grad * ssm * (sig * (1.0 + gate * (1.0 - sig)))
    gate_grad_ref[...] = gate_grad.astype(bf16)
    row = lax.broadcasted_iota(jnp.int32, (8, LANES), 0)
    dots = rows_of((row == 0).astype(bf16), gate_grad * gate)
    kept = []
    for n in range(chunks):
        here = pl.ds(n * CH, CH)
        enter = jnp.exp(cum_ref[here, :]) * marks_ref[here, M_ENTER : M_ENTER + 1]
        pulled = precise_mm(c_turned[:, here], out_grad_ref[here, :] * enter)
        pulled_ref[n] = pulled
        kept.append((enter[CH - 1 : CH, :], pulled))
    first = kept[-1][1]
    for last_enter, pulled in kept[-2::-1]:
        first = last_enter * first + pulled
    first_ref[...] = first

    @pl.when(i == 0)
    def _():
        dots_ref[...] = dots

    @pl.when(i > 0)
    def _():
        dots_ref[...] += dots


def gate_backward(grad, gate, ssm, conv, cum, marks, sums, gain, channels, held=()):
    rows, inner = ssm.shape
    pairs = inner // LANES
    chunks = rows // CH
    block = pl.BlockSpec((rows, LANES), lambda i: (0, i))
    line = pl.BlockSpec((1, LANES), lambda i: (0, i))
    states = pl.BlockSpec((chunks, N, LANES), lambda i: (0, 0, i))
    last = conv.shape[1] // LANES - 1
    return call(
        partial(gate_backward_kernel, chunks, float(channels)),
        held,
        grid=(pairs,),
        in_specs=[
            block, block, block, block, pl.BlockSpec((rows, LANES), lambda i: (0, last)), block,
            whole((rows, LANES)), whole((8, rows)), line,
        ],
        out_specs=[block, block, states, pl.BlockSpec((N, LANES), lambda i: (0, i)), line, line, whole((8, rows))],
        out_shape=[
            jax.ShapeDtypeStruct((rows, inner), f32),
            jax.ShapeDtypeStruct((rows, inner), bf16),
            jax.ShapeDtypeStruct((chunks, N, inner), f32),
            jax.ShapeDtypeStruct((N, inner), f32),
            jax.ShapeDtypeStruct((1, inner), f32),
            jax.ShapeDtypeStruct((1, inner), f32),
            jax.ShapeDtypeStruct((8, rows), f32),
        ],
        scratch_shapes=[pltpu.VMEM((rows, LANES), f32), pltpu.VMEM((rows, LANES), f32), pltpu.VMEM((N, rows), f32)],
        compiler_params=params(),
        cost_estimate=cost(7),
        name="gate_backward",
    )(grad, gate, ssm, conv, conv, cum, marks, sums, gain)


def intra_backward_kernel(
    head_size, chunks, out_grad_ref, conv_ref, b_ref, c_ref, cum_ref, rate_ref, cum_rows_ref, marks_ref, seg_ref,
    scaled_grad_ref, rate_rows_ref, b_grad_ref, c_grad_ref,
    scores, scores_grad,
):
    i = pl.program_id(0)
    per = LANES // head_size
    r, c = iota2((CH, CH))

    @pl.when(i == 0)
    def _():
        for n in range(chunks):
            here = pl.ds(n * CH, CH)
            same = marks_ref[here, M_SEG : M_SEG + 1] == seg_ref[0:1, here]
            value = precise_nt(b_ref[here, :], c_ref[here, :])
            scores[n] = jnp.where((r <= c) & same, value, 0.0)
            scores_grad[n] = jnp.zeros((CH, CH), f32)

    from_row = (r >= c).astype(bf16)
    lane_c = lax.broadcasted_iota(jnp.int32, (CH, LANES), 1)
    rate_rows_ref[...] = jnp.zeros(rate_rows_ref.shape, f32)
    for n in range(chunks):
        here = pl.ds(n * CH, CH)
        scaled = rate_ref[here, :] * conv_ref[here, :]
        grad_parts = right_parts(out_grad_ref[here, :], 1)
        grad_low = grad_parts[:, :LANES]
        out = jnp.zeros((CH, LANES), f32)
        for h in range(per):
            mine = lane_c // head_size == h
            spread = cum_rows_ref[0, h : h + 1, here] - cum_ref[here, h * head_size : h * head_size + 1]
            decay = jnp.exp(jnp.minimum(spread, 0.0))
            weights = scores[n] * decay
            value = mm(weights.astype(bf16), grad_low)
            out = jnp.where(mine, value, out)
            weights_grad = mm_nt(left_parts(jnp.where(mine, scaled, 0.0)), grad_parts)
            scores_grad[n] += decay * weights_grad
            flow = mm((weights * weights_grad).astype(bf16), from_row)
            rate_rows_ref[0, h : h + 1, here] = jnp.sum(jnp.where(r < c, flow, 0.0), axis=0, keepdims=True)
        scaled_grad_ref[here, :] = out

    @pl.when(i == pl.num_programs(0) - 1)
    def _():
        for n in range(chunks):
            here = pl.ds(n * CH, CH)
            same = marks_ref[here, M_SEG : M_SEG + 1] == seg_ref[0:1, here]
            total = jnp.where((r <= c) & same, scores_grad[n], 0.0)
            b_grad_ref[here, :] = precise_mm(total, c_ref[here, :])
            c_grad_ref[here, :] = precise_mm(total.T, b_ref[here, :])


def intra_backward(out_grad, conv, cum, rate, cum_rows, marks, seg_row, head_size, held=()):
    rows, inner = out_grad.shape
    pairs = inner // LANES
    chunks = rows // CH
    block = pl.BlockSpec((rows, LANES), lambda i: (0, i))
    heads = pl.BlockSpec((1, 8, rows), lambda i: (i, 0, 0))
    return call(
        partial(intra_backward_kernel, head_size, chunks),
        held,
        grid=(pairs,),
        in_specs=[
            block, block, pl.BlockSpec((rows, LANES), lambda i: (0, pairs)),
            pl.BlockSpec((rows, LANES), lambda i: (0, pairs + 1)), block, block, heads,
            whole((rows, LANES)), whole((8, rows)),
        ],
        out_specs=[block, heads, whole((rows, N)), whole((rows, N))],
        out_shape=[
            jax.ShapeDtypeStruct((rows, inner), f32),
            jax.ShapeDtypeStruct((pairs, 8, rows), f32),
            jax.ShapeDtypeStruct((rows, N), f32),
            jax.ShapeDtypeStruct((rows, N), f32),
        ],
        scratch_shapes=[pltpu.VMEM((chunks, CH, CH), f32), pltpu.VMEM((chunks, CH, CH), f32)],
        compiler_params=params(),
        cost_estimate=cost(8),
        name="intra_backward",
    )(out_grad, conv, conv, conv, cum, rate, cum_rows, marks, seg_row)


def scan_backward_kernel(
    head_size, rows, pairs, out_grad_ref, scaled_grad_ref, conv_ref, b_ref, c_ref, cum_ref, rate_ref, rate_rows_ref, step_rows_ref,
    entering_ref, pulled_ref, after_ref, skip_ref, decay_ref, b_intra_ref, c_intra_ref, pre_ref, halo_ref, taps_ref, marks_ref,
    conv_grad_ref, taps_grad_ref, step_grad_ref, log_grad_ref, bias_grad_ref,
    padded, b_total, c_total, current,
):
    i = pl.program_id(0)
    chunks = rows // CH
    fill_padded(padded, halo_ref, pre_ref, rows)

    @pl.when(i == 0)
    def _():
        b_total[...] = b_intra_ref[...]
        c_total[...] = c_intra_ref[...]

    @pl.when(i < pairs)
    def _():
        selector = head_selector(head_size)
        r, c = iota2((CH, CH))
        from_row = (r >= c).astype(bf16)
        before = (r < c).astype(bf16)
        after = after_ref[...]
        log_total = jnp.zeros((8, 1), f32)
        bias_total = jnp.zeros((8, 1), f32)
        decay = decay_ref[0, :, 0:1]
        for n in reversed(range(chunks)):
            here = pl.ds(n * CH, CH)
            last = (n + 1) * CH - 1
            mark_enter = marks_ref[here, M_ENTER : M_ENTER + 1]
            mark_leave = marks_ref[here, M_LEAVE : M_LEAVE + 1]
            cum = cum_ref[here, :]
            enter = jnp.exp(cum) * mark_enter
            leave = jnp.exp(cum_ref[last : last + 1, :] - cum) * mark_leave
            conv = conv_ref[here, :]
            rate = rate_ref[here, :]
            scaled = rate * conv
            out_grad = out_grad_ref[here, :]
            state = entering_ref[n]
            state_low = state.astype(bf16)
            after_low = after.astype(bf16)
            left = leave * mm(b_ref[here, :].astype(bf16), after_low)
            scaled_grad = scaled_grad_ref[here, :] + left
            b_total[here, :] += precise_nt(scaled * leave, after)
            entered = out_grad * enter
            c_total[here, :] += precise_nt(entered, state)
            came = rows_of(selector, entered * mm(c_ref[here, :].astype(bf16), state_low))
            gone = rows_of(selector, scaled * left)
            kept = enter[CH - 1 : CH, :]
            through = jnp.sum(rows_of(selector, kept * (state * after)), axis=1, keepdims=True)
            log_rate_grad = rate_rows_ref[0, :, here] + times_mask(came, from_row) + times_mask(gone, before) + through
            direct = rows_of(selector, conv * scaled_grad)
            shifted = step_rows_ref[0, :, here]
            step_grad = (direct + log_rate_grad * decay) * sigmoid(shifted)
            step_grad_ref[0, :, here] = step_grad
            log_total = log_total + jnp.sum(log_rate_grad * softplus(shifted), axis=1, keepdims=True) * decay
            bias_total = bias_total + jnp.sum(step_grad, axis=1, keepdims=True)
            current[here, :] = rate * scaled_grad + skip_ref[...] * out_grad
            after = kept * after + pulled_ref[n]
        log_grad_ref[0] = jnp.broadcast_to(log_total, (8, LANES))
        bias_grad_ref[0] = jnp.broadcast_to(bias_total, (8, LANES))

    @pl.when(i == pairs)
    def _():
        current[...] = b_total[...]

    @pl.when(i == pairs + 1)
    def _():
        current[...] = c_total[...]

    sums = [jnp.zeros((1, LANES), f32) for _ in range(KC + 1)]
    for start in range(0, rows, TILE):
        value = conv_tile(padded, taps_ref, marks_ref, start, TILE)
        sig = sigmoid(value)
        grad = current[pl.ds(start, TILE), :] * (sig * (1.0 + value * (1.0 - sig)))
        conv_grad_ref[pl.ds(start, TILE), :] = grad
        for k in range(KC):
            shifted = padded[pl.ds(start + HALO - KC + 1 + k, TILE), :]
            if k < KC - 1:
                shifted = shifted * marks_ref[start : start + TILE, M_FWD + k : M_FWD + k + 1]
            sums[k] = sums[k] + jnp.sum(grad * shifted, axis=0, keepdims=True)
        sums[KC] = sums[KC] + jnp.sum(grad, axis=0, keepdims=True)
    taps_grad_ref[...] = jnp.concatenate(sums + [jnp.zeros((8 - KC - 1, LANES), f32)], axis=0)


def scan_backward(
    out_grad, scaled_grad, conv, cum, rate, rate_rows, step_rows, entering, pulled, after, skip, decay_rows,
    b_intra, c_intra, pre, halo, taps, marks, head_size, held=(),
):
    rows, inner = out_grad.shape
    mixed = pre.shape[1]
    pairs = inner // LANES
    chunks = rows // CH
    steps = pairs + 2
    own = lambda i: jnp.minimum(i, pairs - 1)
    block = pl.BlockSpec((rows, LANES), lambda i: (0, own(i)))
    column = lambda i: (0, i)
    heads = pl.BlockSpec((1, 8, rows), lambda i: (own(i), 0, 0))
    few = pl.BlockSpec((1, 8, LANES), lambda i: (own(i), 0, 0))
    states = pl.BlockSpec((chunks, N, LANES), lambda i: (0, 0, own(i)))
    return call(
        partial(scan_backward_kernel, head_size, rows, pairs),
        held,
        grid=(steps,),
        in_specs=[
            block, block, block, pl.BlockSpec((rows, LANES), lambda i: (0, pairs)),
            pl.BlockSpec((rows, LANES), lambda i: (0, pairs + 1)), block, block, heads, heads, states, states,
            pl.BlockSpec((N, LANES), lambda i: (0, own(i))), pl.BlockSpec((1, LANES), lambda i: (0, own(i))), few,
            whole((rows, N)), whole((rows, N)), pl.BlockSpec((rows, LANES), column), pl.BlockSpec((HALO, LANES), column),
            pl.BlockSpec((8, LANES), column), whole((rows, LANES)),
        ],
        out_specs=[pl.BlockSpec((rows, LANES), column), pl.BlockSpec((8, LANES), column), heads, few, few],
        out_shape=[
            jax.ShapeDtypeStruct((rows, mixed), f32),
            jax.ShapeDtypeStruct((8, mixed), f32),
            jax.ShapeDtypeStruct((pairs, 8, rows), f32),
            jax.ShapeDtypeStruct((pairs, 8, LANES), f32),
            jax.ShapeDtypeStruct((pairs, 8, LANES), f32),
        ],
        scratch_shapes=[
            pltpu.VMEM((rows + HALO, LANES), f32),
            pltpu.VMEM((rows, N), f32),
            pltpu.VMEM((rows, N), f32),
            pltpu.VMEM((rows, LANES), f32),
        ],
        compiler_params=params(),
        cost_estimate=cost(16),
        name="scan_backward",
    )(
        out_grad, scaled_grad, conv, conv, conv, cum, rate, rate_rows, step_rows, entering, pulled, after, skip, decay_rows,
        b_intra, c_intra, pre, halo, taps, marks,
    )


def conv_backward_kernel(
    rows, pairs, per, conv_grad_ref, next_ref, taps_ref, marks_ref, pre_ref, gate_dots_ref, step_grad_ref, step_rows_ref,
    bias_ref, out_ref, map_grad_ref, dots_ref, padded,
):
    i = pl.program_id(0)
    row = lax.broadcasted_iota(jnp.int32, (8, LANES), 0)

    @pl.when(i == 0)
    def _():
        dots_ref[...] = gate_dots_ref[...]

    @pl.when(i > 0)
    def _():
        padded[pl.ds(0, rows), :] = conv_grad_ref[...]
        padded[pl.ds(rows, 8), :] = next_ref[...]
        selector = (row == 0).astype(bf16)
        for start in range(0, rows, TILE):
            total = taps_ref[KC - 1 : KC, :] * padded[pl.ds(start, TILE), :]
            for k in range(KC - 1):
                shifted = padded[pl.ds(start + KC - 1 - k, TILE), :]
                total = total + taps_ref[k : k + 1, :] * (
                    shifted * marks_ref[start : start + TILE, M_BWD + k : M_BWD + k + 1]
                )
            out_ref[pl.ds(start, TILE), :] = total.astype(bf16)
            map_grad_ref[pl.ds(start, TILE), :] = total
            dots_ref[:, pl.ds(start, TILE)] += rows_of(selector, total * pre_ref[pl.ds(start, TILE), :].astype(f32))

    @pl.when(i == 0)
    def _():
        grads = [step_grad_ref[j, 0:per, :] for j in range(pairs)]
        grads = jnp.concatenate(grads + [jnp.zeros((LANES - per * pairs, rows), f32)], axis=0)
        out_ref[...] = grads.T.astype(bf16)
        total = jnp.zeros((1, rows), f32)
        for j in range(pairs):
            total = total + jnp.sum(
                step_grad_ref[j, 0:per, :] * (step_rows_ref[j, 0:per, :] - bias_ref[j, 0:per, 0:1]), axis=0, keepdims=True
            )
        dots_ref[0:1, :] += total


def conv_backward(conv_grad, next_grad, taps, marks, pre, gate_dots, step_grad, step_rows, bias_rows, head_size, held=()):
    rows, mixed = pre.shape
    pairs = (mixed - 2 * N) // LANES
    steps = pairs + 3
    column = lambda i: (0, jnp.clip(i - 1, 0, pairs + 1))
    return call(
        partial(conv_backward_kernel, rows, pairs, LANES // head_size),
        held,
        grid=(steps,),
        in_specs=[
            pl.BlockSpec((rows, LANES), column), pl.BlockSpec((8, LANES), column), pl.BlockSpec((8, LANES), column),
            whole((rows, LANES)), pl.BlockSpec((rows, LANES), column),
            whole((8, rows)),
            whole((pairs, 8, rows)), whole((pairs, 8, rows)), whole((pairs, 8, LANES)),
        ],
        out_specs=[
            pl.BlockSpec((rows, LANES), lambda i: (0, i)),
            pl.BlockSpec((rows, LANES), lambda i: (0, jnp.clip(i - pairs - 1, 0, 1))),
            whole((8, rows)),
        ],
        out_shape=[
            jax.ShapeDtypeStruct((rows, steps * LANES), bf16),
            jax.ShapeDtypeStruct((rows, 2 * N), f32),
            jax.ShapeDtypeStruct((8, rows), f32),
        ],
        scratch_shapes=[pltpu.VMEM((rows + 8, LANES), f32)],
        compiler_params=params(),
        cost_estimate=cost(6),
        name="conv_backward",
    )(conv_grad, next_grad, taps, marks, pre, gate_dots, step_grad, step_rows, bias_rows)


def join_kernel(count, width, index_ref, *refs):
    blocks, out_ref = refs[:count], refs[count]
    for n in range(count):
        start = pl.multiple_of((index_ref[0] ^ n) * width, LANES)
        out_ref[:, pl.ds(start, width)] = blocks[n][...].astype(out_ref.dtype)


def join(blocks, index, dtype, first_row, held=()):
    count = len(blocks)
    rows, width = blocks[0].shape
    rows -= first_row
    size = min(rows, 256)
    return call(
        partial(join_kernel, count, width),
        held,
        grid=(rows // size,),
        in_specs=[pl.BlockSpec(memory_space=pltpu.SMEM)]
        + [pl.BlockSpec((size, width), lambda i: (i + first_row // size, 0))] * count,
        out_specs=pl.BlockSpec((size, count * width), lambda i: (i, 0)),
        out_shape=jax.ShapeDtypeStruct((rows, count * width), dtype),
        compiler_params=params(),
        cost_estimate=cost(2),
        name="join",
    )(index, *blocks)


def join_norm_kernel(count, width, index_ref, gain_ref, *refs):
    blocks, normed_ref, scale_ref = refs[:count], refs[count], refs[count + 1]
    total = jnp.zeros((blocks[0].shape[0], 1), f32)
    for n in range(count):
        value = blocks[n][...].astype(f32)
        total = total + jnp.sum(value * value, axis=1, keepdims=True)
    scale = lax.rsqrt(total / (count * width) + epsilon)
    scale_ref[...] = jnp.broadcast_to(scale, scale_ref.shape)
    for n in range(count):
        here = pl.ds(pl.multiple_of((index_ref[0] ^ n) * width, LANES), width)
        normed_ref[:, here] = (blocks[n][...].astype(f32) * scale * gain_ref[:, here]).astype(bf16)


def join_norm(blocks, index, gain, rows, held=()):
    count = len(blocks)
    width = blocks[0].shape[1]
    size = 128
    block = pl.BlockSpec((size, width), lambda i: (i, 0))
    return call(
        partial(join_norm_kernel, count, width),
        held,
        grid=(rows // size,),
        in_specs=[pl.BlockSpec(memory_space=pltpu.SMEM), whole((1, count * width))] + [block] * count,
        out_specs=[
            pl.BlockSpec((size, count * width), lambda i: (i, 0)),
            pl.BlockSpec((size, LANES), lambda i: (i, 0)),
        ],
        out_shape=[
            jax.ShapeDtypeStruct((rows, count * width), bf16),
            jax.ShapeDtypeStruct((rows, LANES), f32),
        ],
        compiler_params=params(),
        cost_estimate=cost(3),
        name="join_norm",
    )(index, gain, *blocks)


def input_side_kernel(count, width, own_ref, dots_ref, block_ref, grad_ref, scale_ref, gain_ref, *refs):
    sent, out_ref, norm_ref = refs[: count - 1], refs[count - 1], refs[count]
    normed_grad = own_ref[...]
    for piece in sent:
        normed_grad = normed_grad + piece[...].astype(f32)
    scale = scale_ref[:, 0:1]
    rows = scale.shape[0]
    mean = jnp.broadcast_to(dots_ref[0:1, :] / width, (LANES, rows)).T[:, 0:1]
    normed_x = block_ref[...].astype(f32) * scale
    grad = grad_ref[...].astype(f32) + scale * (gain_ref[...] * normed_grad - normed_x * mean)
    out_ref[...] = grad.astype(bf16)
    norm = jnp.sum(normed_grad * normed_x, axis=0, keepdims=True)

    @pl.when(pl.program_id(0) == 0)
    def _():
        norm_ref[...] = norm

    @pl.when(pl.program_id(0) > 0)
    def _():
        norm_ref[...] += norm


def input_gradient(own, sent, dots, block, grad, scale, gain, width, held=()):
    rows, cols = own.shape
    size = 128
    part = pl.BlockSpec((size, cols), lambda i: (i, 0))
    return call(
        partial(input_side_kernel, len(sent) + 1, float(width)),
        held,
        grid=(rows // size,),
        in_specs=[
            part, pl.BlockSpec((8, size), lambda i: (0, i)), part, part, pl.BlockSpec((size, LANES), lambda i: (i, 0)),
            whole((1, cols)),
        ]
        + [part] * len(sent),
        out_specs=[part, whole((1, cols))],
        out_shape=[jax.ShapeDtypeStruct((rows, cols), bf16), jax.ShapeDtypeStruct((1, cols), f32)],
        compiler_params=params(),
        cost_estimate=cost(3),
        name="input_gradient",
    )(own, dots, block, grad, scale, gain, *sent)


def join_micro_kernel(count, width, held, places_ref, *refs):
    out_ref, refs = refs[-1], refs[held:]
    for n in range(count):
        start = pl.multiple_of((places_ref[0] ^ n) * width, LANES)
        out_ref[:, pl.ds(start, width)] = refs[n][...].astype(out_ref.dtype)


def join_micro(places, blocks, dtype, held=()):
    count = len(blocks)
    rows, width = blocks[0].shape
    size = rows // 4
    return pl.pallas_call(
        partial(join_micro_kernel, count, width, len(held)),
        grid_spec=pltpu.PrefetchScalarGridSpec(
            num_scalar_prefetch=1,
            grid=(4,),
            in_specs=[pl.BlockSpec(memory_space=pl.ANY)] * len(held)
            + [pl.BlockSpec((size, width), lambda i, places: (i, 0))] * count,
            out_specs=pl.BlockSpec((size, count * width), lambda i, places: (places[1] ^ i, 0)),
        ),
        out_shape=jax.ShapeDtypeStruct((rows, count * width), dtype),
        compiler_params=params(),
        cost_estimate=cost(5),
        name="join_micro",
    )(places, *held, *blocks)


def join_gathered_kernel(count, width, held, places_ref, *refs):
    out_ref, blocks_ref = refs[-1], refs[held]
    for n in range(count):
        out_ref[:, n * width : (n + 1) * width] = blocks_ref[n].astype(out_ref.dtype)


def join_gathered(places, blocks, dtype, held=()):
    count, rows, width = blocks.shape
    size = rows // 4
    return pl.pallas_call(
        partial(join_gathered_kernel, count, width, len(held)),
        grid_spec=pltpu.PrefetchScalarGridSpec(
            num_scalar_prefetch=1,
            grid=(4,),
            in_specs=[pl.BlockSpec(memory_space=pl.ANY)] * len(held)
            + [pl.BlockSpec((count, size, width), lambda i, places: (0, i, 0))],
            out_specs=pl.BlockSpec((size, count * width), lambda i, places: (places[1] ^ i, 0)),
        ),
        out_shape=jax.ShapeDtypeStruct((rows, count * width), dtype),
        compiler_params=params(),
        cost_estimate=cost(5),
        name="join_gathered",
    )(places, *held, blocks)


def place_maps_kernel(count, places_ref, term_ref, normed_ref, *refs):
    pieces, out_ref = refs[:count], refs[count]
    rows = pieces[0].shape[0]
    total = jnp.zeros(out_ref.shape, f32)
    for n in range(count):
        here = pl.ds(pl.multiple_of((places_ref[0] ^ n) * rows, 16), rows)
        total = total + mm_tn(normed_ref[here, :], pieces[n][...])
    out_ref[...] = total.astype(bf16)


def place_maps(index, term, normed, pieces, first_column):
    count = len(pieces)
    rows, width = pieces[0].shape
    depth = normed.shape[1]
    return pl.pallas_call(
        partial(place_maps_kernel, count),
        grid=(width // LANES,),
        in_specs=[pl.BlockSpec(memory_space=pltpu.SMEM), pl.BlockSpec(memory_space=pl.ANY), whole(normed.shape)]
        + [pl.BlockSpec((rows, LANES), lambda i: (0, i))] * count,
        out_specs=pl.BlockSpec((depth, LANES), lambda i: (0, i + first_column // LANES)),
        out_shape=jax.ShapeDtypeStruct(term.shape, term.dtype),
        input_output_aliases={1: 0},
        compiler_params=params(),
        cost_estimate=cost(3),
        name="place_maps",
    )(index, term, normed, *pieces)


def from_behind(block, axis, distance):
    devices = range(lax.axis_size(axis))
    route = [(i - distance, i) for i in devices if i - distance in devices]
    return lax.ppermute(block, axis, route)


def prefix(value, axis, join, neutral, backward):
    count, mine = (lax.axis_size(axis), lax.axis_index(axis))
    pieces = jax.tree.map(lambda part: lax.all_gather(part, axis), value)
    if backward:
        pieces = jax.tree.map(lambda part: part[::-1], pieces)
        mine = count - 1 - mine
    total = jax.tree.map(
        lambda part, zero: jnp.full_like(part, 0) + jnp.asarray(zero, part.dtype), value, neutral
    )

    def hop(position, total):
        longer = join(total, jax.tree.map(lambda part: part[position], pieces))
        return jax.tree.map(lambda new, old: jnp.where(position < mine, new, old), longer, total)

    return lax.fori_loop(0, count - 1, hop, total)


def block_step(decay_rate, carried, inputs):
    state_now, seg_before = carried
    x_block, rate_block, b_block, c_block, seg_block = inputs
    cumulative = jnp.cumsum(rate_block * decay_rate[None, :], axis=0)
    width_block = seg_block.shape[0]
    row_index = lax.broadcasted_iota(jnp.int32, (width_block, width_block), 0)
    col_index = lax.broadcasted_iota(jnp.int32, (width_block, width_block), 1)
    within = (row_index >= col_index) & (seg_block[:, None] == seg_block[None, :])
    within_heads = within[:, :, None]
    spread = cumulative[:, None, :] - cumulative[None, :, :]
    decay = jnp.where(within_heads, jnp.exp(jnp.where(within_heads, spread, 0.0)), 0.0)
    scores = jnp.dot(c_block, b_block.T, precision=precise)
    weights = scores[:, :, None] * decay * rate_block[None, :, :]
    output = jnp.einsum("tsh,shp->thp", weights, x_block, precision=precise)
    entering = jnp.exp(cumulative) * (seg_block == seg_before)[:, None].astype(jnp.float32)
    output = output + entering[:, :, None] * jnp.einsum(
        "tn,hpn->thp", c_block, state_now, precision=precise
    )
    leaving = (
        jnp.exp(cumulative[-1][None, :] - cumulative)
        * (seg_block == seg_block[-1])[:, None].astype(jnp.float32)
        * rate_block
    )
    state_next = entering[-1][:, None, None] * state_now + jnp.einsum(
        "sh,shp,sn->hpn", leaving, x_block, b_block, precision=precise
    )
    return ((state_next, seg_block[-1]), output)


def scan_blocks(x_heads, step_rate, b_part, c_part, seg_own, decay_rate, state_start, seg_start):
    blocks = x_heads.shape[0] // CH

    def to_blocks(value):
        return value.reshape((blocks, CH) + value.shape[1:])

    stepper = jax.checkpoint(partial(block_step, decay_rate))
    final_carry, output = lax.scan(
        stepper,
        (state_start, seg_start),
        (
            to_blocks(x_heads),
            to_blocks(step_rate),
            to_blocks(b_part),
            to_blocks(c_part),
            to_blocks(seg_own),
        ),
    )
    return (output.reshape(x_heads.shape), final_carry[0])


def causal_conv(padded_in, kernel, offset, seg_padded):
    own_rows = padded_in.shape[0] - (KC - 1)
    current = seg_padded[KC - 1 :]
    summed = jnp.zeros((own_rows, padded_in.shape[1]), jnp.float32) + offset[None, :]
    for tap_index in range(KC):
        shifted = padded_in[tap_index : tap_index + own_rows]
        same_doc = (seg_padded[tap_index : tap_index + own_rows] == current).astype(jnp.float32)
        summed = summed + kernel[tap_index][None, :] * shifted * same_doc[:, None]
    return summed


def chain_combine(earlier, later):
    return (earlier[0] * later[0], earlier[1] * later[0][:, None, None] + later[1])


def project_in(layer_in, gain_row, zx_full, bc_full, dt_full):
    inputs_f = layer_in.astype(jnp.float32)
    in_scale = lax.rsqrt(jnp.mean(inputs_f * inputs_f, axis=1) + epsilon)
    normed = (inputs_f * in_scale[:, None] * gain_row[None, :]).astype(jnp.bfloat16)
    model_width = zx_full.shape[0]
    inner_local = zx_full.shape[2]
    joined = jnp.dot(
        normed, zx_full.reshape(model_width, 2 * inner_local), preferred_element_type=jnp.float32
    )
    bc_pre = jnp.dot(normed, bc_full, preferred_element_type=jnp.float32)
    mixed_pre = jnp.concatenate([joined[:, inner_local:], bc_pre], axis=1).astype(jnp.bfloat16)
    step_pre = jnp.dot(normed, dt_full, preferred_element_type=jnp.float32)
    return (inputs_f, in_scale, normed, joined[:, :inner_local], mixed_pre, step_pre)


def mixer_parts(padded_in, step_pre, kernel, offset, bias_row, log_rate, seg_padded, heads_local):
    own_rows = step_pre.shape[0]
    inner_local = padded_in.shape[1] - 2 * N
    head_size = inner_local // heads_local
    conv_out = jax.nn.silu(causal_conv(padded_in, kernel, offset, seg_padded))
    x_heads = conv_out[:, :inner_local].reshape(own_rows, heads_local, head_size)
    b_part = conv_out[:, inner_local : inner_local + N]
    c_part = conv_out[:, inner_local + N :]
    step_rate = jax.nn.softplus(step_pre + bias_row[None, :])
    decay_rate = -jnp.exp(log_rate)
    seg_own = seg_padded[KC - 1 :]
    seg_start = seg_padded[KC - 2]
    local_out, local_state = scan_blocks(
        x_heads,
        step_rate,
        b_part,
        c_part,
        seg_own,
        decay_rate,
        jnp.zeros((heads_local, head_size, N), jnp.float32),
        seg_start,
    )
    carried = jnp.exp(jnp.cumsum(step_rate * decay_rate[None, :], axis=0)) * (seg_own == seg_start)[
        :, None
    ].astype(jnp.float32)
    return (x_heads, c_part, local_out, local_state, carried)


def mixer_tail(parts, state_in, gate_pre, skip_row):
    x_heads, c_part, local_out, local_state, carried = parts
    own_rows = gate_pre.shape[0]
    ssm_out = (
        local_out
        + carried[:, :, None] * jnp.einsum("tn,hpn->thp", c_part, state_in, precision=precise)
        + skip_row[None, :, None] * x_heads
    )
    gate_act = jax.nn.silu(gate_pre)
    gated = ssm_out.reshape(own_rows, gate_pre.shape[1]) * gate_act
    state_out = carried[-1][:, None, None] * state_in + local_state
    return ((gated, state_out), (carried, c_part, gate_act))


def select_batch(array_in, chosen):
    return lax.dynamic_index_in_dim(array_in, chosen, 0, keepdims=False)


def store_batch(buffer, value, chosen, valid):
    return jnp.where(valid, lax.dynamic_update_index_in_dim(buffer, value, chosen, 0), buffer)


def body(
    tokens,
    cotangent,
    seg_ids,
    norm_gain,
    in_zx,
    in_bc,
    in_dt,
    conv_x,
    conv_xb,
    conv_bc,
    conv_bcb,
    dt_bias,
    a_log,
    skip_gain,
    gate_gain,
    out_w,
):
    section_index = lax.axis_index("section")
    ctx_index = lax.axis_index("ctx")
    tensor_index = lax.axis_index("tensor")
    section_count = lax.axis_size("section")
    tensor_count = lax.axis_size("tensor")
    batches = tokens.shape[0]
    token_rows = tokens.shape[1]
    model_width = tokens.shape[2]
    zx_full, bc_full, dt_full, out_full = (
        lax.all_gather(in_zx[0], "ctx", axis=0, tiled=True),
        lax.all_gather(in_bc[0], "ctx", axis=0, tiled=True),
        lax.all_gather(in_dt[0], "ctx", axis=0, tiled=True),
        lax.all_gather(out_w[0], "ctx", axis=1, tiled=True),
    )
    inner_local = zx_full.shape[2]
    heads_local = dt_full.shape[1]
    head_size = inner_local // heads_local
    mixed_width = inner_local + 2 * N
    gain_row = norm_gain[0].astype(jnp.float32)
    kernel = jnp.concatenate([conv_x[0], conv_bc[0]], axis=1).astype(jnp.float32)
    offset = jnp.concatenate([conv_xb[0], conv_bcb[0]]).astype(jnp.float32)
    bias_row = dt_bias[0]
    log_rate = a_log[0]
    skip_row = skip_gain[0]
    gate_row = gate_gain[0].astype(jnp.float32)
    seg_lead = jnp.full((batches, KC - 1), -1, jnp.int32)
    seg_all = jnp.concatenate([seg_lead, seg_ids], axis=1)
    seg_local = lax.dynamic_slice_in_dim(seg_all, ctx_index * token_rows, token_rows + KC - 1, 1)
    chain_start = (
        jnp.ones((heads_local,), jnp.float32),
        jnp.zeros((heads_local, head_size, N), jnp.float32),
    )
    kept_inputs = jnp.zeros((batches, token_rows, model_width), jnp.bfloat16)
    kept_states = jnp.zeros((batches, heads_local, head_size, N), jnp.float32)
    kept_scales = jnp.zeros((batches, token_rows), jnp.float32)
    kept_edges = jnp.zeros((batches, KC - 1, mixed_width), jnp.bfloat16)
    section_store = jnp.zeros((batches, token_rows, model_width), jnp.bfloat16)
    received = jnp.zeros((token_rows, model_width), jnp.bfloat16)
    for tick_number in range(batches + section_count - 1):
        batch_index = tick_number - section_index
        valid = (batch_index >= 0) & (batch_index < batches)
        chosen = jnp.clip(batch_index, 0, batches - 1)
        layer_in = jnp.where(section_index == 0, select_batch(tokens, chosen), received)
        seg_padded = select_batch(seg_local, chosen)
        inputs_f, in_scale, normed, gate_pre, mixed_pre, step_pre = project_in(
            layer_in, gain_row, zx_full, bc_full, dt_full
        )
        edge_rows = from_behind(mixed_pre[token_rows - (KC - 1) :], "ctx", 1)
        padded_in = jnp.concatenate([edge_rows, mixed_pre], axis=0).astype(jnp.float32)
        parts = mixer_parts(
            padded_in, step_pre, kernel, offset, bias_row, log_rate, seg_padded, heads_local
        )
        state_in = prefix((parts[4][-1], parts[3]), "ctx", chain_combine, chain_start, False)[1]
        gated = mixer_tail(parts, state_in, gate_pre, skip_row)[0][0]
        squares = lax.psum(jnp.sum(gated * gated, axis=1), "tensor")
        gate_scale = lax.rsqrt(squares / DI + epsilon)
        gate_normed = (gated * gate_scale[:, None] * gate_row[None, :]).astype(jnp.bfloat16)
        projected = lax.psum(
            jnp.dot(gate_normed, out_full, preferred_element_type=jnp.float32), "tensor"
        )
        layer_out = (inputs_f + projected).astype(jnp.bfloat16)
        kept_inputs = store_batch(kept_inputs, layer_in, chosen, valid)
        kept_states = store_batch(kept_states, state_in, chosen, valid)
        kept_scales = store_batch(kept_scales, gate_scale, chosen, valid)
        kept_edges = store_batch(kept_edges, edge_rows, chosen, valid)
        section_store = store_batch(section_store, layer_out, chosen, valid)
        received = from_behind(layer_out, "section", 1)
    acc_zx = jnp.zeros((model_width, 2 * inner_local), jnp.float32)
    acc_dt = jnp.zeros((model_width, heads_local), jnp.float32)
    acc_out = jnp.zeros((inner_local, model_width), jnp.float32)
    acc_bc = jnp.zeros((model_width, 2 * N), jnp.float32)
    acc_gain = jnp.zeros((model_width,), jnp.float32)
    acc_kernel = jnp.zeros((KC, mixed_width), jnp.float32)
    acc_offset = jnp.zeros((mixed_width,), jnp.float32)
    acc_bias = jnp.zeros((heads_local,), jnp.float32)
    acc_log = jnp.zeros((heads_local,), jnp.float32)
    acc_skip = jnp.zeros((heads_local,), jnp.float32)
    acc_gate = jnp.zeros((inner_local,), jnp.float32)
    grad_store = jnp.zeros((batches, token_rows, model_width), jnp.float32)
    received_grad = jnp.zeros((token_rows, model_width), jnp.bfloat16)
    last_section = section_count - 1
    contract = (((0,), (0,)), ((), ()))
    for tick_number in range(batches + section_count - 1):
        batch_index = batches - 1 - tick_number + (last_section - section_index)
        valid = (batch_index >= 0) & (batch_index < batches)
        chosen = jnp.clip(batch_index, 0, batches - 1)
        out_grad = jnp.where(
            section_index == last_section, select_batch(cotangent, chosen), received_grad
        )
        seg_padded = select_batch(seg_local, chosen)
        inputs_f, in_scale, normed, gate_pre, mixed_pre, step_pre = project_in(
            select_batch(kept_inputs, chosen), gain_row, zx_full, bc_full, dt_full
        )
        padded_in = jnp.concatenate([select_batch(kept_edges, chosen), mixed_pre], axis=0).astype(
            jnp.float32
        )
        state_in = select_batch(kept_states, chosen)
        gate_scale = select_batch(kept_scales, chosen)

        def local_mixer(
            padded_arg,
            gate_arg,
            step_arg,
            state_arg,
            kernel_arg,
            offset_arg,
            bias_arg,
            log_arg,
            skip_arg,
        ):
            return mixer_tail(
                mixer_parts(
                    padded_arg,
                    step_arg,
                    kernel_arg,
                    offset_arg,
                    bias_arg,
                    log_arg,
                    seg_padded,
                    heads_local,
                ),
                state_arg,
                gate_arg,
                skip_arg,
            )

        outputs, pullback, extras = jax.vjp(
            local_mixer,
            padded_in,
            gate_pre,
            step_pre,
            state_in,
            kernel,
            offset,
            bias_row,
            log_rate,
            skip_row,
            has_aux=True,
        )
        gated = outputs[0]
        carried, c_part, gate_act = extras
        gate_normed = (gated * gate_scale[:, None] * gate_row[None, :]).astype(jnp.bfloat16)
        normed_gate_grad = jnp.dot(out_grad, out_full.T, preferred_element_type=jnp.float32)
        out_term = lax.dot_general(
            gate_normed, out_grad, contract, preferred_element_type=jnp.float32
        )
        gate_term = jnp.sum(normed_gate_grad * gated * gate_scale[:, None], axis=0)
        projection = lax.psum(
            jnp.sum(normed_gate_grad * gate_row[None, :] * gated, axis=1), "tensor"
        )
        gated_grad = (
            gate_scale[:, None] * gate_row[None, :] * normed_gate_grad
            - gated * (gate_scale**3 * projection / DI)[:, None]
        )
        out_heads = (gated_grad * gate_act).reshape(token_rows, heads_local, head_size)
        pull_state = jnp.einsum("th,thp,tn->hpn", carried, out_heads, c_part, precision=precise)
        state_after = prefix((carried[-1], pull_state), "ctx", chain_combine, chain_start, True)[1]
        (
            padded_grad,
            gate_grad,
            step_grad,
            unused_state,
            kernel_grad,
            offset_grad,
            bias_grad,
            log_grad,
            skip_grad,
        ) = pullback((gated_grad, state_after))
        edge_grad = from_behind(padded_grad[: KC - 1], "ctx", -1)
        mixed_grad = padded_grad[KC - 1 :].at[token_rows - (KC - 1) :].add(edge_grad)
        zx_grad = jnp.concatenate(
            [gate_grad.astype(jnp.bfloat16), mixed_grad[:, :inner_local].astype(jnp.bfloat16)],
            axis=1,
        )
        bc_grad = mixed_grad[:, inner_local:]
        step_low = step_grad.astype(jnp.bfloat16)
        normed_grad = jnp.dot(
            zx_grad,
            zx_full.reshape(model_width, 2 * inner_local).T,
            preferred_element_type=jnp.float32,
        )
        normed_grad = normed_grad + jnp.dot(step_low, dt_full.T, preferred_element_type=jnp.float32)
        normed_grad = normed_grad + jnp.dot(
            bc_grad, bc_full.astype(jnp.float32).T, precision=precise
        )
        zx_term = lax.dot_general(normed, zx_grad, contract, preferred_element_type=jnp.float32)
        dt_term = lax.dot_general(normed, step_low, contract, preferred_element_type=jnp.float32)
        bc_term = lax.dot_general(normed.astype(jnp.float32), bc_grad, contract, precision=precise)
        normed_grad = lax.psum(normed_grad.astype(jnp.bfloat16), "tensor").astype(jnp.float32)
        normed_x = inputs_f * in_scale[:, None]
        weighted = gain_row[None, :] * normed_grad
        input_grad = out_grad.astype(jnp.float32) + in_scale[:, None] * (
            weighted - normed_x * jnp.mean(weighted * normed_x, axis=1)[:, None]
        )
        norm_term = jnp.sum(normed_grad * normed_x, axis=0)
        sent_grad = input_grad.astype(jnp.bfloat16)
        grad_store = store_batch(
            grad_store,
            jnp.where(section_index == 0, input_grad, sent_grad.astype(jnp.float32)),
            chosen,
            valid,
        )
        acc_zx = jnp.where(valid, acc_zx + zx_term, acc_zx)
        acc_dt = jnp.where(valid, acc_dt + dt_term, acc_dt)
        acc_out = jnp.where(valid, acc_out + out_term, acc_out)
        acc_bc = jnp.where(valid, acc_bc + bc_term, acc_bc)
        acc_gain = jnp.where(valid, acc_gain + norm_term, acc_gain)
        acc_kernel = jnp.where(valid, acc_kernel + kernel_grad, acc_kernel)
        acc_offset = jnp.where(valid, acc_offset + offset_grad, acc_offset)
        acc_bias = jnp.where(valid, acc_bias + bias_grad, acc_bias)
        acc_log = jnp.where(valid, acc_log + log_grad, acc_log)
        acc_skip = jnp.where(valid, acc_skip + skip_grad, acc_skip)
        acc_gate = jnp.where(valid, acc_gate + gate_term, acc_gate)
        received_grad = from_behind(sent_grad, "section", -1)
    zx_sum, dt_sum, out_sum = (
        lax.psum_scatter(
            acc_zx.reshape(model_width, 2, inner_local).astype(jnp.bfloat16),
            "ctx",
            scatter_dimension=0,
            tiled=True,
        ).astype(jnp.float32),
        lax.psum_scatter(
            acc_dt.astype(jnp.bfloat16), "ctx", scatter_dimension=0, tiled=True
        ).astype(jnp.float32),
        lax.psum_scatter(
            acc_out.astype(jnp.bfloat16), "ctx", scatter_dimension=1, tiled=True
        ).astype(jnp.float32),
    )
    first_tensor = (tensor_index == 0).astype(jnp.float32)

    def widen(piece):
        full_shape = piece.shape[:-1] + (piece.shape[-1] * tensor_count,)
        return lax.dynamic_update_slice_in_dim(
            jnp.zeros(full_shape, jnp.float32),
            piece,
            tensor_index * piece.shape[-1],
            piece.ndim - 1,
        )

    def narrow(full_array):
        own_width = full_array.shape[-1] // tensor_count
        return lax.dynamic_slice_in_dim(
            full_array, tensor_index * own_width, own_width, full_array.ndim - 1
        )

    sums = lax.psum(
        (
            acc_bc,
            acc_gain * first_tensor,
            acc_kernel[:, inner_local:],
            acc_offset[inner_local:],
            widen(acc_kernel[:, :inner_local]),
            widen(acc_offset[:inner_local]),
            widen(acc_bias),
            widen(acc_log),
            widen(acc_skip),
            widen(acc_gate),
        ),
        ("ctx", "tensor"),
    )
    rows_own = in_bc.shape[1]
    bc_rows = lax.dynamic_slice_in_dim(sums[0], ctx_index * rows_own, rows_own, 0)
    return (
        section_store[None],
        grad_store[None],
        sums[1][None],
        zx_sum[None],
        bc_rows[None],
        dt_sum[None],
        narrow(sums[4])[None],
        narrow(sums[5])[None],
        sums[2][None],
        sums[3][None],
        narrow(sums[6])[None],
        narrow(sums[7])[None],
        narrow(sums[8])[None],
        narrow(sums[9])[None],
        out_sum[None],
    )


def swap_section(value):
    return lax.ppermute(value, "section", [(0, 1), (1, 0)])


def from_partner(value, distance):
    count = lax.axis_size("tensor")
    return lax.ppermute(value, "tensor", [(i, i ^ distance) for i in range(count)])


def with_partners(value):
    return [value] + [from_partner(value, k) for k in range(1, lax.axis_size("tensor"))]


def sum_over_tensor(value):
    return sum(with_partners(value)[1:], value)


def column_block(value, index, width):
    return lax.dynamic_slice_in_dim(value, index * width, width, value.ndim - 1)


def zero_of(value):
    return jnp.minimum(jnp.abs(value[(0,) * value.ndim].astype(f32)).astype(jnp.int32), 0)


def to_micro(value):
    section, ctx, tensor = (lax.axis_index(a) for a in ("section", "ctx", "tensor"))
    count = lax.axis_size("ctx")
    width = value.shape[2] // lax.axis_size("tensor")
    came = []
    for e in range(2):
        sent = 2 * section + ((ctx & 1) ^ e)
        piece = lax.dynamic_slice(value, (sent, 0, tensor * width), (1, value.shape[1], width))[0]
        route = [(s * count + c, (c >> 1) * count + 2 * s + ((c & 1) ^ e)) for s in range(2) for c in range(count)]
        came.append(lax.ppermute(piece, ("section", "ctx"), route))
    even = (ctx & 1) == 0
    return jnp.concatenate([jnp.where(even, came[0], came[1]), jnp.where(even, came[1], came[0])], axis=0)


def to_owners(blocks):
    section, ctx, count = lax.axis_index("section"), lax.axis_index("ctx"), lax.axis_size("ctx")
    rows = blocks[0].shape[0] // 2
    pieces = []
    for e in range(count):
        half, layer = (ctx ^ e) & 1, (ctx ^ e) >> 1
        piece = lax.dynamic_slice_in_dim(jnp.where(layer == 0, blocks[0], blocks[1]), half * rows, rows, 0)
        route = [
            (s * count + z, ((z ^ e) >> 1) * count + 2 * s + ((z ^ e) & 1)) for s in range(2) for z in range(count)
        ]
        pieces.append(lax.ppermute(piece, ("section", "ctx"), route))
    ordered = []
    for n in range(count):
        wanted = ctx ^ n
        e = ((wanted ^ ctx) & 1) | ((((wanted >> 1) ^ section) & 1) << 1)
        chosen = pieces[count - 1]
        for k in range(count - 1):
            chosen = jnp.where(e == k, pieces[k], chosen)
        ordered.append(chosen)
    return jnp.concatenate(ordered, axis=0)


def in_halves(own, section):
    half = own.shape[0] // 2
    keep = lax.dynamic_slice_in_dim(own, section * half, half, 0)
    came = swap_section(lax.dynamic_slice_in_dim(own, (1 - section) * half, half, 0))
    return [jnp.where(section == layer, keep, came) for layer in range(2)]


def own_layer(halves, section):
    keep = jnp.where(section == 0, halves[0], halves[1])
    came = swap_section(jnp.where(section == 0, halves[1], halves[0]))
    return jnp.concatenate([jnp.where(section == 0, keep, came), jnp.where(section == 0, came, keep)], axis=0)


def token_marks(seg_around, rows):
    own = seg_around[HALO : HALO + rows]
    columns = [seg_around[HALO - KC + 1 + k : HALO - KC + 1 + k + rows] == own for k in range(KC)]
    columns += [seg_around[HALO + KC - 1 - k : HALO + KC - 1 - k + rows] == own for k in range(KC)]
    chunks = rows // CH
    before = seg_around[HALO - 1 : HALO - 1 + rows].reshape(chunks, CH)[:, :1]
    last = own.reshape(chunks, CH)[:, -1:]
    columns.append((own.reshape(chunks, CH) == before).reshape(rows))
    columns.append((own.reshape(chunks, CH) == last).reshape(rows))
    columns = [column.astype(f32) for column in columns] + [own.astype(f32)]
    marks = jnp.pad(jnp.stack(columns, axis=1), ((0, 0), (0, LANES - len(columns))))
    return marks, jnp.broadcast_to(own.astype(f32)[None, :], (8, rows))


class Layer:
    pass


def lane_row(values):
    return jnp.pad(values, (0, LANES - values.shape[0]))[None, :]


def pair_rows(values, per):
    pairs = values.shape[0] // per
    padded = jnp.pad(values.reshape(pairs, per), ((0, 0), (0, 8 - per)))
    return jnp.broadcast_to(padded[:, :, None], (pairs, 8, LANES))


def from_pairs(values, per):
    return values[:, :per, 0].reshape(-1)


def unpack(pack, heads, head_size, inner, width):
    layer = Layer()
    layer.taps = jnp.concatenate([pack[: KC + 1, : inner + 2 * N], jnp.zeros((8 - KC - 1, inner + 2 * N), f32)], axis=0)
    layer.norm_gain = pack[KC + 1 : KC + 2, :width]
    layer.gate_gain = pack[KC + 2 : KC + 3, :inner]
    small = pack[KC + 3, : 3 * heads].reshape(3, heads)
    per = LANES // head_size
    decay = -jnp.exp(small[1])
    layer.bias_lanes, layer.decay_lanes = lane_row(small[0]), lane_row(decay)
    layer.bias_rows, layer.decay_rows = pair_rows(small[0], per), pair_rows(decay, per)
    layer.skip = jnp.repeat(small[2], head_size)[None, :]
    return layer


transposed = (((0,), (0,)), ((), ()))
across = (((1,), (1,)), ((), ()))


def project(layer, marks, seg_row, head_size, held=()):
    layer.pre = jnp.dot(layer.normed, layer.mix[:, LANES:], preferred_element_type=f32).astype(bf16)
    step = jnp.dot(layer.normed, layer.mix[:, :LANES], preferred_element_type=f32)
    layer.halo = lax.ppermute(layer.pre[-HALO:], "section", [(0, 1)])
    (layer.conv, layer.y, layer.own_state, last_state, layer.cum, layer.rate, layer.cum_rows, layer.step_rows) = scan_forward(
        layer.pre, layer.halo, layer.taps, marks, seg_row, step, layer.bias_lanes, layer.decay_lanes, head_size, held
    )
    layer.state_in = lax.ppermute(last_state, "section", [(0, 1)])


def gate(layer, marks, grad=None):
    layer.gate = jnp.dot(layer.normed, layer.gate_weight, preferred_element_type=f32)
    layer.ssm, layer.gained, layer.entering, sums = gate_forward(
        layer.y, layer.conv, layer.cum, marks, layer.own_state, layer.state_in, layer.gate, layer.skip, layer.gate_gain, grad
    )
    return sum_over_tensor(sums)


def gate_side(layer, grad, sums, marks, channels, held=()):
    (layer.out_grad, layer.gate_grad, layer.pulled, first, layer.gain_grad, layer.skip_grad, layer.gate_dots) = gate_backward(
        grad, layer.gate, layer.ssm, layer.conv, layer.cum, marks, sums, layer.gate_gain, channels, held
    )
    layer.after = lax.ppermute(first, "section", [(1, 0)])


def scan_side(layer, marks, seg_row, head_size, held_intra=(), held_scan=(), held_conv=(), after_intra=None, late_held=None):
    per = LANES // head_size
    scaled_grad, rate_rows, b_intra, c_intra = intra_backward(
        layer.out_grad, layer.conv, layer.cum, layer.rate, layer.cum_rows, marks, seg_row, head_size, held_intra
    )
    if after_intra is not None:
        held_conv = (*held_conv, *after_intra(rate_rows))
    conv_grad, layer.taps_grad, step_grad, log_grad, bias_grad = scan_backward(
        layer.out_grad, scaled_grad, layer.conv, layer.cum, layer.rate, rate_rows, layer.step_rows, layer.entering,
        layer.pulled, layer.after, layer.skip, layer.decay_rows, b_intra, c_intra, layer.pre, layer.halo,
        layer.taps, marks, head_size, held_scan,
    )
    next_grad = lax.ppermute(conv_grad[:8], "section", [(1, 0)])
    if late_held is not None:
        held_conv = (*held_conv, *late_held(conv_grad))
    layer.mix_grad, layer.map_grad, dots = conv_backward(
        conv_grad, next_grad, layer.taps, marks, layer.pre, layer.gate_dots, step_grad, layer.step_rows,
        layer.bias_rows, head_size, held_conv,
    )
    layer.dots = sum_over_tensor(dots)
    heads = layer.skip_grad.shape[1] // head_size
    layer.small = jnp.concatenate([
        from_pairs(bias_grad, per), from_pairs(log_grad, per), layer.skip_grad.reshape(heads, head_size).sum(axis=1)
    ])


def scatter_rows(term):
    return lax.psum_scatter(term, ("ctx", "section"), scatter_dimension=0, tiled=True)


def whole_micro_body(
    tokens, cotangent, seg_ids, norm_gain, in_zx, in_bc, in_dt, conv_x, conv_xb, conv_bc, conv_bcb, dt_bias, a_log,
    skip_gain, gate_gain, out_w,
):
    section, ctx, tensor = (lax.axis_index(a) for a in ("section", "ctx", "tensor"))
    tensors, ctxs = lax.axis_size("tensor"), lax.axis_size("ctx")
    width = tokens.shape[2]
    own_width = width // tensors
    inner = conv_x.shape[2]
    heads = dt_bias.shape[1]
    head_size = inner // heads
    mixed = inner + 2 * N
    channels = inner * tensors
    rows = seg_ids.shape[1] // 2
    index = tensor.astype(jnp.int32).reshape(1)

    def block_rows(weight, b):
        return lax.dynamic_slice_in_dim(weight, b * own_width, own_width, 0)

    def gather_rows(half):
        return lax.all_gather(half, ("ctx", "section"), axis=0, tiled=True)

    own_mix = jnp.concatenate([jnp.pad(in_dt[0], ((0, 0), (0, LANES - heads))), in_zx[0, :, 1], in_bc[0]], axis=1)
    mix_halves = in_halves(own_mix, section)
    mix_first = gather_rows(mix_halves[0])
    token_block = to_micro(tokens)
    rest_halves = in_halves(jnp.concatenate([in_zx[0, :, 0], out_w[0].T], axis=1), section)

    def line(values):
        return jnp.pad(values.astype(f32), (0, width - values.shape[0]))[None, :]

    own_pack = jnp.concatenate(
        [line(jnp.concatenate([conv_x[0, k], conv_bc[0, k]])) for k in range(KC)]
        + [
            line(jnp.concatenate([conv_xb[0], conv_bcb[0]])), line(norm_gain[0]), line(gate_gain[0]),
            line(jnp.concatenate([dt_bias[0], a_log[0], skip_gain[0]])),
        ],
        axis=0,
    )
    other_pack = swap_section(own_pack)
    first, second = (
        unpack(jnp.where(section == n, own_pack, other_pack), heads, head_size, inner, width) for n in range(2)
    )
    seg_mine = lax.dynamic_index_in_dim(seg_ids, ctx, 0, keepdims=False)
    seg_around = jnp.concatenate([jnp.full((HALO,), -1, jnp.int32), seg_mine, jnp.full((HALO,), -2, jnp.int32)])
    seg_around = lax.dynamic_slice_in_dim(seg_around, section * rows, rows + 2 * HALO, 0)
    marks, seg_row = token_marks(seg_around, rows)

    first.block = token_block
    first.gate_weight = gather_rows(ordered(rest_halves[0][:, :inner], token_block))
    first.normed, first.in_scale = join_norm(with_partners(first.block), index, first.norm_gain, rows)
    first.out_turned = gather_rows(ordered(rest_halves[0][:, inner:], first.normed))
    first.mix = mix_first
    project(first, marks, seg_row, head_size)
    second.mix = gather_rows(ordered(mix_halves[1], first.pre))
    rest_second = gather_rows(ordered(rest_halves[1], first.conv))
    second.gate_weight, second.out_turned = rest_second[:, :inner], rest_second[:, inner:]
    cot_block = to_micro(ordered(cotangent, first.pre))
    sums_first = gate(first, marks)

    def gate_low(layer, sums):
        layer.gated = (layer.gained * lax.rsqrt(sums[0] / channels + epsilon)[:, None]).astype(bf16)

    def blocks_of(total, dtype):
        parts = [column_block(total, tensor ^ n, own_width) for n in range(tensors)]
        return [parts[0]] + [part.astype(dtype) for part in parts[1:]]

    def out_terms(layer, dtype):
        return blocks_of(lax.dot_general(layer.gated, layer.out_turned, across, preferred_element_type=f32), dtype)

    gate_low(first, sums_first)
    terms = out_terms(first, f32)
    projected = sum([from_partner(terms[n], n) for n in range(1, tensors)], terms[0])
    second.block = (first.block.astype(f32) + projected).astype(bf16)

    second.normed, second.in_scale = join_norm(with_partners(second.block), index, second.norm_gain, rows)
    project(second, marks, seg_row, head_size)
    cot_full = join(with_partners(ordered(cot_block, second.pre)), index, bf16, 0)
    grad_second = jnp.dot(cot_full, second.out_turned, preferred_element_type=f32)
    sums_second = gate(second, marks, grad_second)

    def input_terms(layer):
        total = lax.dot_general(layer.gate_grad, layer.gate_weight, across, preferred_element_type=f32)
        total = total + lax.dot_general(layer.mix_grad, layer.mix, across, preferred_element_type=f32)
        return blocks_of(total, bf16)

    def send_terms(layer, terms):
        return [from_partner(ordered(terms[n], layer.dots), n) for n in range(1, tensors)]

    def input_side(layer, own, sent, out_grad_block, held=()):
        return input_gradient(
            own, sent, layer.dots, layer.block, out_grad_block, layer.in_scale,
            column_block(layer.norm_gain, tensor, own_width), width, held,
        )

    def rest_term(layer, out_grad, *others):
        low = [
            lax.dot_general(layer.normed, ordered(layer.gate_grad, *others), transposed, preferred_element_type=f32).astype(bf16),
            lax.dot_general(out_grad, layer.gated, transposed, preferred_element_type=f32).astype(bf16),
        ]
        return jnp.concatenate(low, axis=1)

    def share(layer, *others):
        count = rows // tensors
        map_grad = ordered(layer.map_grad, *others)

        def part(b):
            return lax.dynamic_slice_in_dim(map_grad, b * count, count, 0)

        total = sum([from_partner(part(tensor ^ k), k) for k in range(1, tensors)], part(tensor))
        layer.map_share = total.astype(bf16)

    def mix_start(layer):
        return lax.dot_general(layer.normed, layer.mix_grad, transposed, preferred_element_type=f32).astype(bf16)

    def mix_term(layer, started, *others):
        pieces = [ordered(piece, *others) for piece in with_partners(layer.map_share)]
        return place_maps(index, started, layer.normed, pieces, LANES + inner)

    def small_pack(layer, norm_grad):
        def row(values):
            return jnp.pad(values, (0, mixed - values.shape[0]))[None, :]

        return jnp.concatenate(
            [layer.taps_grad, row(layer.gain_grad[0]), row(layer.small), row(norm_grad[0]), jnp.zeros((5, mixed), f32)], axis=0
        )

    gate_low(second, sums_second)
    out_second = lax.dot_general(second.gated, second.out_turned, across, preferred_element_type=f32).astype(bf16)
    result = lax.psum_scatter(out_second, "tensor", scatter_dimension=1, tiled=True)
    gate_side(second, grad_second, sums_second, marks, channels, (out_second,))
    rest_term_second = rest_term(second, cot_full)
    rest_sum_second = scatter_rows(rest_term_second)
    scan_side(second, marks, seg_row, head_size, held_scan=(rest_term_second,), held_conv=(result,))
    terms = input_terms(second)
    sent = send_terms(second, terms)
    middle_block, norm_second = input_side(second, terms[0], sent, cot_block)
    share(second, *sent)
    result = (second.block.astype(f32) + ordered(result, second.dots).astype(f32)).astype(bf16)
    output_pieces = to_owners([second.block, result])
    mix_started = mix_start(second)
    middle = join(with_partners(middle_block), index, bf16, 0, (mix_started, output_pieces))
    mix_term_second = mix_term(second, mix_started, rest_sum_second, middle)
    mix_sum_second = scatter_rows(mix_term_second)

    grad_first = jnp.dot(middle, first.out_turned, preferred_element_type=f32)
    crossed = jnp.sum(grad_first * first.gained, axis=1)
    crossed = sum_over_tensor(jnp.broadcast_to(crossed[None, :], (8, rows)))
    sums_first = jnp.concatenate([sums_first[:1], crossed[:1], sums_first[2:]], axis=0)
    gate_side(first, grad_first, sums_first, marks, channels)
    outputs = lax.all_gather(ordered(output_pieces, first.out_grad), "tensor", axis=0, tiled=False)
    rest_terms = []

    def after_scan(conv_grad):
        rest_terms.append(rest_term(first, middle, conv_grad))
        return rest_terms

    scan_side(
        first, marks, seg_row, head_size, held_intra=(mix_term_second,), held_conv=(rest_sum_second, mix_sum_second), late_held=after_scan,
    )
    rest_sum_first = scatter_rows(rest_terms[0])
    terms = input_terms(first)
    sent = send_terms(first, terms)
    share(first, first.dots)
    last_block, norm_first = input_side(first, terms[0], sent, middle_block, (outputs,))
    grad_pieces = to_owners([last_block, middle_block])
    grads = with_partners(grad_pieces)
    mix_sum_first = scatter_rows(mix_term(first, mix_start(first), rest_sum_first, grad_pieces))
    places = jnp.stack([tensor, ctx]).astype(jnp.int32)
    outputs = join_gathered(places, outputs, bf16, (last_block,))

    rest_sum = own_layer([rest_sum_first, rest_sum_second], section).astype(f32)
    mix_sum = own_layer([mix_sum_first, mix_sum_second], section).astype(f32)
    bc_sum = mix_sum[:, LANES + inner :]
    pack_first, pack_second = ordered(small_pack(first, norm_first), grads[1]), small_pack(second, norm_second)
    pack = jnp.where(section == 0, pack_first, pack_second) + swap_section(
        jnp.where(section == 0, pack_second, pack_first)
    )
    pack = sum(
        [lax.ppermute(pack, "ctx", [(c, (c + d) % ctxs) for c in range(ctxs)]) for d in range(1, ctxs)], pack
    )
    shared = with_partners(jnp.concatenate([pack[:8, inner:], jnp.broadcast_to(pack[10:11, :own_width], (8, own_width))], axis=1))
    taps_bc = sum([piece[:, : 2 * N] for piece in shared[1:]], shared[0][:, : 2 * N])
    norm = join([piece[:, 2 * N :] for piece in shared], index, f32, 0)[0]
    small = pack[9, : 3 * heads].reshape(3, heads)
    zx_sum = jnp.stack([rest_sum[:, :inner], mix_sum[:, LANES : LANES + inner]], axis=1)
    out_sum = rest_sum[:, inner:].T
    input_grads = join_micro(places, grads, f32, (outputs,))
    return (
        outputs.reshape(1, ctxs, -1, width),
        input_grads.reshape(1, ctxs, -1, width),
        norm[None],
        zx_sum[None],
        bc_sum[None],
        mix_sum[:, :heads][None],
        pack[:KC, :inner][None],
        pack[KC, :inner][None],
        taps_bc[:KC][None],
        taps_bc[KC][None],
        small[0][None],
        small[1][None],
        small[2][None],
        pack[8, :inner][None],
        out_sum[None],
    )


def fits(shape, batches):
    return shape["ctx"] == batches == 4 and shape["section"] == 2 and shape["tensor"] & (shape["tensor"] - 1) == 0


def solution(mesh):
    def step(*args):
        chosen = whole_micro_body if fits(dict(mesh.shape), args[0].shape[0]) else body
        return jax.shard_map(
            chosen,
            mesh=mesh,
            in_specs=(
                P(None, "ctx", None),
                P(None, "ctx", None),
                P(),
                P("section", None),
                P("section", "ctx", None, "tensor"),
                P("section", "ctx", None),
                P("section", "ctx", "tensor"),
                P("section", None, "tensor"),
                P("section", "tensor"),
                P("section", None, None),
                P("section", None),
                P("section", "tensor"),
                P("section", "tensor"),
                P("section", "tensor"),
                P("section", "tensor"),
                P("section", "tensor", "ctx"),
            ),
            out_specs=(
                P("section", None, "ctx", None),
                P("section", None, "ctx", None),
                P("section", None),
                P("section", "ctx", None, "tensor"),
                P("section", "ctx", None),
                P("section", "ctx", "tensor"),
                P("section", None, "tensor"),
                P("section", "tensor"),
                P("section", None, None),
                P("section", None),
                P("section", "tensor"),
                P("section", "tensor"),
                P("section", "tensor"),
                P("section", "tensor"),
                P("section", "tensor", "ctx"),
            ),
            check_vma=False,
        )(*args)

    return step
```

```python
from functools import partial

import jax
import jax.numpy as jnp
from jax import lax
from jax.experimental import pallas as pl
from jax.experimental.pallas import tpu as pltpu
from jax.sharding import PartitionSpec as P

bf16 = jnp.bfloat16
f32 = jnp.float32
precise = lax.Precision.HIGHEST
epsilon = 1e-05
N = 128
KC = 4
CH = 256
DI = 3072
HALO = 16
LANES = 128
VMEM_BYTES = 60 * 1024 * 1024

M_FWD, M_BWD, M_ENTER, M_LEAVE, M_SEG = 0, 4, 8, 9, 10


def mm(a, b):
    return lax.dot_general(a, b, (((1,), (0,)), ((), ())), preferred_element_type=f32)


def mm_nt(a, b, precision=None):
    return lax.dot_general(a, b, (((1,), (1,)), ((), ())), preferred_element_type=f32, precision=precision)


def mm_tn(a, b):
    return lax.dot_general(a, b, (((0,), (0,)), ((), ())), preferred_element_type=f32)


def split(v):
    high = v.astype(bf16)
    return high, (v - high.astype(f32)).astype(bf16)


def rows_of(selector, values):
    high, low = split(values)
    return mm_nt(selector, high) + mm_nt(selector, low)


def times_mask(rows, mask):
    high, low = split(rows)
    return mm(high, mask) + mm(low, mask)


def left_parts(a):
    high, low = split(a)
    return jnp.concatenate([high, low, high], axis=1)


def right_parts(b, axis):
    high, low = split(b)
    return jnp.concatenate([high, high, low], axis=axis)


def thirds(v):
    high = v.astype(bf16)
    rest = v - high.astype(f32)
    middle = rest.astype(bf16)
    return high, middle, (rest - middle.astype(f32)).astype(bf16)


def left_exact(a):
    high, middle, low = thirds(a)
    return jnp.concatenate([high, middle, high, middle, low, high], axis=1)


def right_exact(b, axis):
    high, middle, low = thirds(b)
    return jnp.concatenate([high, high, middle, middle, high, low], axis=axis)


def precise_nt(a, b):
    return mm_nt(left_parts(a), right_parts(b, 1))


def precise_mm(a, b):
    return mm(left_parts(a), right_parts(b, 0))


def iota2(shape):
    return lax.broadcasted_iota(jnp.int32, shape, 0), lax.broadcasted_iota(jnp.int32, shape, 1)


def sigmoid(v):
    return 1.0 / (1.0 + jnp.exp(-v))


def softplus(v):
    return jnp.maximum(v, 0.0) + jnp.log1p(jnp.exp(-jnp.abs(v)))


def fill_padded(padded, halo_ref, pre_ref, rows):
    padded[pl.ds(0, HALO), :] = halo_ref[...].astype(f32)
    padded[pl.ds(HALO, rows), :] = pre_ref[...].astype(f32)


def spread_marks(wide, marks_ref, first):
    for k in range(KC - 1):
        wide[k] = jnp.broadcast_to(marks_ref[:, first + k : first + k + 1], wide.shape[1:])


def conv_tile(padded, taps_ref, marks, start, count):
    total = jnp.zeros((count, LANES), f32) + taps_ref[KC : KC + 1, :]
    for k in range(KC):
        shifted = padded[pl.ds(start + HALO - KC + 1 + k, count), :]
        if k == KC - 1:
            total = total + taps_ref[k : k + 1, :] * shifted
        else:
            total = total + taps_ref[k : k + 1, :] * (shifted * marks[k, pl.ds(start, count), :])
    return total


TILE = 128


def scan_forward_kernel(
    head_size, rows, pre_ref, halo_ref, taps_ref, marks_ref, seg_ref, step_ref, bias_ref, decay_ref,
    conv_ref, y_ref, own_state_ref, last_state_ref, cum_ref, rate_ref, cum_rows_ref, step_rows_ref,
    padded, b_all, b_turned, scores, cum_all, rate_all, step_all, cum_turned, step_turned, wide_marks,
):
    i = pl.program_id(0)
    chunks = rows // CH
    fill_padded(padded, halo_ref, pre_ref, rows)

    @pl.when(i == 0)
    def _():
        spread_marks(wide_marks, marks_ref, M_FWD)

    for start in range(0, rows, TILE):
        value = conv_tile(padded, taps_ref, wide_marks, start, TILE)
        conv_ref[pl.ds(start, TILE), :] = value / (1.0 + jnp.exp(-value))

    @pl.when(i == 0)
    def _():
        b_all[...] = conv_ref[...]
        b_turned[...] = conv_ref[...].T
        shifted = step_ref[...] + bias_ref[...]
        rate = softplus(shifted)
        step_all[...] = shifted
        rate_all[...] = rate
        r, c = iota2((CH, CH))
        tri = (r >= c).astype(f32)
        for n in range(chunks):
            part = rate[n * CH : (n + 1) * CH, :] * decay_ref[...]
            cum_all[pl.ds(n * CH, CH), :] = lax.dot_general(
                tri, part, (((1,), (0,)), ((), ())), preferred_element_type=f32, precision=precise
            )

    @pl.when(i == 1)
    def _():
        r, c = iota2((CH, CH))
        for n in range(chunks):
            here = pl.ds(n * CH, CH)
            same = marks_ref[here, M_SEG : M_SEG + 1] == seg_ref[0:1, here]
            value = mm_nt(left_exact(conv_ref[here, :]), right_exact(b_all[here, :], 1))
            scores[n] = jnp.where((r >= c) & same, value, 0.0)
        per = LANES // head_size
        for turned, values in ((cum_turned, cum_all), (step_turned, step_all)):
            rows_all = values[...].T
            for j in range(turned.shape[0]):
                turned[j, 0:per, :] = rows_all[per * j : per * (j + 1), :]

    @pl.when(i >= 2)
    def _():
        j = i - 2
        per = LANES // head_size
        row, lane = iota2((LANES, LANES))
        widen = (row == per * j + lane // head_size).astype(f32)
        cum = lax.dot_general(cum_all[...], widen, (((1,), (0,)), ((), ())), preferred_element_type=f32, precision=precise)
        rate = lax.dot_general(rate_all[...], widen, (((1,), (0,)), ((), ())), preferred_element_type=f32, precision=precise)
        cum_rows = cum_turned[j]
        cum_rows_ref[0] = cum_rows
        step_rows_ref[0] = step_turned[j]
        cum_ref[...] = cum
        rate_ref[...] = rate
        lane_c = lax.broadcasted_iota(jnp.int32, (CH, LANES), 1)
        states = []
        for n in range(chunks):
            here = pl.ds(n * CH, CH)
            span = slice(n * CH, (n + 1) * CH)
            scaled = rate[span] * conv_ref[here, :]
            out = jnp.zeros((CH, LANES), f32)
            for h in range(per):
                column = cum[span, h * head_size : h * head_size + 1]
                value = []
                for first, past in ((0, CH // 2), (CH // 2, CH)):
                    spread = column[first:past] - cum_rows[h : h + 1, n * CH : n * CH + past]
                    weights = scores[n, first:past, :past] * jnp.exp(jnp.minimum(spread, 0.0))
                    value.append(mm(left_exact(weights), right_exact(scaled[:past], 0)))
                value = jnp.concatenate(value, axis=0)
                out = value if per == 1 else jnp.where(lane_c // head_size == h, value, out)
            y_ref[here, :] = out
            leave = jnp.exp(cum[(n + 1) * CH - 1 : (n + 1) * CH, :] - cum[span]) * marks_ref[here, M_LEAVE : M_LEAVE + 1]
            state = mm(left_exact(b_turned[:, here]), right_exact(scaled * leave, 0))
            own_state_ref[n] = state
            states.append(state)
        total = states[0]
        for n in range(1, chunks):
            last = (n + 1) * CH - 1
            kept = jnp.exp(cum[last : last + 1, :]) * marks_ref[last : last + 1, M_ENTER : M_ENTER + 1]
            total = kept * total + states[n]
        last_state_ref[...] = total


def call(kernel, held, in_specs, **rest):
    count = len(held)

    def run(*refs):
        kernel(*refs[count:])

    made = pl.pallas_call(run, in_specs=[pl.BlockSpec(memory_space=pl.ANY)] * count + in_specs, **rest)
    return lambda *args: made(*held, *args)


def ordered(value, *others):
    anywhere = pl.BlockSpec(memory_space=pl.ANY)
    return pl.pallas_call(
        lambda *refs: None,
        in_specs=[anywhere] * (1 + len(others)),
        out_specs=anywhere,
        out_shape=jax.ShapeDtypeStruct(value.shape, value.dtype),
        input_output_aliases={0: 0},
        cost_estimate=cost(0),
        name="ordered",
    )(value, *others)


def whole(shape):
    return pl.BlockSpec(shape, lambda i: (0,) * len(shape))


def params(limit=VMEM_BYTES):
    return pltpu.CompilerParams(vmem_limit_bytes=limit, dimension_semantics=("arbitrary",))


def cost(microseconds):
    return pl.CostEstimate(flops=0, bytes_accessed=int(microseconds * 3e6), transcendentals=0)


def scan_forward(pre, halo, taps, marks, seg_row, step, bias, decay, head_size, held=()):
    rows, mixed = pre.shape
    inner = mixed - 2 * N
    pairs = inner // LANES
    chunks = rows // CH
    steps = pairs + 2
    column = lambda i: (0, (i + pairs) % steps)
    pair = lambda i: (0, jnp.maximum(i - 2, 0))
    return call(
        partial(scan_forward_kernel, head_size, rows),
        held,
        grid=(steps,),
        in_specs=[
            pl.BlockSpec((rows, LANES), column),
            pl.BlockSpec((HALO, LANES), column),
            pl.BlockSpec((8, LANES), column),
            whole((rows, LANES)),
            whole((8, rows)),
            whole((rows, LANES)),
            whole((1, LANES)),
            whole((1, LANES)),
        ],
        out_specs=[
            pl.BlockSpec((rows, LANES), column),
            pl.BlockSpec((rows, LANES), pair),
            pl.BlockSpec((chunks, N, LANES), lambda i: (0, 0, jnp.maximum(i - 2, 0))),
            pl.BlockSpec((N, LANES), pair),
            pl.BlockSpec((rows, LANES), pair),
            pl.BlockSpec((rows, LANES), pair),
            pl.BlockSpec((1, 8, rows), lambda i: (jnp.maximum(i - 2, 0), 0, 0)),
            pl.BlockSpec((1, 8, rows), lambda i: (jnp.maximum(i - 2, 0), 0, 0)),
        ],
        out_shape=[
            jax.ShapeDtypeStruct((rows, mixed), f32),
            jax.ShapeDtypeStruct((rows, inner), f32),
            jax.ShapeDtypeStruct((chunks, N, inner), f32),
            jax.ShapeDtypeStruct((N, inner), f32),
            jax.ShapeDtypeStruct((rows, inner), f32),
            jax.ShapeDtypeStruct((rows, inner), f32),
            jax.ShapeDtypeStruct((pairs, 8, rows), f32),
            jax.ShapeDtypeStruct((pairs, 8, rows), f32),
        ],
        scratch_shapes=[
            pltpu.VMEM((rows + HALO, LANES), f32),
            pltpu.VMEM((rows, LANES), f32),
            pltpu.VMEM((N, rows), f32),
            pltpu.VMEM((chunks, CH, CH), f32),
            pltpu.VMEM((rows, LANES), f32),
            pltpu.VMEM((rows, LANES), f32),
            pltpu.VMEM((rows, LANES), f32),
            pltpu.VMEM((pairs, 8, rows), f32),
            pltpu.VMEM((pairs, 8, rows), f32),
            pltpu.VMEM((KC - 1, rows, LANES), f32),
        ],
        compiler_params=params(),
        cost_estimate=cost(15),
        name="scan_forward",
    )(pre, halo, taps, marks, seg_row, step, bias, decay)


def gate_kernel(
    chunks, with_grad, y_ref, conv_ref, c_ref, cum_ref, marks_ref, own_state_ref, state_ref, gate_ref, skip_ref, gain_ref,
    *rest,
):
    if with_grad:
        grad_ref, ssm_ref, gated_ref, entering_ref, sums_ref, c_parts, squares, products = rest
    else:
        ssm_ref, gated_ref, entering_ref, sums_ref, c_parts, squares = rest
    i = pl.program_id(0)

    @pl.when(i == 0)
    def _():
        c_parts[...] = left_exact(c_ref[...])

    state = state_ref[...]
    for n in range(chunks):
        here = pl.ds(n * CH, CH)
        entering_ref[n] = state
        enter = jnp.exp(cum_ref[here, :]) * marks_ref[here, M_ENTER : M_ENTER + 1]
        ssm_ref[here, :] = (
            y_ref[here, :]
            + enter * mm(c_parts[here, :], right_exact(state, 0))
            + skip_ref[...] * conv_ref[here, :]
        )
        state = enter[CH - 1 : CH, :] * state + own_state_ref[n]
    gate = gate_ref[...]
    gated = ssm_ref[...] * (gate * sigmoid(gate))
    scaled = gated * gain_ref[...]
    gated_ref[...] = scaled
    totals = [(squares, gated * gated)] + ([(products, scaled * grad_ref[...])] if with_grad else [])

    @pl.when(i == 0)
    def _():
        for total, value in totals:
            total[...] = value

    @pl.when(i > 0)
    def _():
        for total, value in totals:
            total[...] += value

    @pl.when(i == pl.num_programs(0) - 1)
    def _():
        row = lax.broadcasted_iota(jnp.int32, (8, LANES), 0)
        sums = [rows_of((row == n).astype(bf16), total[...]) for n, (total, _) in enumerate(totals)]
        sums_ref[...] = sum(sums[1:], sums[0])


def gate_forward(y, conv, cum, marks, own_state, state_in, gate, skip, gain, grad=None, held=()):
    rows, inner = y.shape
    pairs = inner // LANES
    chunks = rows // CH
    block = pl.BlockSpec((rows, LANES), lambda i: (0, i))
    line = pl.BlockSpec((1, LANES), lambda i: (0, i))
    states = pl.BlockSpec((chunks, N, LANES), lambda i: (0, 0, i))
    last = conv.shape[1] // LANES - 1
    in_specs = [
        block, block, pl.BlockSpec((rows, LANES), lambda i: (0, last)), block, whole((rows, LANES)), states,
        pl.BlockSpec((N, LANES), lambda i: (0, i)), block, line, line,
    ]
    args = [y, conv, conv, cum, marks, own_state, state_in, gate, skip, gain]
    if grad is not None:
        in_specs.append(block)
        args.append(grad)
    return call(
        partial(gate_kernel, chunks, grad is not None),
        held,
        grid=(pairs,),
        in_specs=in_specs,
        out_specs=[block, block, states, whole((8, rows))],
        out_shape=[
            jax.ShapeDtypeStruct((rows, inner), f32),
            jax.ShapeDtypeStruct((rows, inner), f32),
            jax.ShapeDtypeStruct((chunks, N, inner), f32),
            jax.ShapeDtypeStruct((8, rows), f32),
        ],
        scratch_shapes=[pltpu.VMEM((rows, 6 * N), bf16)] + [pltpu.VMEM((rows, LANES), f32)] * (1 if grad is None else 2),
        compiler_params=params(),
        cost_estimate=cost(6),
        name="gate_forward",
    )(*args)


def gate_backward_kernel(
    chunks, channels, grad_ref, gate_ref, ssm_ref, conv_ref, c_ref, cum_ref, marks_ref, sums_ref, gain_ref,
    out_grad_ref, gate_grad_ref, pulled_ref, first_ref, gain_grad_ref, skip_grad_ref, dots_ref,
    scale_all, shift_all, c_turned, products,
):
    i = pl.program_id(0)

    @pl.when(i == 0)
    def _():
        scale = lax.rsqrt(sums_ref[0:1, :] / channels + epsilon)
        shift = scale * scale * scale * sums_ref[1:2, :] / channels
        rows = scale.shape[1]
        scale_all[...] = jnp.broadcast_to(scale, (LANES, rows)).T
        shift_all[...] = jnp.broadcast_to(shift, (LANES, rows)).T
        for n in range(chunks):
            c_turned[n] = left_parts(c_ref[pl.ds(n * CH, CH), :].T)

    gate = gate_ref[...]
    sig = sigmoid(gate)
    act = gate * sig
    ssm = ssm_ref[...]
    gated = ssm * act
    grad = grad_ref[...]
    scale = scale_all[...]
    gated_grad = scale * gain_ref[...] * grad - gated * shift_all[...]
    gain_grad_ref[...] = jnp.sum(grad * gated * scale, axis=0, keepdims=True)
    out_grad = gated_grad * act
    out_grad_ref[...] = out_grad
    skip_grad_ref[...] = jnp.sum(out_grad * conv_ref[...], axis=0, keepdims=True)
    gate_grad = gated_grad * ssm * (sig * (1.0 + gate * (1.0 - sig)))
    gate_grad_ref[...] = gate_grad.astype(bf16)
    dots = gate_grad * gate
    kept = []
    for n in range(chunks):
        here = pl.ds(n * CH, CH)
        enter = jnp.exp(cum_ref[here, :]) * marks_ref[here, M_ENTER : M_ENTER + 1]
        pulled = mm(c_turned[n], right_parts(out_grad_ref[here, :] * enter, 0))
        pulled_ref[n] = pulled
        kept.append((enter[CH - 1 : CH, :], pulled))
    first = kept[-1][1]
    for last_enter, pulled in kept[-2::-1]:
        first = last_enter * first + pulled
    first_ref[...] = first

    @pl.when(i == 0)
    def _():
        products[...] = dots

    @pl.when(i > 0)
    def _():
        products[...] += dots

    @pl.when(i == pl.num_programs(0) - 1)
    def _():
        row = lax.broadcasted_iota(jnp.int32, (8, LANES), 0)
        dots_ref[...] = rows_of((row == 0).astype(bf16), products[...])


def gate_backward(grad, gate, ssm, conv, cum, marks, sums, gain, channels, held=()):
    rows, inner = ssm.shape
    pairs = inner // LANES
    chunks = rows // CH
    block = pl.BlockSpec((rows, LANES), lambda i: (0, i))
    line = pl.BlockSpec((1, LANES), lambda i: (0, i))
    states = pl.BlockSpec((chunks, N, LANES), lambda i: (0, 0, i))
    last = conv.shape[1] // LANES - 1
    return call(
        partial(gate_backward_kernel, chunks, float(channels)),
        held,
        grid=(pairs,),
        in_specs=[
            block, block, block, block, pl.BlockSpec((rows, LANES), lambda i: (0, last)), block,
            whole((rows, LANES)), whole((8, rows)), line,
        ],
        out_specs=[block, block, states, pl.BlockSpec((N, LANES), lambda i: (0, i)), line, line, whole((8, rows))],
        out_shape=[
            jax.ShapeDtypeStruct((rows, inner), f32),
            jax.ShapeDtypeStruct((rows, inner), bf16),
            jax.ShapeDtypeStruct((chunks, N, inner), f32),
            jax.ShapeDtypeStruct((N, inner), f32),
            jax.ShapeDtypeStruct((1, inner), f32),
            jax.ShapeDtypeStruct((1, inner), f32),
            jax.ShapeDtypeStruct((8, rows), f32),
        ],
        scratch_shapes=[
            pltpu.VMEM((rows, LANES), f32), pltpu.VMEM((rows, LANES), f32), pltpu.VMEM((chunks, N, 3 * CH), bf16),
            pltpu.VMEM((rows, LANES), f32),
        ],
        compiler_params=params(),
        cost_estimate=cost(7),
        name="gate_backward",
    )(grad, gate, ssm, conv, conv, cum, marks, sums, gain)


def intra_backward_kernel(
    head_size, chunks, out_grad_ref, conv_ref, b_ref, c_ref, cum_ref, rate_ref, cum_rows_ref, marks_ref, seg_ref,
    scaled_grad_ref, rate_rows_ref, b_grad_ref, c_grad_ref,
    scores, scores_grad,
):
    i = pl.program_id(0)
    per = LANES // head_size
    r, c = iota2((CH, CH))

    @pl.when(i == 0)
    def _():
        for n in range(chunks):
            here = pl.ds(n * CH, CH)
            same = marks_ref[here, M_SEG : M_SEG + 1] == seg_ref[0:1, here]
            value = precise_nt(b_ref[here, :], c_ref[here, :])
            scores[n] = jnp.where((r <= c) & same, value, 0.0)
            scores_grad[n] = jnp.zeros((CH, CH), f32)

    from_row = (r >= c).astype(bf16)
    from_row = jnp.concatenate([from_row, from_row], axis=0)
    lane_c = lax.broadcasted_iota(jnp.int32, (CH, LANES), 1)
    rate_rows_ref[...] = jnp.zeros(rate_rows_ref.shape, f32)
    for n in range(chunks):
        here = pl.ds(n * CH, CH)
        scaled = rate_ref[here, :] * conv_ref[here, :]
        grad_parts = right_parts(out_grad_ref[here, :], 1)
        grad_low = grad_parts[:, :LANES]
        out = jnp.zeros((CH, LANES), f32)
        for h in range(per):
            mine = lane_c // head_size == h
            spread = cum_rows_ref[0, h : h + 1, here] - cum_ref[here, h * head_size : h * head_size + 1]
            decay = jnp.exp(jnp.minimum(spread, 0.0))
            weights = scores[n] * decay
            value = mm(weights.astype(bf16), grad_low)
            out = jnp.where(mine, value, out)
            weights_grad = mm_nt(left_parts(jnp.where(mine, scaled, 0.0)), grad_parts)
            scores_grad[n] += decay * weights_grad
            flow = mm(jnp.concatenate(split(weights * weights_grad), axis=1), from_row)
            rate_rows_ref[0, h : h + 1, here] = jnp.sum(jnp.where(r < c, flow, 0.0), axis=0, keepdims=True)
        scaled_grad_ref[here, :] = out

    @pl.when(i == pl.num_programs(0) - 1)
    def _():
        for n in range(chunks):
            here = pl.ds(n * CH, CH)
            same = marks_ref[here, M_SEG : M_SEG + 1] == seg_ref[0:1, here]
            total = jnp.where((r <= c) & same, scores_grad[n], 0.0)
            b_grad_ref[here, :] = precise_mm(total, c_ref[here, :])
            c_grad_ref[here, :] = precise_mm(total.T, b_ref[here, :])


def intra_backward(out_grad, conv, cum, rate, cum_rows, marks, seg_row, head_size, held=()):
    rows, inner = out_grad.shape
    pairs = inner // LANES
    chunks = rows // CH
    block = pl.BlockSpec((rows, LANES), lambda i: (0, i))
    heads = pl.BlockSpec((1, 8, rows), lambda i: (i, 0, 0))
    return call(
        partial(intra_backward_kernel, head_size, chunks),
        held,
        grid=(pairs,),
        in_specs=[
            block, block, pl.BlockSpec((rows, LANES), lambda i: (0, pairs)),
            pl.BlockSpec((rows, LANES), lambda i: (0, pairs + 1)), block, block, heads,
            whole((rows, LANES)), whole((8, rows)),
        ],
        out_specs=[block, heads, whole((rows, N)), whole((rows, N))],
        out_shape=[
            jax.ShapeDtypeStruct((rows, inner), f32),
            jax.ShapeDtypeStruct((pairs, 8, rows), f32),
            jax.ShapeDtypeStruct((rows, N), f32),
            jax.ShapeDtypeStruct((rows, N), f32),
        ],
        scratch_shapes=[pltpu.VMEM((chunks, CH, CH), f32), pltpu.VMEM((chunks, CH, CH), f32)],
        compiler_params=params(),
        cost_estimate=cost(3),
        name="intra_backward",
    )(out_grad, conv, conv, conv, cum, rate, cum_rows, marks, seg_row)


def scan_backward_kernel(
    head_size, rows, pairs, out_grad_ref, scaled_grad_ref, conv_ref, b_ref, c_ref, cum_ref, rate_ref, rate_rows_ref, step_rows_ref,
    entering_ref, pulled_ref, after_ref, skip_ref, decay_ref, b_intra_ref, c_intra_ref, pre_ref, halo_ref, taps_ref, marks_ref,
    conv_grad_ref, taps_grad_ref, step_grad_ref, log_grad_ref, bias_grad_ref,
    padded, b_total, c_total, current, head_sums, wide_marks,
):
    i = pl.program_id(0)
    chunks = rows // CH
    fill_padded(padded, halo_ref, pre_ref, rows)

    per = LANES // head_size

    @pl.when(i == 0)
    def _():
        b_total[...] = b_intra_ref[...]
        c_total[...] = c_intra_ref[...]
        head_sums[...] = jnp.zeros(head_sums.shape, f32)
        spread_marks(wide_marks, marks_ref, M_FWD)

    @pl.when(i < pairs)
    def _():
        after = after_ref[...]
        row, lane = iota2((6 * LANES, LANES))
        quantity = (row // LANES) % 3
        selector = (lane == 8 * i + per * quantity + (row % LANES) // head_size).astype(bf16)
        last_row = lax.broadcasted_iota(jnp.int32, (CH, LANES), 0) == CH - 1
        for n in reversed(range(chunks)):
            here = pl.ds(n * CH, CH)
            last = (n + 1) * CH - 1
            mark_enter = marks_ref[here, M_ENTER : M_ENTER + 1]
            mark_leave = marks_ref[here, M_LEAVE : M_LEAVE + 1]
            cum = cum_ref[here, :]
            enter = jnp.exp(cum) * mark_enter
            leave = jnp.exp(cum_ref[last : last + 1, :] - cum) * mark_leave
            conv = conv_ref[here, :]
            rate = rate_ref[here, :]
            scaled = rate * conv
            out_grad = out_grad_ref[here, :]
            state = entering_ref[n]
            left = leave * precise_mm(b_ref[here, :], after)
            scaled_grad = scaled_grad_ref[here, :] + left
            b_total[here, :] += precise_nt(scaled * leave, after)
            entered = out_grad * enter
            c_total[here, :] += precise_nt(entered, state)
            kept = enter[CH - 1 : CH, :]
            through = jnp.sum(kept * (state * after), axis=0, keepdims=True)
            came = entered * precise_mm(c_ref[here, :], state) + jnp.where(last_row, through, 0.0)
            parts = [split(value) for value in (came, scaled * left, conv * scaled_grad)]
            stacked = jnp.concatenate([high for high, _ in parts] + [low for _, low in parts], axis=1)
            head_sums[here, :] += mm(stacked, selector)
            current[here, :] = rate * scaled_grad + skip_ref[...] * out_grad
            after = kept * after + pulled_ref[n]

    @pl.when(i == pairs)
    def _():
        current[...] = b_total[...]
        r, c = iota2((CH, CH))
        from_row = (r >= c).astype(bf16)
        before = (r < c).astype(bf16)
        totals = [(jnp.zeros((per, 1), f32), jnp.zeros((per, 1), f32)) for _ in range(pairs)]
        for n in range(chunks):
            here = pl.ds(n * CH, CH)
            turned = head_sums[here, :].T
            came, gone = times_mask(turned, from_row), times_mask(turned, before)
            for j in range(pairs):
                first = 8 * j
                log_rate_grad = (
                    rate_rows_ref[j, 0:per, here] + came[first : first + per] + gone[first + per : first + 2 * per]
                )
                direct = turned[first + 2 * per : first + 3 * per]
                shifted = step_rows_ref[j, 0:per, here]
                decay = decay_ref[j, 0:per, 0:1]
                step_grad = (direct + log_rate_grad * decay) * sigmoid(shifted)
                step_grad_ref[j, 0:per, here] = step_grad
                log_total, bias_total = totals[j]
                totals[j] = (
                    log_total + jnp.sum(log_rate_grad * softplus(shifted), axis=1, keepdims=True) * decay,
                    bias_total + jnp.sum(step_grad, axis=1, keepdims=True),
                )
        for j, (log_total, bias_total) in enumerate(totals):
            log_grad_ref[j, 0:per, :] = jnp.broadcast_to(log_total, (per, LANES))
            bias_grad_ref[j, 0:per, :] = jnp.broadcast_to(bias_total, (per, LANES))

    @pl.when(i == pairs + 1)
    def _():
        current[...] = c_total[...]

    sums = [jnp.zeros((1, LANES), f32) for _ in range(KC + 1)]
    for start in range(0, rows, TILE):
        value = conv_tile(padded, taps_ref, wide_marks, start, TILE)
        sig = sigmoid(value)
        grad = current[pl.ds(start, TILE), :] * (sig * (1.0 + value * (1.0 - sig)))
        conv_grad_ref[pl.ds(start, TILE), :] = grad
        for k in range(KC):
            shifted = padded[pl.ds(start + HALO - KC + 1 + k, TILE), :]
            if k < KC - 1:
                shifted = shifted * wide_marks[k, pl.ds(start, TILE), :]
            sums[k] = sums[k] + jnp.sum(grad * shifted, axis=0, keepdims=True)
        sums[KC] = sums[KC] + jnp.sum(grad, axis=0, keepdims=True)
    taps_grad_ref[...] = jnp.concatenate(sums + [jnp.zeros((8 - KC - 1, LANES), f32)], axis=0)


def scan_backward(
    out_grad, scaled_grad, conv, cum, rate, rate_rows, step_rows, entering, pulled, after, skip, decay_rows,
    b_intra, c_intra, pre, halo, taps, marks, head_size, held=(),
):
    rows, inner = out_grad.shape
    mixed = pre.shape[1]
    pairs = inner // LANES
    chunks = rows // CH
    steps = pairs + 2
    own = lambda i: jnp.minimum(i, pairs - 1)
    block = pl.BlockSpec((rows, LANES), lambda i: (0, own(i)))
    column = lambda i: (0, i)
    heads, few = whole((pairs, 8, rows)), whole((pairs, 8, LANES))
    states = pl.BlockSpec((chunks, N, LANES), lambda i: (0, 0, own(i)))
    return call(
        partial(scan_backward_kernel, head_size, rows, pairs),
        held,
        grid=(steps,),
        in_specs=[
            block, block, block, pl.BlockSpec((rows, LANES), lambda i: (0, pairs)),
            pl.BlockSpec((rows, LANES), lambda i: (0, pairs + 1)), block, block, heads, heads, states, states,
            pl.BlockSpec((N, LANES), lambda i: (0, own(i))), pl.BlockSpec((1, LANES), lambda i: (0, own(i))), few,
            whole((rows, N)), whole((rows, N)), pl.BlockSpec((rows, LANES), column), pl.BlockSpec((HALO, LANES), column),
            pl.BlockSpec((8, LANES), column), whole((rows, LANES)),
        ],
        out_specs=[pl.BlockSpec((rows, LANES), column), pl.BlockSpec((8, LANES), column), heads, few, few],
        out_shape=[
            jax.ShapeDtypeStruct((rows, mixed), f32),
            jax.ShapeDtypeStruct((8, mixed), f32),
            jax.ShapeDtypeStruct((pairs, 8, rows), f32),
            jax.ShapeDtypeStruct((pairs, 8, LANES), f32),
            jax.ShapeDtypeStruct((pairs, 8, LANES), f32),
        ],
        scratch_shapes=[
            pltpu.VMEM((rows + HALO, LANES), f32),
            pltpu.VMEM((rows, N), f32),
            pltpu.VMEM((rows, N), f32),
            pltpu.VMEM((rows, LANES), f32),
            pltpu.VMEM((rows, LANES), f32),
            pltpu.VMEM((KC - 1, rows, LANES), f32),
        ],
        compiler_params=params(),
        cost_estimate=cost(3),
        name="scan_backward",
    )(
        out_grad, scaled_grad, conv, conv, conv, cum, rate, rate_rows, step_rows, entering, pulled, after, skip, decay_rows,
        b_intra, c_intra, pre, halo, taps, marks,
    )


def conv_backward_kernel(
    rows, pairs, per, conv_grad_ref, next_ref, taps_ref, marks_ref, pre_ref, gate_dots_ref, step_grad_ref, step_rows_ref,
    bias_ref, out_ref, map_grad_ref, dots_ref, padded, products, wide_marks,
):
    i = pl.program_id(0)
    row = lax.broadcasted_iota(jnp.int32, (8, LANES), 0)

    @pl.when(i == 0)
    def _():
        dots_ref[...] = gate_dots_ref[...]
        products[...] = jnp.zeros(products.shape, f32)
        spread_marks(wide_marks, marks_ref, M_BWD)

    @pl.when(i > 0)
    def _():
        padded[pl.ds(0, rows), :] = conv_grad_ref[...]
        padded[pl.ds(rows, 8), :] = next_ref[...]
        for start in range(0, rows, TILE):
            total = taps_ref[KC - 1 : KC, :] * padded[pl.ds(start, TILE), :]
            for k in range(KC - 1):
                shifted = padded[pl.ds(start + KC - 1 - k, TILE), :]
                total = total + taps_ref[k : k + 1, :] * (
                    shifted * wide_marks[k, pl.ds(start, TILE), :]
                )
            out_ref[pl.ds(start, TILE), :] = total.astype(bf16)
            map_grad_ref[pl.ds(start, TILE), :] = total
            products[pl.ds(start, TILE), :] += total * pre_ref[pl.ds(start, TILE), :].astype(f32)

    @pl.when(i == 0)
    def _():
        grads = [step_grad_ref[j, 0:per, :] for j in range(pairs)]
        grads = jnp.concatenate(grads + [jnp.zeros((LANES - per * pairs, rows), f32)], axis=0)
        out_ref[...] = grads.T.astype(bf16)
        total = jnp.zeros((1, rows), f32)
        for j in range(pairs):
            total = total + jnp.sum(
                step_grad_ref[j, 0:per, :] * (step_rows_ref[j, 0:per, :] - bias_ref[j, 0:per, 0:1]), axis=0, keepdims=True
            )
        dots_ref[0:1, :] += total

    @pl.when(i == pl.num_programs(0) - 1)
    def _():
        dots_ref[...] += rows_of((row == 0).astype(bf16), products[...])


def conv_backward(conv_grad, next_grad, taps, marks, pre, gate_dots, step_grad, step_rows, bias_rows, head_size, held=()):
    rows, mixed = pre.shape
    pairs = (mixed - 2 * N) // LANES
    steps = pairs + 3
    column = lambda i: (0, jnp.clip(i - 1, 0, pairs + 1))
    return call(
        partial(conv_backward_kernel, rows, pairs, LANES // head_size),
        held,
        grid=(steps,),
        in_specs=[
            pl.BlockSpec((rows, LANES), column), pl.BlockSpec((8, LANES), column), pl.BlockSpec((8, LANES), column),
            whole((rows, LANES)), pl.BlockSpec((rows, LANES), column),
            whole((8, rows)),
            whole((pairs, 8, rows)), whole((pairs, 8, rows)), whole((pairs, 8, LANES)),
        ],
        out_specs=[
            pl.BlockSpec((rows, LANES), lambda i: (0, i)),
            pl.BlockSpec((rows, LANES), lambda i: (0, jnp.clip(i - pairs - 1, 0, 1))),
            whole((8, rows)),
        ],
        out_shape=[
            jax.ShapeDtypeStruct((rows, steps * LANES), bf16),
            jax.ShapeDtypeStruct((rows, 2 * N), f32),
            jax.ShapeDtypeStruct((8, rows), f32),
        ],
        scratch_shapes=[
            pltpu.VMEM((rows + 8, LANES), f32), pltpu.VMEM((rows, LANES), f32), pltpu.VMEM((KC - 1, rows, LANES), f32),
        ],
        compiler_params=params(),
        cost_estimate=cost(6),
        name="conv_backward",
    )(conv_grad, next_grad, taps, marks, pre, gate_dots, step_grad, step_rows, bias_rows)


def join_kernel(count, width, index_ref, *refs):
    blocks, out_ref = refs[:count], refs[count]
    for n in range(count):
        start = pl.multiple_of((index_ref[0] ^ n) * width, LANES)
        out_ref[:, pl.ds(start, width)] = blocks[n][...].astype(out_ref.dtype)


def join(blocks, index, dtype, first_row, held=()):
    count = len(blocks)
    rows, width = blocks[0].shape
    rows -= first_row
    size = min(rows, 256)
    return call(
        partial(join_kernel, count, width),
        held,
        grid=(rows // size,),
        in_specs=[pl.BlockSpec(memory_space=pltpu.SMEM)]
        + [pl.BlockSpec((size, width), lambda i: (i + first_row // size, 0))] * count,
        out_specs=pl.BlockSpec((size, count * width), lambda i: (i, 0)),
        out_shape=jax.ShapeDtypeStruct((rows, count * width), dtype),
        compiler_params=params(),
        cost_estimate=cost(2),
        name="join",
    )(index, *blocks)


def join_norm_kernel(count, width, index_ref, gain_ref, *refs):
    blocks, normed_ref, scale_ref = refs[:count], refs[count], refs[count + 1]
    total = jnp.zeros((blocks[0].shape[0], 1), f32)
    for n in range(count):
        value = blocks[n][...].astype(f32)
        total = total + jnp.sum(value * value, axis=1, keepdims=True)
    scale = lax.rsqrt(total / (count * width) + epsilon)
    scale_ref[...] = jnp.broadcast_to(scale, scale_ref.shape)
    for n in range(count):
        here = pl.ds(pl.multiple_of((index_ref[0] ^ n) * width, LANES), width)
        normed_ref[:, here] = (blocks[n][...].astype(f32) * scale * gain_ref[:, here]).astype(bf16)


def join_norm(blocks, index, gain, rows, held=()):
    count = len(blocks)
    width = blocks[0].shape[1]
    size = 128
    block = pl.BlockSpec((size, width), lambda i: (i, 0))
    return call(
        partial(join_norm_kernel, count, width),
        held,
        grid=(rows // size,),
        in_specs=[pl.BlockSpec(memory_space=pltpu.SMEM), whole((1, count * width))] + [block] * count,
        out_specs=[
            pl.BlockSpec((size, count * width), lambda i: (i, 0)),
            pl.BlockSpec((size, LANES), lambda i: (i, 0)),
        ],
        out_shape=[
            jax.ShapeDtypeStruct((rows, count * width), bf16),
            jax.ShapeDtypeStruct((rows, LANES), f32),
        ],
        compiler_params=params(),
        cost_estimate=cost(3),
        name="join_norm",
    )(index, gain, *blocks)


def input_side_kernel(count, width, own_ref, dots_ref, block_ref, grad_ref, scale_ref, gain_ref, *refs):
    sent, out_ref, norm_ref = refs[: count - 1], refs[count - 1], refs[count]
    normed_grad = own_ref[...]
    for piece in sent:
        normed_grad = normed_grad + piece[...].astype(f32)
    scale = scale_ref[:, 0:1]
    rows = scale.shape[0]
    mean = jnp.broadcast_to(dots_ref[0:1, :] / width, (LANES, rows)).T[:, 0:1]
    normed_x = block_ref[...].astype(f32) * scale
    grad = grad_ref[...].astype(f32) + scale * (gain_ref[...] * normed_grad - normed_x * mean)
    out_ref[...] = grad.astype(bf16)
    norm = jnp.sum(normed_grad * normed_x, axis=0, keepdims=True)

    @pl.when(pl.program_id(0) == 0)
    def _():
        norm_ref[...] = norm

    @pl.when(pl.program_id(0) > 0)
    def _():
        norm_ref[...] += norm


def input_gradient(own, sent, dots, block, grad, scale, gain, width, held=()):
    rows, cols = own.shape
    size = 128
    part = pl.BlockSpec((size, cols), lambda i: (i, 0))
    return call(
        partial(input_side_kernel, len(sent) + 1, float(width)),
        held,
        grid=(rows // size,),
        in_specs=[
            part, pl.BlockSpec((8, size), lambda i: (0, i)), part, part, pl.BlockSpec((size, LANES), lambda i: (i, 0)),
            whole((1, cols)),
        ]
        + [part] * len(sent),
        out_specs=[part, whole((1, cols))],
        out_shape=[jax.ShapeDtypeStruct((rows, cols), bf16), jax.ShapeDtypeStruct((1, cols), f32)],
        compiler_params=params(),
        cost_estimate=cost(3),
        name="input_gradient",
    )(own, dots, block, grad, scale, gain, *sent)


def join_micro_kernel(count, width, held, places_ref, *refs):
    out_ref, refs = refs[-1], refs[held:]
    for n in range(count):
        start = pl.multiple_of((places_ref[0] ^ n) * width, LANES)
        out_ref[:, pl.ds(start, width)] = refs[n][...].astype(out_ref.dtype)


def join_micro(places, blocks, dtype, held=()):
    count = len(blocks)
    rows, width = blocks[0].shape
    size = rows // 4
    return pl.pallas_call(
        partial(join_micro_kernel, count, width, len(held)),
        grid_spec=pltpu.PrefetchScalarGridSpec(
            num_scalar_prefetch=1,
            grid=(4,),
            in_specs=[pl.BlockSpec(memory_space=pl.ANY)] * len(held)
            + [pl.BlockSpec((size, width), lambda i, places: (i, 0))] * count,
            out_specs=pl.BlockSpec((size, count * width), lambda i, places: (places[1] ^ i, 0)),
        ),
        out_shape=jax.ShapeDtypeStruct((rows, count * width), dtype),
        compiler_params=params(),
        cost_estimate=cost(5),
        name="join_micro",
    )(places, *held, *blocks)


def join_gathered_kernel(count, width, held, places_ref, *refs):
    out_ref, blocks_ref = refs[-1], refs[held]
    for n in range(count):
        out_ref[:, n * width : (n + 1) * width] = blocks_ref[n].astype(out_ref.dtype)


def join_gathered(places, blocks, dtype, held=()):
    count, rows, width = blocks.shape
    size = rows // 4
    return pl.pallas_call(
        partial(join_gathered_kernel, count, width, len(held)),
        grid_spec=pltpu.PrefetchScalarGridSpec(
            num_scalar_prefetch=1,
            grid=(4,),
            in_specs=[pl.BlockSpec(memory_space=pl.ANY)] * len(held)
            + [pl.BlockSpec((count, size, width), lambda i, places: (0, i, 0))],
            out_specs=pl.BlockSpec((size, count * width), lambda i, places: (places[1] ^ i, 0)),
        ),
        out_shape=jax.ShapeDtypeStruct((rows, count * width), dtype),
        compiler_params=params(),
        cost_estimate=cost(5),
        name="join_gathered",
    )(places, *held, blocks)


def place_maps_kernel(count, places_ref, term_ref, normed_ref, *refs):
    pieces, out_ref = refs[:count], refs[count]
    rows = pieces[0].shape[0]
    total = jnp.zeros(out_ref.shape, f32)
    for n in range(count):
        here = pl.ds(pl.multiple_of((places_ref[0] ^ n) * rows, 16), rows)
        total = total + mm_tn(normed_ref[here, :], pieces[n][...])
    out_ref[...] = total.astype(bf16)


def place_maps(index, term, normed, pieces, first_column):
    count = len(pieces)
    rows, width = pieces[0].shape
    depth = normed.shape[1]
    return pl.pallas_call(
        partial(place_maps_kernel, count),
        grid=(width // LANES,),
        in_specs=[pl.BlockSpec(memory_space=pltpu.SMEM), pl.BlockSpec(memory_space=pl.ANY), whole(normed.shape)]
        + [pl.BlockSpec((rows, LANES), lambda i: (0, i))] * count,
        out_specs=pl.BlockSpec((depth, LANES), lambda i: (0, i + first_column // LANES)),
        out_shape=jax.ShapeDtypeStruct(term.shape, term.dtype),
        input_output_aliases={1: 0},
        compiler_params=params(),
        cost_estimate=cost(3),
        name="place_maps",
    )(index, term, normed, *pieces)


def from_behind(block, axis, distance):
    devices = range(lax.axis_size(axis))
    route = [(i - distance, i) for i in devices if i - distance in devices]
    return lax.ppermute(block, axis, route)


def prefix(value, axis, join, neutral, backward):
    count, mine = (lax.axis_size(axis), lax.axis_index(axis))
    pieces = jax.tree.map(lambda part: lax.all_gather(part, axis), value)
    if backward:
        pieces = jax.tree.map(lambda part: part[::-1], pieces)
        mine = count - 1 - mine
    total = jax.tree.map(
        lambda part, zero: jnp.full_like(part, 0) + jnp.asarray(zero, part.dtype), value, neutral
    )

    def hop(position, total):
        longer = join(total, jax.tree.map(lambda part: part[position], pieces))
        return jax.tree.map(lambda new, old: jnp.where(position < mine, new, old), longer, total)

    return lax.fori_loop(0, count - 1, hop, total)


def block_step(decay_rate, carried, inputs):
    state_now, seg_before = carried
    x_block, rate_block, b_block, c_block, seg_block = inputs
    cumulative = jnp.cumsum(rate_block * decay_rate[None, :], axis=0)
    width_block = seg_block.shape[0]
    row_index = lax.broadcasted_iota(jnp.int32, (width_block, width_block), 0)
    col_index = lax.broadcasted_iota(jnp.int32, (width_block, width_block), 1)
    within = (row_index >= col_index) & (seg_block[:, None] == seg_block[None, :])
    within_heads = within[:, :, None]
    spread = cumulative[:, None, :] - cumulative[None, :, :]
    decay = jnp.where(within_heads, jnp.exp(jnp.where(within_heads, spread, 0.0)), 0.0)
    scores = jnp.dot(c_block, b_block.T, precision=precise)
    weights = scores[:, :, None] * decay * rate_block[None, :, :]
    output = jnp.einsum("tsh,shp->thp", weights, x_block, precision=precise)
    entering = jnp.exp(cumulative) * (seg_block == seg_before)[:, None].astype(jnp.float32)
    output = output + entering[:, :, None] * jnp.einsum(
        "tn,hpn->thp", c_block, state_now, precision=precise
    )
    leaving = (
        jnp.exp(cumulative[-1][None, :] - cumulative)
        * (seg_block == seg_block[-1])[:, None].astype(jnp.float32)
        * rate_block
    )
    state_next = entering[-1][:, None, None] * state_now + jnp.einsum(
        "sh,shp,sn->hpn", leaving, x_block, b_block, precision=precise
    )
    return ((state_next, seg_block[-1]), output)


def scan_blocks(x_heads, step_rate, b_part, c_part, seg_own, decay_rate, state_start, seg_start):
    blocks = x_heads.shape[0] // CH

    def to_blocks(value):
        return value.reshape((blocks, CH) + value.shape[1:])

    stepper = jax.checkpoint(partial(block_step, decay_rate))
    final_carry, output = lax.scan(
        stepper,
        (state_start, seg_start),
        (
            to_blocks(x_heads),
            to_blocks(step_rate),
            to_blocks(b_part),
            to_blocks(c_part),
            to_blocks(seg_own),
        ),
    )
    return (output.reshape(x_heads.shape), final_carry[0])


def causal_conv(padded_in, kernel, offset, seg_padded):
    own_rows = padded_in.shape[0] - (KC - 1)
    current = seg_padded[KC - 1 :]
    summed = jnp.zeros((own_rows, padded_in.shape[1]), jnp.float32) + offset[None, :]
    for tap_index in range(KC):
        shifted = padded_in[tap_index : tap_index + own_rows]
        same_doc = (seg_padded[tap_index : tap_index + own_rows] == current).astype(jnp.float32)
        summed = summed + kernel[tap_index][None, :] * shifted * same_doc[:, None]
    return summed


def chain_combine(earlier, later):
    return (earlier[0] * later[0], earlier[1] * later[0][:, None, None] + later[1])


def project_in(layer_in, gain_row, zx_full, bc_full, dt_full):
    inputs_f = layer_in.astype(jnp.float32)
    in_scale = lax.rsqrt(jnp.mean(inputs_f * inputs_f, axis=1) + epsilon)
    normed = (inputs_f * in_scale[:, None] * gain_row[None, :]).astype(jnp.bfloat16)
    model_width = zx_full.shape[0]
    inner_local = zx_full.shape[2]
    joined = jnp.dot(
        normed, zx_full.reshape(model_width, 2 * inner_local), preferred_element_type=jnp.float32
    )
    bc_pre = jnp.dot(normed, bc_full, preferred_element_type=jnp.float32)
    mixed_pre = jnp.concatenate([joined[:, inner_local:], bc_pre], axis=1).astype(jnp.bfloat16)
    step_pre = jnp.dot(normed, dt_full, preferred_element_type=jnp.float32)
    return (inputs_f, in_scale, normed, joined[:, :inner_local], mixed_pre, step_pre)


def mixer_parts(padded_in, step_pre, kernel, offset, bias_row, log_rate, seg_padded, heads_local):
    own_rows = step_pre.shape[0]
    inner_local = padded_in.shape[1] - 2 * N
    head_size = inner_local // heads_local
    conv_out = jax.nn.silu(causal_conv(padded_in, kernel, offset, seg_padded))
    x_heads = conv_out[:, :inner_local].reshape(own_rows, heads_local, head_size)
    b_part = conv_out[:, inner_local : inner_local + N]
    c_part = conv_out[:, inner_local + N :]
    step_rate = jax.nn.softplus(step_pre + bias_row[None, :])
    decay_rate = -jnp.exp(log_rate)
    seg_own = seg_padded[KC - 1 :]
    seg_start = seg_padded[KC - 2]
    local_out, local_state = scan_blocks(
        x_heads,
        step_rate,
        b_part,
        c_part,
        seg_own,
        decay_rate,
        jnp.zeros((heads_local, head_size, N), jnp.float32),
        seg_start,
    )
    carried = jnp.exp(jnp.cumsum(step_rate * decay_rate[None, :], axis=0)) * (seg_own == seg_start)[
        :, None
    ].astype(jnp.float32)
    return (x_heads, c_part, local_out, local_state, carried)


def mixer_tail(parts, state_in, gate_pre, skip_row):
    x_heads, c_part, local_out, local_state, carried = parts
    own_rows = gate_pre.shape[0]
    ssm_out = (
        local_out
        + carried[:, :, None] * jnp.einsum("tn,hpn->thp", c_part, state_in, precision=precise)
        + skip_row[None, :, None] * x_heads
    )
    gate_act = jax.nn.silu(gate_pre)
    gated = ssm_out.reshape(own_rows, gate_pre.shape[1]) * gate_act
    state_out = carried[-1][:, None, None] * state_in + local_state
    return ((gated, state_out), (carried, c_part, gate_act))


def select_batch(array_in, chosen):
    return lax.dynamic_index_in_dim(array_in, chosen, 0, keepdims=False)


def store_batch(buffer, value, chosen, valid):
    return jnp.where(valid, lax.dynamic_update_index_in_dim(buffer, value, chosen, 0), buffer)


def body(
    tokens,
    cotangent,
    seg_ids,
    norm_gain,
    in_zx,
    in_bc,
    in_dt,
    conv_x,
    conv_xb,
    conv_bc,
    conv_bcb,
    dt_bias,
    a_log,
    skip_gain,
    gate_gain,
    out_w,
):
    section_index = lax.axis_index("section")
    ctx_index = lax.axis_index("ctx")
    tensor_index = lax.axis_index("tensor")
    section_count = lax.axis_size("section")
    tensor_count = lax.axis_size("tensor")
    batches = tokens.shape[0]
    token_rows = tokens.shape[1]
    model_width = tokens.shape[2]
    zx_full, bc_full, dt_full, out_full = (
        lax.all_gather(in_zx[0], "ctx", axis=0, tiled=True),
        lax.all_gather(in_bc[0], "ctx", axis=0, tiled=True),
        lax.all_gather(in_dt[0], "ctx", axis=0, tiled=True),
        lax.all_gather(out_w[0], "ctx", axis=1, tiled=True),
    )
    inner_local = zx_full.shape[2]
    heads_local = dt_full.shape[1]
    head_size = inner_local // heads_local
    mixed_width = inner_local + 2 * N
    gain_row = norm_gain[0].astype(jnp.float32)
    kernel = jnp.concatenate([conv_x[0], conv_bc[0]], axis=1).astype(jnp.float32)
    offset = jnp.concatenate([conv_xb[0], conv_bcb[0]]).astype(jnp.float32)
    bias_row = dt_bias[0]
    log_rate = a_log[0]
    skip_row = skip_gain[0]
    gate_row = gate_gain[0].astype(jnp.float32)
    seg_lead = jnp.full((batches, KC - 1), -1, jnp.int32)
    seg_all = jnp.concatenate([seg_lead, seg_ids], axis=1)
    seg_local = lax.dynamic_slice_in_dim(seg_all, ctx_index * token_rows, token_rows + KC - 1, 1)
    chain_start = (
        jnp.ones((heads_local,), jnp.float32),
        jnp.zeros((heads_local, head_size, N), jnp.float32),
    )
    kept_inputs = jnp.zeros((batches, token_rows, model_width), jnp.bfloat16)
    kept_states = jnp.zeros((batches, heads_local, head_size, N), jnp.float32)
    kept_scales = jnp.zeros((batches, token_rows), jnp.float32)
    kept_edges = jnp.zeros((batches, KC - 1, mixed_width), jnp.bfloat16)
    section_store = jnp.zeros((batches, token_rows, model_width), jnp.bfloat16)
    received = jnp.zeros((token_rows, model_width), jnp.bfloat16)
    for tick_number in range(batches + section_count - 1):
        batch_index = tick_number - section_index
        valid = (batch_index >= 0) & (batch_index < batches)
        chosen = jnp.clip(batch_index, 0, batches - 1)
        layer_in = jnp.where(section_index == 0, select_batch(tokens, chosen), received)
        seg_padded = select_batch(seg_local, chosen)
        inputs_f, in_scale, normed, gate_pre, mixed_pre, step_pre = project_in(
            layer_in, gain_row, zx_full, bc_full, dt_full
        )
        edge_rows = from_behind(mixed_pre[token_rows - (KC - 1) :], "ctx", 1)
        padded_in = jnp.concatenate([edge_rows, mixed_pre], axis=0).astype(jnp.float32)
        parts = mixer_parts(
            padded_in, step_pre, kernel, offset, bias_row, log_rate, seg_padded, heads_local
        )
        state_in = prefix((parts[4][-1], parts[3]), "ctx", chain_combine, chain_start, False)[1]
        gated = mixer_tail(parts, state_in, gate_pre, skip_row)[0][0]
        squares = lax.psum(jnp.sum(gated * gated, axis=1), "tensor")
        gate_scale = lax.rsqrt(squares / DI + epsilon)
        gate_normed = (gated * gate_scale[:, None] * gate_row[None, :]).astype(jnp.bfloat16)
        projected = lax.psum(
            jnp.dot(gate_normed, out_full, preferred_element_type=jnp.float32), "tensor"
        )
        layer_out = (inputs_f + projected).astype(jnp.bfloat16)
        kept_inputs = store_batch(kept_inputs, layer_in, chosen, valid)
        kept_states = store_batch(kept_states, state_in, chosen, valid)
        kept_scales = store_batch(kept_scales, gate_scale, chosen, valid)
        kept_edges = store_batch(kept_edges, edge_rows, chosen, valid)
        section_store = store_batch(section_store, layer_out, chosen, valid)
        received = from_behind(layer_out, "section", 1)
    acc_zx = jnp.zeros((model_width, 2 * inner_local), jnp.float32)
    acc_dt = jnp.zeros((model_width, heads_local), jnp.float32)
    acc_out = jnp.zeros((inner_local, model_width), jnp.float32)
    acc_bc = jnp.zeros((model_width, 2 * N), jnp.float32)
    acc_gain = jnp.zeros((model_width,), jnp.float32)
    acc_kernel = jnp.zeros((KC, mixed_width), jnp.float32)
    acc_offset = jnp.zeros((mixed_width,), jnp.float32)
    acc_bias = jnp.zeros((heads_local,), jnp.float32)
    acc_log = jnp.zeros((heads_local,), jnp.float32)
    acc_skip = jnp.zeros((heads_local,), jnp.float32)
    acc_gate = jnp.zeros((inner_local,), jnp.float32)
    grad_store = jnp.zeros((batches, token_rows, model_width), jnp.float32)
    received_grad = jnp.zeros((token_rows, model_width), jnp.bfloat16)
    last_section = section_count - 1
    contract = (((0,), (0,)), ((), ()))
    for tick_number in range(batches + section_count - 1):
        batch_index = batches - 1 - tick_number + (last_section - section_index)
        valid = (batch_index >= 0) & (batch_index < batches)
        chosen = jnp.clip(batch_index, 0, batches - 1)
        out_grad = jnp.where(
            section_index == last_section, select_batch(cotangent, chosen), received_grad
        )
        seg_padded = select_batch(seg_local, chosen)
        inputs_f, in_scale, normed, gate_pre, mixed_pre, step_pre = project_in(
            select_batch(kept_inputs, chosen), gain_row, zx_full, bc_full, dt_full
        )
        padded_in = jnp.concatenate([select_batch(kept_edges, chosen), mixed_pre], axis=0).astype(
            jnp.float32
        )
        state_in = select_batch(kept_states, chosen)
        gate_scale = select_batch(kept_scales, chosen)

        def local_mixer(
            padded_arg,
            gate_arg,
            step_arg,
            state_arg,
            kernel_arg,
            offset_arg,
            bias_arg,
            log_arg,
            skip_arg,
        ):
            return mixer_tail(
                mixer_parts(
                    padded_arg,
                    step_arg,
                    kernel_arg,
                    offset_arg,
                    bias_arg,
                    log_arg,
                    seg_padded,
                    heads_local,
                ),
                state_arg,
                gate_arg,
                skip_arg,
            )

        outputs, pullback, extras = jax.vjp(
            local_mixer,
            padded_in,
            gate_pre,
            step_pre,
            state_in,
            kernel,
            offset,
            bias_row,
            log_rate,
            skip_row,
            has_aux=True,
        )
        gated = outputs[0]
        carried, c_part, gate_act = extras
        gate_normed = (gated * gate_scale[:, None] * gate_row[None, :]).astype(jnp.bfloat16)
        normed_gate_grad = jnp.dot(out_grad, out_full.T, preferred_element_type=jnp.float32)
        out_term = lax.dot_general(
            gate_normed, out_grad, contract, preferred_element_type=jnp.float32
        )
        gate_term = jnp.sum(normed_gate_grad * gated * gate_scale[:, None], axis=0)
        projection = lax.psum(
            jnp.sum(normed_gate_grad * gate_row[None, :] * gated, axis=1), "tensor"
        )
        gated_grad = (
            gate_scale[:, None] * gate_row[None, :] * normed_gate_grad
            - gated * (gate_scale**3 * projection / DI)[:, None]
        )
        out_heads = (gated_grad * gate_act).reshape(token_rows, heads_local, head_size)
        pull_state = jnp.einsum("th,thp,tn->hpn", carried, out_heads, c_part, precision=precise)
        state_after = prefix((carried[-1], pull_state), "ctx", chain_combine, chain_start, True)[1]
        (
            padded_grad,
            gate_grad,
            step_grad,
            unused_state,
            kernel_grad,
            offset_grad,
            bias_grad,
            log_grad,
            skip_grad,
        ) = pullback((gated_grad, state_after))
        edge_grad = from_behind(padded_grad[: KC - 1], "ctx", -1)
        mixed_grad = padded_grad[KC - 1 :].at[token_rows - (KC - 1) :].add(edge_grad)
        zx_grad = jnp.concatenate(
            [gate_grad.astype(jnp.bfloat16), mixed_grad[:, :inner_local].astype(jnp.bfloat16)],
            axis=1,
        )
        bc_grad = mixed_grad[:, inner_local:]
        step_low = step_grad.astype(jnp.bfloat16)
        normed_grad = jnp.dot(
            zx_grad,
            zx_full.reshape(model_width, 2 * inner_local).T,
            preferred_element_type=jnp.float32,
        )
        normed_grad = normed_grad + jnp.dot(step_low, dt_full.T, preferred_element_type=jnp.float32)
        normed_grad = normed_grad + jnp.dot(
            bc_grad, bc_full.astype(jnp.float32).T, precision=precise
        )
        zx_term = lax.dot_general(normed, zx_grad, contract, preferred_element_type=jnp.float32)
        dt_term = lax.dot_general(normed, step_low, contract, preferred_element_type=jnp.float32)
        bc_term = lax.dot_general(normed.astype(jnp.float32), bc_grad, contract, precision=precise)
        normed_grad = lax.psum(normed_grad.astype(jnp.bfloat16), "tensor").astype(jnp.float32)
        normed_x = inputs_f * in_scale[:, None]
        weighted = gain_row[None, :] * normed_grad
        input_grad = out_grad.astype(jnp.float32) + in_scale[:, None] * (
            weighted - normed_x * jnp.mean(weighted * normed_x, axis=1)[:, None]
        )
        norm_term = jnp.sum(normed_grad * normed_x, axis=0)
        sent_grad = input_grad.astype(jnp.bfloat16)
        grad_store = store_batch(
            grad_store,
            jnp.where(section_index == 0, input_grad, sent_grad.astype(jnp.float32)),
            chosen,
            valid,
        )
        acc_zx = jnp.where(valid, acc_zx + zx_term, acc_zx)
        acc_dt = jnp.where(valid, acc_dt + dt_term, acc_dt)
        acc_out = jnp.where(valid, acc_out + out_term, acc_out)
        acc_bc = jnp.where(valid, acc_bc + bc_term, acc_bc)
        acc_gain = jnp.where(valid, acc_gain + norm_term, acc_gain)
        acc_kernel = jnp.where(valid, acc_kernel + kernel_grad, acc_kernel)
        acc_offset = jnp.where(valid, acc_offset + offset_grad, acc_offset)
        acc_bias = jnp.where(valid, acc_bias + bias_grad, acc_bias)
        acc_log = jnp.where(valid, acc_log + log_grad, acc_log)
        acc_skip = jnp.where(valid, acc_skip + skip_grad, acc_skip)
        acc_gate = jnp.where(valid, acc_gate + gate_term, acc_gate)
        received_grad = from_behind(sent_grad, "section", -1)
    zx_sum, dt_sum, out_sum = (
        lax.psum_scatter(
            acc_zx.reshape(model_width, 2, inner_local).astype(jnp.bfloat16),
            "ctx",
            scatter_dimension=0,
            tiled=True,
        ).astype(jnp.float32),
        lax.psum_scatter(
            acc_dt.astype(jnp.bfloat16), "ctx", scatter_dimension=0, tiled=True
        ).astype(jnp.float32),
        lax.psum_scatter(
            acc_out.astype(jnp.bfloat16), "ctx", scatter_dimension=1, tiled=True
        ).astype(jnp.float32),
    )
    first_tensor = (tensor_index == 0).astype(jnp.float32)

    def widen(piece):
        full_shape = piece.shape[:-1] + (piece.shape[-1] * tensor_count,)
        return lax.dynamic_update_slice_in_dim(
            jnp.zeros(full_shape, jnp.float32),
            piece,
            tensor_index * piece.shape[-1],
            piece.ndim - 1,
        )

    def narrow(full_array):
        own_width = full_array.shape[-1] // tensor_count
        return lax.dynamic_slice_in_dim(
            full_array, tensor_index * own_width, own_width, full_array.ndim - 1
        )

    sums = lax.psum(
        (
            acc_bc,
            acc_gain * first_tensor,
            acc_kernel[:, inner_local:],
            acc_offset[inner_local:],
            widen(acc_kernel[:, :inner_local]),
            widen(acc_offset[:inner_local]),
            widen(acc_bias),
            widen(acc_log),
            widen(acc_skip),
            widen(acc_gate),
        ),
        ("ctx", "tensor"),
    )
    rows_own = in_bc.shape[1]
    bc_rows = lax.dynamic_slice_in_dim(sums[0], ctx_index * rows_own, rows_own, 0)
    return (
        section_store[None],
        grad_store[None],
        sums[1][None],
        zx_sum[None],
        bc_rows[None],
        dt_sum[None],
        narrow(sums[4])[None],
        narrow(sums[5])[None],
        sums[2][None],
        sums[3][None],
        narrow(sums[6])[None],
        narrow(sums[7])[None],
        narrow(sums[8])[None],
        narrow(sums[9])[None],
        out_sum[None],
    )


def swap_section(value):
    return lax.ppermute(value, "section", [(0, 1), (1, 0)])


def from_partner(value, distance):
    count = lax.axis_size("tensor")
    return lax.ppermute(value, "tensor", [(i, i ^ distance) for i in range(count)])


def with_partners(value):
    return [value] + [from_partner(value, k) for k in range(1, lax.axis_size("tensor"))]


def sum_over_tensor(value):
    return sum(with_partners(value)[1:], value)


def column_block(value, index, width):
    return lax.dynamic_slice_in_dim(value, index * width, width, value.ndim - 1)


def zero_of(value):
    return jnp.minimum(jnp.abs(value[(0,) * value.ndim].astype(f32)).astype(jnp.int32), 0)


def to_micro(value):
    section, ctx, tensor = (lax.axis_index(a) for a in ("section", "ctx", "tensor"))
    count = lax.axis_size("ctx")
    width = value.shape[2] // lax.axis_size("tensor")
    came = []
    for e in range(2):
        sent = 2 * section + ((ctx & 1) ^ e)
        piece = lax.dynamic_slice(value, (sent, 0, tensor * width), (1, value.shape[1], width))[0]
        route = [(s * count + c, (c >> 1) * count + 2 * s + ((c & 1) ^ e)) for s in range(2) for c in range(count)]
        came.append(lax.ppermute(piece, ("section", "ctx"), route))
    even = (ctx & 1) == 0
    return jnp.concatenate([jnp.where(even, came[0], came[1]), jnp.where(even, came[1], came[0])], axis=0)


def to_owners(blocks):
    section, ctx, count = lax.axis_index("section"), lax.axis_index("ctx"), lax.axis_size("ctx")
    rows = blocks[0].shape[0] // 2
    pieces = []
    for e in range(count):
        half, layer = (ctx ^ e) & 1, (ctx ^ e) >> 1
        piece = lax.dynamic_slice_in_dim(jnp.where(layer == 0, blocks[0], blocks[1]), half * rows, rows, 0)
        route = [
            (s * count + z, ((z ^ e) >> 1) * count + 2 * s + ((z ^ e) & 1)) for s in range(2) for z in range(count)
        ]
        pieces.append(lax.ppermute(piece, ("section", "ctx"), route))
    ordered = []
    for n in range(count):
        wanted = ctx ^ n
        e = ((wanted ^ ctx) & 1) | ((((wanted >> 1) ^ section) & 1) << 1)
        chosen = pieces[count - 1]
        for k in range(count - 1):
            chosen = jnp.where(e == k, pieces[k], chosen)
        ordered.append(chosen)
    return jnp.concatenate(ordered, axis=0)


def in_halves(own, section):
    half = own.shape[0] // 2
    keep = lax.dynamic_slice_in_dim(own, section * half, half, 0)
    came = swap_section(lax.dynamic_slice_in_dim(own, (1 - section) * half, half, 0))
    return [jnp.where(section == layer, keep, came) for layer in range(2)]


def own_layer(halves, section):
    keep = jnp.where(section == 0, halves[0], halves[1])
    came = swap_section(jnp.where(section == 0, halves[1], halves[0]))
    return jnp.concatenate([jnp.where(section == 0, keep, came), jnp.where(section == 0, came, keep)], axis=0)


def token_marks(seg_around, rows):
    own = seg_around[HALO : HALO + rows]
    columns = [seg_around[HALO - KC + 1 + k : HALO - KC + 1 + k + rows] == own for k in range(KC)]
    columns += [seg_around[HALO + KC - 1 - k : HALO + KC - 1 - k + rows] == own for k in range(KC)]
    chunks = rows // CH
    before = seg_around[HALO - 1 : HALO - 1 + rows].reshape(chunks, CH)[:, :1]
    last = own.reshape(chunks, CH)[:, -1:]
    columns.append((own.reshape(chunks, CH) == before).reshape(rows))
    columns.append((own.reshape(chunks, CH) == last).reshape(rows))
    columns = [column.astype(f32) for column in columns] + [own.astype(f32)]
    marks = jnp.pad(jnp.stack(columns, axis=1), ((0, 0), (0, LANES - len(columns))))
    return marks, jnp.broadcast_to(own.astype(f32)[None, :], (8, rows))


class Layer:
    pass


def lane_row(values):
    return jnp.pad(values, (0, LANES - values.shape[0]))[None, :]


def pair_rows(values, per):
    pairs = values.shape[0] // per
    padded = jnp.pad(values.reshape(pairs, per), ((0, 0), (0, 8 - per)))
    return jnp.broadcast_to(padded[:, :, None], (pairs, 8, LANES))


def from_pairs(values, per):
    return values[:, :per, 0].reshape(-1)


def unpack(pack, heads, head_size, inner, width):
    layer = Layer()
    layer.taps = jnp.concatenate([pack[: KC + 1, : inner + 2 * N], jnp.zeros((8 - KC - 1, inner + 2 * N), f32)], axis=0)
    layer.norm_gain = pack[KC + 1 : KC + 2, :width]
    layer.gate_gain = pack[KC + 2 : KC + 3, :inner]
    small = pack[KC + 3, : 3 * heads].reshape(3, heads)
    per = LANES // head_size
    decay = -jnp.exp(small[1])
    layer.bias_lanes, layer.decay_lanes = lane_row(small[0]), lane_row(decay)
    layer.bias_rows, layer.decay_rows = pair_rows(small[0], per), pair_rows(decay, per)
    layer.skip = jnp.repeat(small[2], head_size)[None, :]
    return layer


transposed = (((0,), (0,)), ((), ()))
across = (((1,), (1,)), ((), ()))


def project(layer, marks, seg_row, head_size, held=()):
    layer.pre = jnp.dot(layer.normed, layer.mix[:, LANES:], preferred_element_type=f32).astype(bf16)
    step = jnp.dot(layer.normed, layer.mix[:, :LANES], preferred_element_type=f32)
    layer.halo = lax.ppermute(layer.pre[-HALO:], "section", [(0, 1)])
    (layer.conv, layer.y, layer.own_state, last_state, layer.cum, layer.rate, layer.cum_rows, layer.step_rows) = scan_forward(
        layer.pre, layer.halo, layer.taps, marks, seg_row, step, layer.bias_lanes, layer.decay_lanes, head_size, held
    )
    layer.state_in = lax.ppermute(last_state, "section", [(0, 1)])


def gate(layer, marks, grad=None):
    layer.gate = jnp.dot(layer.normed, layer.gate_weight, preferred_element_type=f32)
    layer.ssm, layer.gained, layer.entering, sums = gate_forward(
        layer.y, layer.conv, layer.cum, marks, layer.own_state, layer.state_in, layer.gate, layer.skip, layer.gate_gain, grad
    )
    return sum_over_tensor(sums)


def gate_side(layer, grad, sums, marks, channels, held=()):
    (layer.out_grad, layer.gate_grad, layer.pulled, first, layer.gain_grad, layer.skip_grad, layer.gate_dots) = gate_backward(
        grad, layer.gate, layer.ssm, layer.conv, layer.cum, marks, sums, layer.gate_gain, channels, held
    )
    layer.after = lax.ppermute(first, "section", [(1, 0)])


def scan_side(layer, marks, seg_row, head_size, held_intra=(), held_scan=(), held_conv=(), after_intra=None, late_held=None):
    per = LANES // head_size
    scaled_grad, rate_rows, b_intra, c_intra = intra_backward(
        layer.out_grad, layer.conv, layer.cum, layer.rate, layer.cum_rows, marks, seg_row, head_size, held_intra
    )
    if after_intra is not None:
        held_conv = (*held_conv, *after_intra(rate_rows))
    conv_grad, layer.taps_grad, step_grad, log_grad, bias_grad = scan_backward(
        layer.out_grad, scaled_grad, layer.conv, layer.cum, layer.rate, rate_rows, layer.step_rows, layer.entering,
        layer.pulled, layer.after, layer.skip, layer.decay_rows, b_intra, c_intra, layer.pre, layer.halo,
        layer.taps, marks, head_size, held_scan,
    )
    next_grad = lax.ppermute(conv_grad[:8], "section", [(1, 0)])
    if late_held is not None:
        held_conv = (*held_conv, *late_held(conv_grad))
    layer.mix_grad, layer.map_grad, dots = conv_backward(
        conv_grad, next_grad, layer.taps, marks, layer.pre, layer.gate_dots, step_grad, layer.step_rows,
        layer.bias_rows, head_size, held_conv,
    )
    layer.dots = sum_over_tensor(dots)
    heads = layer.skip_grad.shape[1] // head_size
    layer.small = jnp.concatenate([
        from_pairs(bias_grad, per), from_pairs(log_grad, per), layer.skip_grad.reshape(heads, head_size).sum(axis=1)
    ])


def scatter_rows(term):
    return lax.psum_scatter(term, ("ctx", "section"), scatter_dimension=0, tiled=True)


def whole_micro_body(
    tokens, cotangent, seg_ids, norm_gain, in_zx, in_bc, in_dt, conv_x, conv_xb, conv_bc, conv_bcb, dt_bias, a_log,
    skip_gain, gate_gain, out_w,
):
    section, ctx, tensor = (lax.axis_index(a) for a in ("section", "ctx", "tensor"))
    tensors, ctxs = lax.axis_size("tensor"), lax.axis_size("ctx")
    width = tokens.shape[2]
    own_width = width // tensors
    inner = conv_x.shape[2]
    heads = dt_bias.shape[1]
    head_size = inner // heads
    mixed = inner + 2 * N
    channels = inner * tensors
    rows = seg_ids.shape[1] // 2
    index = tensor.astype(jnp.int32).reshape(1)

    def block_rows(weight, b):
        return lax.dynamic_slice_in_dim(weight, b * own_width, own_width, 0)

    def gather_rows(half):
        return lax.all_gather(half, ("ctx", "section"), axis=0, tiled=True)

    own_mix = jnp.concatenate([jnp.pad(in_dt[0], ((0, 0), (0, LANES - heads))), in_zx[0, :, 1], in_bc[0]], axis=1)
    mix_halves = in_halves(own_mix, section)
    mix_first = gather_rows(mix_halves[0])
    token_block = to_micro(tokens)
    rest_halves = in_halves(jnp.concatenate([in_zx[0, :, 0], out_w[0].T], axis=1), section)

    def line(values):
        return jnp.pad(values.astype(f32), (0, width - values.shape[0]))[None, :]

    own_pack = jnp.concatenate(
        [line(jnp.concatenate([conv_x[0, k], conv_bc[0, k]])) for k in range(KC)]
        + [
            line(jnp.concatenate([conv_xb[0], conv_bcb[0]])), line(norm_gain[0]), line(gate_gain[0]),
            line(jnp.concatenate([dt_bias[0], a_log[0], skip_gain[0]])),
        ],
        axis=0,
    )
    other_pack = swap_section(own_pack)
    first, second = (
        unpack(jnp.where(section == n, own_pack, other_pack), heads, head_size, inner, width) for n in range(2)
    )
    seg_mine = lax.dynamic_index_in_dim(seg_ids, ctx, 0, keepdims=False)
    seg_around = jnp.concatenate([jnp.full((HALO,), -1, jnp.int32), seg_mine, jnp.full((HALO,), -2, jnp.int32)])
    seg_around = lax.dynamic_slice_in_dim(seg_around, section * rows, rows + 2 * HALO, 0)
    marks, seg_row = token_marks(seg_around, rows)

    first.block = token_block
    first.gate_weight = gather_rows(ordered(rest_halves[0][:, :inner], token_block))
    first.normed, first.in_scale = join_norm(with_partners(first.block), index, first.norm_gain, rows)
    first.out_turned = gather_rows(ordered(rest_halves[0][:, inner:], first.normed))
    first.mix = mix_first
    project(first, marks, seg_row, head_size)
    second.mix = gather_rows(ordered(mix_halves[1], first.pre))
    rest_second = gather_rows(ordered(rest_halves[1], first.conv))
    second.gate_weight, second.out_turned = rest_second[:, :inner], rest_second[:, inner:]
    cot_block = to_micro(ordered(cotangent, first.pre))
    sums_first = gate(first, marks)

    def gate_low(layer, sums):
        layer.gated = (layer.gained * lax.rsqrt(sums[0] / channels + epsilon)[:, None]).astype(bf16)

    def blocks_of(total, dtype):
        parts = [column_block(total, tensor ^ n, own_width) for n in range(tensors)]
        return [parts[0]] + [part.astype(dtype) for part in parts[1:]]

    def out_terms(layer, dtype):
        return blocks_of(lax.dot_general(layer.gated, layer.out_turned, across, preferred_element_type=f32), dtype)

    gate_low(first, sums_first)
    terms = out_terms(first, f32)
    projected = sum([from_partner(terms[n], n) for n in range(1, tensors)], terms[0])
    second.block = (first.block.astype(f32) + projected).astype(bf16)

    second.normed, second.in_scale = join_norm(with_partners(second.block), index, second.norm_gain, rows)
    project(second, marks, seg_row, head_size)
    cot_full = join(with_partners(ordered(cot_block, second.pre)), index, bf16, 0)
    grad_second = jnp.dot(cot_full, second.out_turned, preferred_element_type=f32)
    sums_second = gate(second, marks, grad_second)

    def input_terms(layer):
        total = lax.dot_general(layer.gate_grad, layer.gate_weight, across, preferred_element_type=f32)
        total = total + lax.dot_general(layer.mix_grad, layer.mix, across, preferred_element_type=f32)
        rest = (layer.map_grad - layer.mix_grad[:, LANES + inner :].astype(f32)).astype(bf16)
        total = total + lax.dot_general(rest, layer.mix[:, LANES + inner :], across, preferred_element_type=f32)
        return blocks_of(total, bf16)

    def send_terms(layer, terms):
        return [from_partner(ordered(terms[n], layer.dots), n) for n in range(1, tensors)]

    def input_side(layer, own, sent, out_grad_block, held=()):
        return input_gradient(
            own, sent, layer.dots, layer.block, out_grad_block, layer.in_scale,
            column_block(layer.norm_gain, tensor, own_width), width, held,
        )

    def rest_term(layer, out_grad, *others):
        low = [
            lax.dot_general(layer.normed, ordered(layer.gate_grad, *others), transposed, preferred_element_type=f32).astype(bf16),
            lax.dot_general(out_grad, layer.gated, transposed, preferred_element_type=f32).astype(bf16),
        ]
        return jnp.concatenate(low, axis=1)

    def share(layer, *others):
        count = rows // tensors
        map_grad = ordered(layer.map_grad, *others)

        def part(b):
            return lax.dynamic_slice_in_dim(map_grad, b * count, count, 0)

        total = sum([from_partner(part(tensor ^ k), k) for k in range(1, tensors)], part(tensor))
        layer.map_share = total.astype(bf16)

    def mix_start(layer):
        return lax.dot_general(layer.normed, layer.mix_grad, transposed, preferred_element_type=f32).astype(bf16)

    def mix_term(layer, started, *others):
        pieces = [ordered(piece, *others) for piece in with_partners(layer.map_share)]
        return place_maps(index, started, layer.normed, pieces, LANES + inner)

    def small_pack(layer, norm_grad):
        def row(values):
            return jnp.pad(values, (0, mixed - values.shape[0]))[None, :]

        return jnp.concatenate(
            [layer.taps_grad, row(layer.gain_grad[0]), row(layer.small), row(norm_grad[0]), jnp.zeros((5, mixed), f32)], axis=0
        )

    gate_low(second, sums_second)
    out_second = lax.dot_general(second.gated, second.out_turned, across, preferred_element_type=f32).astype(bf16)
    result = lax.psum_scatter(out_second, "tensor", scatter_dimension=1, tiled=True)
    gate_side(second, grad_second, sums_second, marks, channels, (out_second,))
    rest_term_second = rest_term(second, cot_full)
    rest_sum_second = scatter_rows(rest_term_second)
    scan_side(second, marks, seg_row, head_size, held_scan=(rest_term_second,), held_conv=(result,))
    terms = input_terms(second)
    sent = send_terms(second, terms)
    middle_block, norm_second = input_side(second, terms[0], sent, cot_block)
    share(second, *sent)
    result = (second.block.astype(f32) + ordered(result, second.dots).astype(f32)).astype(bf16)
    output_pieces = to_owners([second.block, result])
    mix_started = mix_start(second)
    middle = join(with_partners(middle_block), index, bf16, 0, (mix_started, output_pieces))
    mix_term_second = mix_term(second, mix_started, rest_sum_second, middle)
    mix_sum_second = scatter_rows(mix_term_second)

    grad_first = jnp.dot(middle, first.out_turned, preferred_element_type=f32)
    crossed = jnp.sum(grad_first * first.gained, axis=1)
    crossed = sum_over_tensor(jnp.broadcast_to(crossed[None, :], (8, rows)))
    sums_first = jnp.concatenate([sums_first[:1], crossed[:1], sums_first[2:]], axis=0)
    gate_side(first, grad_first, sums_first, marks, channels)
    outputs = with_partners(ordered(output_pieces, first.out_grad))
    rest_terms = []

    def after_scan(conv_grad):
        rest_terms.append(rest_term(first, middle, conv_grad, *outputs[1:]))
        return rest_terms

    scan_side(
        first, marks, seg_row, head_size, held_intra=(mix_term_second,), held_conv=(rest_sum_second, mix_sum_second), late_held=after_scan,
    )
    rest_sum_first = scatter_rows(rest_terms[0])
    terms = input_terms(first)
    sent = send_terms(first, terms)
    share(first, first.dots)
    last_block, norm_first = input_side(first, terms[0], sent, middle_block)
    grad_pieces = to_owners([last_block, middle_block])
    grads = with_partners(grad_pieces)
    mix_sum_first = scatter_rows(mix_term(first, mix_start(first), rest_sum_first, grad_pieces))
    places = jnp.stack([tensor, ctx]).astype(jnp.int32)
    outputs = join_micro(places, outputs, bf16, (last_block,))

    rest_sum = own_layer([rest_sum_first, rest_sum_second], section).astype(f32)
    mix_sum = own_layer([mix_sum_first, mix_sum_second], section).astype(f32)
    bc_sum = mix_sum[:, LANES + inner :]
    pack_first, pack_second = ordered(small_pack(first, norm_first), grads[1]), small_pack(second, norm_second)
    pack = jnp.where(section == 0, pack_first, pack_second) + swap_section(
        jnp.where(section == 0, pack_second, pack_first)
    )
    pack = sum(
        [lax.ppermute(pack, "ctx", [(c, (c + d) % ctxs) for c in range(ctxs)]) for d in range(1, ctxs)], pack
    )
    shared = with_partners(jnp.concatenate([pack[:8, inner:], jnp.broadcast_to(pack[10:11, :own_width], (8, own_width))], axis=1))
    taps_bc = sum([piece[:, : 2 * N] for piece in shared[1:]], shared[0][:, : 2 * N])
    norm = join([piece[:, 2 * N :] for piece in shared], index, f32, 0)[0]
    small = pack[9, : 3 * heads].reshape(3, heads)
    zx_sum = jnp.stack([rest_sum[:, :inner], mix_sum[:, LANES : LANES + inner]], axis=1)
    out_sum = rest_sum[:, inner:].T
    input_grads = join_micro(places, grads, f32, (outputs,))
    return (
        outputs.reshape(1, ctxs, -1, width),
        input_grads.reshape(1, ctxs, -1, width),
        norm[None],
        zx_sum[None],
        bc_sum[None],
        mix_sum[:, :heads][None],
        pack[:KC, :inner][None],
        pack[KC, :inner][None],
        taps_bc[:KC][None],
        taps_bc[KC][None],
        small[0][None],
        small[1][None],
        small[2][None],
        pack[8, :inner][None],
        out_sum[None],
    )


def fits(shape, batches):
    return shape["ctx"] == batches == 4 and shape["section"] == 2 and shape["tensor"] & (shape["tensor"] - 1) == 0


def solution(mesh):
    def step(*args):
        chosen = whole_micro_body if fits(dict(mesh.shape), args[0].shape[0]) else body
        return jax.shard_map(
            chosen,
            mesh=mesh,
            in_specs=(
                P(None, "ctx", None),
                P(None, "ctx", None),
                P(),
                P("section", None),
                P("section", "ctx", None, "tensor"),
                P("section", "ctx", None),
                P("section", "ctx", "tensor"),
                P("section", None, "tensor"),
                P("section", "tensor"),
                P("section", None, None),
                P("section", None),
                P("section", "tensor"),
                P("section", "tensor"),
                P("section", "tensor"),
                P("section", "tensor"),
                P("section", "tensor", "ctx"),
            ),
            out_specs=(
                P("section", None, "ctx", None),
                P("section", None, "ctx", None),
                P("section", None),
                P("section", "ctx", None, "tensor"),
                P("section", "ctx", None),
                P("section", "ctx", "tensor"),
                P("section", None, "tensor"),
                P("section", "tensor"),
                P("section", None, None),
                P("section", None),
                P("section", "tensor"),
                P("section", "tensor"),
                P("section", "tensor"),
                P("section", "tensor"),
                P("section", "tensor", "ctx"),
            ),
            check_vma=False,
        )(*args)

    return step
```

```python
from functools import partial

import jax
import jax.numpy as jnp
from jax import lax
from jax.experimental import pallas as pl
from jax.experimental.pallas import tpu as pltpu
from jax.sharding import PartitionSpec as P

bf16 = jnp.bfloat16
f32 = jnp.float32
precise = lax.Precision.HIGHEST
epsilon = 1e-05
N = 128
KC = 4
CH = 256
DI = 3072
HALO = 16
LANES = 128
VMEM_BYTES = 60 * 1024 * 1024

M_FWD, M_BWD, M_ENTER, M_LEAVE, M_SEG = 0, 4, 8, 9, 10


def mm(a, b):
    return lax.dot_general(a, b, (((1,), (0,)), ((), ())), preferred_element_type=f32)


def mm_nt(a, b, precision=None):
    return lax.dot_general(a, b, (((1,), (1,)), ((), ())), preferred_element_type=f32, precision=precision)


def mm_tn(a, b):
    return lax.dot_general(a, b, (((0,), (0,)), ((), ())), preferred_element_type=f32)


def split(v):
    high = v.astype(bf16)
    return high, (v - high.astype(f32)).astype(bf16)


def rows_of(selector, values):
    high, low = split(values)
    return mm_nt(selector, high) + mm_nt(selector, low)


def times_mask(rows, mask):
    high, low = split(rows)
    return mm(high, mask) + mm(low, mask)


def left_parts(a):
    high, low = split(a)
    return jnp.concatenate([high, low, high], axis=1)


def right_parts(b, axis):
    high, low = split(b)
    return jnp.concatenate([high, high, low], axis=axis)


def thirds(v):
    high = v.astype(bf16)
    rest = v - high.astype(f32)
    middle = rest.astype(bf16)
    return high, middle, (rest - middle.astype(f32)).astype(bf16)


def left_exact(a):
    high, middle, low = thirds(a)
    return jnp.concatenate([high, middle, high, middle, low, high], axis=1)


def right_exact(b, axis):
    high, middle, low = thirds(b)
    return jnp.concatenate([high, high, middle, middle, high, low], axis=axis)


def precise_nt(a, b):
    return mm_nt(left_parts(a), right_parts(b, 1))


def precise_mm(a, b):
    return mm(left_parts(a), right_parts(b, 0))


def iota2(shape):
    return lax.broadcasted_iota(jnp.int32, shape, 0), lax.broadcasted_iota(jnp.int32, shape, 1)


def sigmoid(v):
    return 1.0 / (1.0 + jnp.exp(-v))


def softplus(v):
    return jnp.maximum(v, 0.0) + jnp.log1p(jnp.exp(-jnp.abs(v)))


def fill_padded(padded, halo_ref, pre_ref, rows):
    padded[pl.ds(0, HALO), :] = halo_ref[...].astype(f32)
    padded[pl.ds(HALO, rows), :] = pre_ref[...].astype(f32)


def spread_marks(wide, marks_ref, first):
    for k in range(KC - 1):
        wide[k] = jnp.broadcast_to(marks_ref[:, first + k : first + k + 1], wide.shape[1:])


def conv_tile(padded, taps_ref, marks, start, count):
    total = jnp.zeros((count, LANES), f32) + taps_ref[KC : KC + 1, :]
    for k in range(KC):
        shifted = padded[pl.ds(start + HALO - KC + 1 + k, count), :]
        if k == KC - 1:
            total = total + taps_ref[k : k + 1, :] * shifted
        else:
            total = total + taps_ref[k : k + 1, :] * (shifted * marks[k, pl.ds(start, count), :])
    return total


TILE = 128


def scan_forward_kernel(
    head_size, rows, pre_ref, halo_ref, taps_ref, marks_ref, seg_ref, step_ref, bias_ref, decay_ref,
    conv_ref, y_ref, own_state_ref, last_state_ref, cum_ref, rate_ref, cum_rows_ref, step_rows_ref,
    padded, b_all, b_turned, scores, cum_all, rate_all, step_all, cum_turned, step_turned, wide_marks,
):
    i = pl.program_id(0)
    chunks = rows // CH
    fill_padded(padded, halo_ref, pre_ref, rows)

    @pl.when(i == 0)
    def _():
        spread_marks(wide_marks, marks_ref, M_FWD)

    for start in range(0, rows, TILE):
        value = conv_tile(padded, taps_ref, wide_marks, start, TILE)
        conv_ref[pl.ds(start, TILE), :] = value / (1.0 + jnp.exp(-value))

    @pl.when(i == 0)
    def _():
        b_all[...] = conv_ref[...]
        b_turned[...] = conv_ref[...].T
        shifted = step_ref[...] + bias_ref[...]
        rate = softplus(shifted)
        step_all[...] = shifted
        rate_all[...] = rate
        r, c = iota2((CH, CH))
        tri = (r >= c).astype(f32)
        for n in range(chunks):
            part = rate[n * CH : (n + 1) * CH, :] * decay_ref[...]
            cum_all[pl.ds(n * CH, CH), :] = lax.dot_general(
                tri, part, (((1,), (0,)), ((), ())), preferred_element_type=f32, precision=precise
            )

    @pl.when(i == 1)
    def _():
        r, c = iota2((CH, CH))
        for n in range(chunks):
            here = pl.ds(n * CH, CH)
            same = marks_ref[here, M_SEG : M_SEG + 1] == seg_ref[0:1, here]
            value = mm_nt(left_exact(conv_ref[here, :]), right_exact(b_all[here, :], 1))
            scores[n] = jnp.where((r >= c) & same, value, 0.0)
        per = LANES // head_size
        for turned, values in ((cum_turned, cum_all), (step_turned, step_all)):
            rows_all = values[...].T
            for j in range(turned.shape[0]):
                turned[j, 0:per, :] = rows_all[per * j : per * (j + 1), :]

    @pl.when(i >= 2)
    def _():
        j = i - 2
        per = LANES // head_size
        row, lane = iota2((LANES, LANES))
        widen = (row == per * j + lane // head_size).astype(f32)
        cum = lax.dot_general(cum_all[...], widen, (((1,), (0,)), ((), ())), preferred_element_type=f32, precision=precise)
        rate = lax.dot_general(rate_all[...], widen, (((1,), (0,)), ((), ())), preferred_element_type=f32, precision=precise)
        cum_rows = cum_turned[j]
        cum_rows_ref[0] = cum_rows
        step_rows_ref[0] = step_turned[j]
        cum_ref[...] = cum
        rate_ref[...] = rate
        lane_c = lax.broadcasted_iota(jnp.int32, (CH, LANES), 1)
        states = []
        for n in range(chunks):
            here = pl.ds(n * CH, CH)
            span = slice(n * CH, (n + 1) * CH)
            scaled = rate[span] * conv_ref[here, :]
            out = jnp.zeros((CH, LANES), f32)
            for h in range(per):
                column = cum[span, h * head_size : h * head_size + 1]
                value = []
                for first, past in ((0, CH // 2), (CH // 2, CH)):
                    spread = column[first:past] - cum_rows[h : h + 1, n * CH : n * CH + past]
                    weights = scores[n, first:past, :past] * jnp.exp(jnp.minimum(spread, 0.0))
                    value.append(mm(left_exact(weights), right_exact(scaled[:past], 0)))
                value = jnp.concatenate(value, axis=0)
                out = value if per == 1 else jnp.where(lane_c // head_size == h, value, out)
            y_ref[here, :] = out
            leave = jnp.exp(cum[(n + 1) * CH - 1 : (n + 1) * CH, :] - cum[span]) * marks_ref[here, M_LEAVE : M_LEAVE + 1]
            state = mm(left_exact(b_turned[:, here]), right_exact(scaled * leave, 0))
            own_state_ref[n] = state
            states.append(state)
        total = states[0]
        for n in range(1, chunks):
            last = (n + 1) * CH - 1
            kept = jnp.exp(cum[last : last + 1, :]) * marks_ref[last : last + 1, M_ENTER : M_ENTER + 1]
            total = kept * total + states[n]
        last_state_ref[...] = total


def call(kernel, held, in_specs, **rest):
    count = len(held)

    def run(*refs):
        kernel(*refs[count:])

    made = pl.pallas_call(run, in_specs=[pl.BlockSpec(memory_space=pl.ANY)] * count + in_specs, **rest)
    return lambda *args: made(*held, *args)


def ordered(value, *others):
    anywhere = pl.BlockSpec(memory_space=pl.ANY)
    return pl.pallas_call(
        lambda *refs: None,
        in_specs=[anywhere] * (1 + len(others)),
        out_specs=anywhere,
        out_shape=jax.ShapeDtypeStruct(value.shape, value.dtype),
        input_output_aliases={0: 0},
        cost_estimate=cost(0),
        name="ordered",
    )(value, *others)


def whole(shape):
    return pl.BlockSpec(shape, lambda i: (0,) * len(shape))


def params(limit=VMEM_BYTES):
    return pltpu.CompilerParams(vmem_limit_bytes=limit, dimension_semantics=("arbitrary",))


def cost(microseconds):
    return pl.CostEstimate(flops=0, bytes_accessed=int(microseconds * 3e6), transcendentals=0)


def scan_forward(pre, halo, taps, marks, seg_row, step, bias, decay, head_size, held=()):
    rows, mixed = pre.shape
    inner = mixed - 2 * N
    pairs = inner // LANES
    chunks = rows // CH
    steps = pairs + 2
    column = lambda i: (0, (i + pairs) % steps)
    pair = lambda i: (0, jnp.maximum(i - 2, 0))
    return call(
        partial(scan_forward_kernel, head_size, rows),
        held,
        grid=(steps,),
        in_specs=[
            pl.BlockSpec((rows, LANES), column),
            pl.BlockSpec((HALO, LANES), column),
            pl.BlockSpec((8, LANES), column),
            whole((rows, LANES)),
            whole((8, rows)),
            whole((rows, LANES)),
            whole((1, LANES)),
            whole((1, LANES)),
        ],
        out_specs=[
            pl.BlockSpec((rows, LANES), column),
            pl.BlockSpec((rows, LANES), pair),
            pl.BlockSpec((chunks, N, LANES), lambda i: (0, 0, jnp.maximum(i - 2, 0))),
            pl.BlockSpec((N, LANES), pair),
            pl.BlockSpec((rows, LANES), pair),
            pl.BlockSpec((rows, LANES), pair),
            pl.BlockSpec((1, 8, rows), lambda i: (jnp.maximum(i - 2, 0), 0, 0)),
            pl.BlockSpec((1, 8, rows), lambda i: (jnp.maximum(i - 2, 0), 0, 0)),
        ],
        out_shape=[
            jax.ShapeDtypeStruct((rows, mixed), f32),
            jax.ShapeDtypeStruct((rows, inner), f32),
            jax.ShapeDtypeStruct((chunks, N, inner), f32),
            jax.ShapeDtypeStruct((N, inner), f32),
            jax.ShapeDtypeStruct((rows, inner), f32),
            jax.ShapeDtypeStruct((rows, inner), f32),
            jax.ShapeDtypeStruct((pairs, 8, rows), f32),
            jax.ShapeDtypeStruct((pairs, 8, rows), f32),
        ],
        scratch_shapes=[
            pltpu.VMEM((rows + HALO, LANES), f32),
            pltpu.VMEM((rows, LANES), f32),
            pltpu.VMEM((N, rows), f32),
            pltpu.VMEM((chunks, CH, CH), f32),
            pltpu.VMEM((rows, LANES), f32),
            pltpu.VMEM((rows, LANES), f32),
            pltpu.VMEM((rows, LANES), f32),
            pltpu.VMEM((pairs, 8, rows), f32),
            pltpu.VMEM((pairs, 8, rows), f32),
            pltpu.VMEM((KC - 1, rows, LANES), f32),
        ],
        compiler_params=params(),
        cost_estimate=cost(15),
        name="scan_forward",
    )(pre, halo, taps, marks, seg_row, step, bias, decay)


def gate_kernel(
    chunks, with_grad, y_ref, conv_ref, c_ref, cum_ref, marks_ref, own_state_ref, state_ref, gate_ref, skip_ref, gain_ref,
    *rest,
):
    if with_grad:
        grad_ref, ssm_ref, gated_ref, entering_ref, sums_ref, c_parts, squares, products = rest
    else:
        ssm_ref, gated_ref, entering_ref, sums_ref, c_parts, squares = rest
    i = pl.program_id(0)

    @pl.when(i == 0)
    def _():
        c_parts[...] = left_exact(c_ref[...])

    state = state_ref[...]
    for n in range(chunks):
        here = pl.ds(n * CH, CH)
        entering_ref[n] = state
        enter = jnp.exp(cum_ref[here, :]) * marks_ref[here, M_ENTER : M_ENTER + 1]
        ssm_ref[here, :] = (
            y_ref[here, :]
            + enter * mm(c_parts[here, :], right_exact(state, 0))
            + skip_ref[...] * conv_ref[here, :]
        )
        state = enter[CH - 1 : CH, :] * state + own_state_ref[n]
    gate = gate_ref[...]
    gated = ssm_ref[...] * (gate * sigmoid(gate))
    scaled = gated * gain_ref[...]
    gated_ref[...] = scaled
    totals = [(squares, gated * gated)] + ([(products, scaled * grad_ref[...])] if with_grad else [])

    @pl.when(i == 0)
    def _():
        for total, value in totals:
            total[...] = value

    @pl.when(i > 0)
    def _():
        for total, value in totals:
            total[...] += value

    @pl.when(i == pl.num_programs(0) - 1)
    def _():
        row = lax.broadcasted_iota(jnp.int32, (8, LANES), 0)
        sums = [rows_of((row == n).astype(bf16), total[...]) for n, (total, _) in enumerate(totals)]
        sums_ref[...] = sum(sums[1:], sums[0])


def gate_forward(y, conv, cum, marks, own_state, state_in, gate, skip, gain, grad=None, held=()):
    rows, inner = y.shape
    pairs = inner // LANES
    chunks = rows // CH
    block = pl.BlockSpec((rows, LANES), lambda i: (0, i))
    line = pl.BlockSpec((1, LANES), lambda i: (0, i))
    states = pl.BlockSpec((chunks, N, LANES), lambda i: (0, 0, i))
    last = conv.shape[1] // LANES - 1
    in_specs = [
        block, block, pl.BlockSpec((rows, LANES), lambda i: (0, last)), block, whole((rows, LANES)), states,
        pl.BlockSpec((N, LANES), lambda i: (0, i)), block, line, line,
    ]
    args = [y, conv, conv, cum, marks, own_state, state_in, gate, skip, gain]
    if grad is not None:
        in_specs.append(block)
        args.append(grad)
    return call(
        partial(gate_kernel, chunks, grad is not None),
        held,
        grid=(pairs,),
        in_specs=in_specs,
        out_specs=[block, block, states, whole((8, rows))],
        out_shape=[
            jax.ShapeDtypeStruct((rows, inner), f32),
            jax.ShapeDtypeStruct((rows, inner), f32),
            jax.ShapeDtypeStruct((chunks, N, inner), f32),
            jax.ShapeDtypeStruct((8, rows), f32),
        ],
        scratch_shapes=[pltpu.VMEM((rows, 6 * N), bf16)] + [pltpu.VMEM((rows, LANES), f32)] * (1 if grad is None else 2),
        compiler_params=params(),
        cost_estimate=cost(6),
        name="gate_forward",
    )(*args)


def gate_backward_kernel(
    chunks, channels, grad_ref, gate_ref, ssm_ref, conv_ref, c_ref, cum_ref, marks_ref, sums_ref, gain_ref,
    out_grad_ref, gate_grad_ref, pulled_ref, first_ref, gain_grad_ref, skip_grad_ref, dots_ref,
    scale_all, shift_all, c_turned, products,
):
    i = pl.program_id(0)

    @pl.when(i == 0)
    def _():
        scale = lax.rsqrt(sums_ref[0:1, :] / channels + epsilon)
        shift = scale * scale * scale * sums_ref[1:2, :] / channels
        rows = scale.shape[1]
        scale_all[...] = jnp.broadcast_to(scale, (LANES, rows)).T
        shift_all[...] = jnp.broadcast_to(shift, (LANES, rows)).T
        for n in range(chunks):
            c_turned[n] = left_parts(c_ref[pl.ds(n * CH, CH), :].T)

    gate = gate_ref[...]
    sig = sigmoid(gate)
    act = gate * sig
    ssm = ssm_ref[...]
    gated = ssm * act
    grad = grad_ref[...]
    scale = scale_all[...]
    gated_grad = scale * gain_ref[...] * grad - gated * shift_all[...]
    gain_grad_ref[...] = jnp.sum(grad * gated * scale, axis=0, keepdims=True)
    out_grad = gated_grad * act
    out_grad_ref[...] = out_grad
    skip_grad_ref[...] = jnp.sum(out_grad * conv_ref[...], axis=0, keepdims=True)
    gate_grad = gated_grad * ssm * (sig * (1.0 + gate * (1.0 - sig)))
    gate_grad_ref[...] = gate_grad.astype(bf16)
    dots = gate_grad * gate
    kept = []
    for n in range(chunks):
        here = pl.ds(n * CH, CH)
        enter = jnp.exp(cum_ref[here, :]) * marks_ref[here, M_ENTER : M_ENTER + 1]
        pulled = mm(c_turned[n], right_parts(out_grad_ref[here, :] * enter, 0))
        pulled_ref[n] = pulled
        kept.append((enter[CH - 1 : CH, :], pulled))
    first = kept[-1][1]
    for last_enter, pulled in kept[-2::-1]:
        first = last_enter * first + pulled
    first_ref[...] = first

    @pl.when(i == 0)
    def _():
        products[...] = dots

    @pl.when(i > 0)
    def _():
        products[...] += dots

    @pl.when(i == pl.num_programs(0) - 1)
    def _():
        row = lax.broadcasted_iota(jnp.int32, (8, LANES), 0)
        dots_ref[...] = rows_of((row == 0).astype(bf16), products[...])


def gate_backward(grad, gate, ssm, conv, cum, marks, sums, gain, channels, held=()):
    rows, inner = ssm.shape
    pairs = inner // LANES
    chunks = rows // CH
    block = pl.BlockSpec((rows, LANES), lambda i: (0, i))
    line = pl.BlockSpec((1, LANES), lambda i: (0, i))
    states = pl.BlockSpec((chunks, N, LANES), lambda i: (0, 0, i))
    last = conv.shape[1] // LANES - 1
    return call(
        partial(gate_backward_kernel, chunks, float(channels)),
        held,
        grid=(pairs,),
        in_specs=[
            block, block, block, block, pl.BlockSpec((rows, LANES), lambda i: (0, last)), block,
            whole((rows, LANES)), whole((8, rows)), line,
        ],
        out_specs=[block, block, states, pl.BlockSpec((N, LANES), lambda i: (0, i)), line, line, whole((8, rows))],
        out_shape=[
            jax.ShapeDtypeStruct((rows, inner), f32),
            jax.ShapeDtypeStruct((rows, inner), bf16),
            jax.ShapeDtypeStruct((chunks, N, inner), f32),
            jax.ShapeDtypeStruct((N, inner), f32),
            jax.ShapeDtypeStruct((1, inner), f32),
            jax.ShapeDtypeStruct((1, inner), f32),
            jax.ShapeDtypeStruct((8, rows), f32),
        ],
        scratch_shapes=[
            pltpu.VMEM((rows, LANES), f32), pltpu.VMEM((rows, LANES), f32), pltpu.VMEM((chunks, N, 3 * CH), bf16),
            pltpu.VMEM((rows, LANES), f32),
        ],
        compiler_params=params(),
        cost_estimate=cost(7),
        name="gate_backward",
    )(grad, gate, ssm, conv, conv, cum, marks, sums, gain)


def intra_backward_kernel(
    head_size, chunks, out_grad_ref, conv_ref, b_ref, c_ref, cum_ref, rate_ref, cum_rows_ref, marks_ref, seg_ref,
    scaled_grad_ref, rate_rows_ref, b_grad_ref, c_grad_ref,
    scores, scores_grad,
):
    i = pl.program_id(0)
    per = LANES // head_size
    r, c = iota2((CH, CH))

    @pl.when(i == 0)
    def _():
        for n in range(chunks):
            here = pl.ds(n * CH, CH)
            same = marks_ref[here, M_SEG : M_SEG + 1] == seg_ref[0:1, here]
            value = precise_nt(b_ref[here, :], c_ref[here, :])
            scores[n] = jnp.where((r <= c) & same, value, 0.0)
            scores_grad[n] = jnp.zeros((CH, CH), f32)

    from_row = (r >= c).astype(bf16)
    from_row = jnp.concatenate([from_row, from_row], axis=0)
    lane_c = lax.broadcasted_iota(jnp.int32, (CH, LANES), 1)
    rate_rows_ref[...] = jnp.zeros(rate_rows_ref.shape, f32)
    for n in range(chunks):
        here = pl.ds(n * CH, CH)
        scaled = rate_ref[here, :] * conv_ref[here, :]
        grad_parts = right_parts(out_grad_ref[here, :], 1)
        grad_low = grad_parts[:, :LANES]
        out = jnp.zeros((CH, LANES), f32)
        for h in range(per):
            mine = lane_c // head_size == h
            spread = cum_rows_ref[0, h : h + 1, here] - cum_ref[here, h * head_size : h * head_size + 1]
            decay = jnp.exp(jnp.minimum(spread, 0.0))
            weights = scores[n] * decay
            value = mm(weights.astype(bf16), grad_low)
            out = jnp.where(mine, value, out)
            weights_grad = mm_nt(left_parts(jnp.where(mine, scaled, 0.0)), grad_parts)
            scores_grad[n] += decay * weights_grad
            flow = mm(jnp.concatenate(split(weights * weights_grad), axis=1), from_row)
            rate_rows_ref[0, h : h + 1, here] = jnp.sum(jnp.where(r < c, flow, 0.0), axis=0, keepdims=True)
        scaled_grad_ref[here, :] = out

    @pl.when(i == pl.num_programs(0) - 1)
    def _():
        for n in range(chunks):
            here = pl.ds(n * CH, CH)
            same = marks_ref[here, M_SEG : M_SEG + 1] == seg_ref[0:1, here]
            total = jnp.where((r <= c) & same, scores_grad[n], 0.0)
            b_grad_ref[here, :] = precise_mm(total, c_ref[here, :])
            c_grad_ref[here, :] = precise_mm(total.T, b_ref[here, :])


def intra_backward(out_grad, conv, cum, rate, cum_rows, marks, seg_row, head_size, held=()):
    rows, inner = out_grad.shape
    pairs = inner // LANES
    chunks = rows // CH
    block = pl.BlockSpec((rows, LANES), lambda i: (0, i))
    heads = pl.BlockSpec((1, 8, rows), lambda i: (i, 0, 0))
    return call(
        partial(intra_backward_kernel, head_size, chunks),
        held,
        grid=(pairs,),
        in_specs=[
            block, block, pl.BlockSpec((rows, LANES), lambda i: (0, pairs)),
            pl.BlockSpec((rows, LANES), lambda i: (0, pairs + 1)), block, block, heads,
            whole((rows, LANES)), whole((8, rows)),
        ],
        out_specs=[block, heads, whole((rows, N)), whole((rows, N))],
        out_shape=[
            jax.ShapeDtypeStruct((rows, inner), f32),
            jax.ShapeDtypeStruct((pairs, 8, rows), f32),
            jax.ShapeDtypeStruct((rows, N), f32),
            jax.ShapeDtypeStruct((rows, N), f32),
        ],
        scratch_shapes=[pltpu.VMEM((chunks, CH, CH), f32), pltpu.VMEM((chunks, CH, CH), f32)],
        compiler_params=params(),
        cost_estimate=cost(3),
        name="intra_backward",
    )(out_grad, conv, conv, conv, cum, rate, cum_rows, marks, seg_row)


def scan_backward_kernel(
    head_size, rows, pairs, out_grad_ref, scaled_grad_ref, conv_ref, b_ref, c_ref, cum_ref, rate_ref, rate_rows_ref, step_rows_ref,
    entering_ref, pulled_ref, after_ref, skip_ref, decay_ref, b_intra_ref, c_intra_ref, pre_ref, halo_ref, taps_ref, marks_ref,
    conv_grad_ref, taps_grad_ref, step_grad_ref, log_grad_ref, bias_grad_ref,
    padded, b_total, c_total, current, head_sums, wide_marks,
):
    i = pl.program_id(0)
    chunks = rows // CH
    fill_padded(padded, halo_ref, pre_ref, rows)

    per = LANES // head_size

    @pl.when(i == 0)
    def _():
        b_total[...] = b_intra_ref[...]
        c_total[...] = c_intra_ref[...]
        head_sums[...] = jnp.zeros(head_sums.shape, f32)
        spread_marks(wide_marks, marks_ref, M_FWD)

    @pl.when(i < pairs)
    def _():
        after = after_ref[...]
        row, lane = iota2((6 * LANES, LANES))
        quantity = (row // LANES) % 3
        selector = (lane == 8 * i + per * quantity + (row % LANES) // head_size).astype(bf16)
        last_row = lax.broadcasted_iota(jnp.int32, (CH, LANES), 0) == CH - 1
        for n in reversed(range(chunks)):
            here = pl.ds(n * CH, CH)
            last = (n + 1) * CH - 1
            mark_enter = marks_ref[here, M_ENTER : M_ENTER + 1]
            mark_leave = marks_ref[here, M_LEAVE : M_LEAVE + 1]
            cum = cum_ref[here, :]
            enter = jnp.exp(cum) * mark_enter
            leave = jnp.exp(cum_ref[last : last + 1, :] - cum) * mark_leave
            conv = conv_ref[here, :]
            rate = rate_ref[here, :]
            scaled = rate * conv
            out_grad = out_grad_ref[here, :]
            state = entering_ref[n]
            left = leave * precise_mm(b_ref[here, :], after)
            scaled_grad = scaled_grad_ref[here, :] + left
            b_total[here, :] += precise_nt(scaled * leave, after)
            entered = out_grad * enter
            c_total[here, :] += precise_nt(entered, state)
            kept = enter[CH - 1 : CH, :]
            through = jnp.sum(kept * (state * after), axis=0, keepdims=True)
            came = entered * precise_mm(c_ref[here, :], state) + jnp.where(last_row, through, 0.0)
            parts = [split(value) for value in (came, scaled * left, conv * scaled_grad)]
            stacked = jnp.concatenate([high for high, _ in parts] + [low for _, low in parts], axis=1)
            head_sums[here, :] += mm(stacked, selector)
            current[here, :] = rate * scaled_grad + skip_ref[...] * out_grad
            after = kept * after + pulled_ref[n]

    @pl.when(i == pairs)
    def _():
        current[...] = b_total[...]
        r, c = iota2((CH, CH))
        from_row = (r >= c).astype(bf16)
        before = (r < c).astype(bf16)
        totals = [(jnp.zeros((per, 1), f32), jnp.zeros((per, 1), f32)) for _ in range(pairs)]
        for n in range(chunks):
            here = pl.ds(n * CH, CH)
            turned = head_sums[here, :].T
            came, gone = times_mask(turned, from_row), times_mask(turned, before)
            for j in range(pairs):
                first = 8 * j
                log_rate_grad = (
                    rate_rows_ref[j, 0:per, here] + came[first : first + per] + gone[first + per : first + 2 * per]
                )
                direct = turned[first + 2 * per : first + 3 * per]
                shifted = step_rows_ref[j, 0:per, here]
                decay = decay_ref[j, 0:per, 0:1]
                step_grad = (direct + log_rate_grad * decay) * sigmoid(shifted)
                step_grad_ref[j, 0:per, here] = step_grad
                log_total, bias_total = totals[j]
                totals[j] = (
                    log_total + jnp.sum(log_rate_grad * softplus(shifted), axis=1, keepdims=True) * decay,
                    bias_total + jnp.sum(step_grad, axis=1, keepdims=True),
                )
        for j, (log_total, bias_total) in enumerate(totals):
            log_grad_ref[j, 0:per, :] = jnp.broadcast_to(log_total, (per, LANES))
            bias_grad_ref[j, 0:per, :] = jnp.broadcast_to(bias_total, (per, LANES))

    @pl.when(i == pairs + 1)
    def _():
        current[...] = c_total[...]

    sums = [jnp.zeros((1, LANES), f32) for _ in range(KC + 1)]
    for start in range(0, rows, TILE):
        value = conv_tile(padded, taps_ref, wide_marks, start, TILE)
        sig = sigmoid(value)
        grad = current[pl.ds(start, TILE), :] * (sig * (1.0 + value * (1.0 - sig)))
        conv_grad_ref[pl.ds(start, TILE), :] = grad
        for k in range(KC):
            shifted = padded[pl.ds(start + HALO - KC + 1 + k, TILE), :]
            if k < KC - 1:
                shifted = shifted * wide_marks[k, pl.ds(start, TILE), :]
            sums[k] = sums[k] + jnp.sum(grad * shifted, axis=0, keepdims=True)
        sums[KC] = sums[KC] + jnp.sum(grad, axis=0, keepdims=True)
    taps_grad_ref[...] = jnp.concatenate(sums + [jnp.zeros((8 - KC - 1, LANES), f32)], axis=0)


def scan_backward(
    out_grad, scaled_grad, conv, cum, rate, rate_rows, step_rows, entering, pulled, after, skip, decay_rows,
    b_intra, c_intra, pre, halo, taps, marks, head_size, held=(),
):
    rows, inner = out_grad.shape
    mixed = pre.shape[1]
    pairs = inner // LANES
    chunks = rows // CH
    steps = pairs + 2
    own = lambda i: jnp.minimum(i, pairs - 1)
    block = pl.BlockSpec((rows, LANES), lambda i: (0, own(i)))
    column = lambda i: (0, i)
    heads, few = whole((pairs, 8, rows)), whole((pairs, 8, LANES))
    states = pl.BlockSpec((chunks, N, LANES), lambda i: (0, 0, own(i)))
    return call(
        partial(scan_backward_kernel, head_size, rows, pairs),
        held,
        grid=(steps,),
        in_specs=[
            block, block, block, pl.BlockSpec((rows, LANES), lambda i: (0, pairs)),
            pl.BlockSpec((rows, LANES), lambda i: (0, pairs + 1)), block, block, heads, heads, states, states,
            pl.BlockSpec((N, LANES), lambda i: (0, own(i))), pl.BlockSpec((1, LANES), lambda i: (0, own(i))), few,
            whole((rows, N)), whole((rows, N)), pl.BlockSpec((rows, LANES), column), pl.BlockSpec((HALO, LANES), column),
            pl.BlockSpec((8, LANES), column), whole((rows, LANES)),
        ],
        out_specs=[pl.BlockSpec((rows, LANES), column), pl.BlockSpec((8, LANES), column), heads, few, few],
        out_shape=[
            jax.ShapeDtypeStruct((rows, mixed), f32),
            jax.ShapeDtypeStruct((8, mixed), f32),
            jax.ShapeDtypeStruct((pairs, 8, rows), f32),
            jax.ShapeDtypeStruct((pairs, 8, LANES), f32),
            jax.ShapeDtypeStruct((pairs, 8, LANES), f32),
        ],
        scratch_shapes=[
            pltpu.VMEM((rows + HALO, LANES), f32),
            pltpu.VMEM((rows, N), f32),
            pltpu.VMEM((rows, N), f32),
            pltpu.VMEM((rows, LANES), f32),
            pltpu.VMEM((rows, LANES), f32),
            pltpu.VMEM((KC - 1, rows, LANES), f32),
        ],
        compiler_params=params(),
        cost_estimate=cost(3),
        name="scan_backward",
    )(
        out_grad, scaled_grad, conv, conv, conv, cum, rate, rate_rows, step_rows, entering, pulled, after, skip, decay_rows,
        b_intra, c_intra, pre, halo, taps, marks,
    )


def conv_backward_kernel(
    rows, pairs, per, conv_grad_ref, next_ref, taps_ref, marks_ref, pre_ref, gate_dots_ref, step_grad_ref, step_rows_ref,
    bias_ref, out_ref, map_grad_ref, dots_ref, padded, products, wide_marks,
):
    i = pl.program_id(0)
    row = lax.broadcasted_iota(jnp.int32, (8, LANES), 0)

    @pl.when(i == 0)
    def _():
        dots_ref[...] = gate_dots_ref[...]
        products[...] = jnp.zeros(products.shape, f32)
        spread_marks(wide_marks, marks_ref, M_BWD)

    @pl.when(i > 0)
    def _():
        padded[pl.ds(0, rows), :] = conv_grad_ref[...]
        padded[pl.ds(rows, 8), :] = next_ref[...]
        for start in range(0, rows, TILE):
            total = taps_ref[KC - 1 : KC, :] * padded[pl.ds(start, TILE), :]
            for k in range(KC - 1):
                shifted = padded[pl.ds(start + KC - 1 - k, TILE), :]
                total = total + taps_ref[k : k + 1, :] * (
                    shifted * wide_marks[k, pl.ds(start, TILE), :]
                )
            out_ref[pl.ds(start, TILE), :] = total.astype(bf16)
            map_grad_ref[pl.ds(start, TILE), :] = total
            products[pl.ds(start, TILE), :] += total * pre_ref[pl.ds(start, TILE), :].astype(f32)

    @pl.when(i == 0)
    def _():
        grads = [step_grad_ref[j, 0:per, :] for j in range(pairs)]
        grads = jnp.concatenate(grads + [jnp.zeros((LANES - per * pairs, rows), f32)], axis=0)
        out_ref[...] = grads.T.astype(bf16)
        total = jnp.zeros((1, rows), f32)
        for j in range(pairs):
            total = total + jnp.sum(
                step_grad_ref[j, 0:per, :] * (step_rows_ref[j, 0:per, :] - bias_ref[j, 0:per, 0:1]), axis=0, keepdims=True
            )
        dots_ref[0:1, :] += total

    @pl.when(i == pl.num_programs(0) - 1)
    def _():
        dots_ref[...] += rows_of((row == 0).astype(bf16), products[...])


def conv_backward(conv_grad, next_grad, taps, marks, pre, gate_dots, step_grad, step_rows, bias_rows, head_size, held=()):
    rows, mixed = pre.shape
    pairs = (mixed - 2 * N) // LANES
    steps = pairs + 3
    column = lambda i: (0, jnp.clip(i - 1, 0, pairs + 1))
    return call(
        partial(conv_backward_kernel, rows, pairs, LANES // head_size),
        held,
        grid=(steps,),
        in_specs=[
            pl.BlockSpec((rows, LANES), column), pl.BlockSpec((8, LANES), column), pl.BlockSpec((8, LANES), column),
            whole((rows, LANES)), pl.BlockSpec((rows, LANES), column),
            whole((8, rows)),
            whole((pairs, 8, rows)), whole((pairs, 8, rows)), whole((pairs, 8, LANES)),
        ],
        out_specs=[
            pl.BlockSpec((rows, LANES), lambda i: (0, i)),
            pl.BlockSpec((rows, LANES), lambda i: (0, jnp.clip(i - pairs - 1, 0, 1))),
            whole((8, rows)),
        ],
        out_shape=[
            jax.ShapeDtypeStruct((rows, steps * LANES), bf16),
            jax.ShapeDtypeStruct((rows, 2 * N), f32),
            jax.ShapeDtypeStruct((8, rows), f32),
        ],
        scratch_shapes=[
            pltpu.VMEM((rows + 8, LANES), f32), pltpu.VMEM((rows, LANES), f32), pltpu.VMEM((KC - 1, rows, LANES), f32),
        ],
        compiler_params=params(32 * 1024 * 1024),
        cost_estimate=cost(6),
        name="conv_backward",
    )(conv_grad, next_grad, taps, marks, pre, gate_dots, step_grad, step_rows, bias_rows)


def join_kernel(count, width, index_ref, *refs):
    blocks, out_ref = refs[:count], refs[count]
    for n in range(count):
        start = pl.multiple_of((index_ref[0] ^ n) * width, LANES)
        out_ref[:, pl.ds(start, width)] = blocks[n][...].astype(out_ref.dtype)


def join(blocks, index, dtype, first_row, held=()):
    count = len(blocks)
    rows, width = blocks[0].shape
    rows -= first_row
    size = min(rows, 256)
    return call(
        partial(join_kernel, count, width),
        held,
        grid=(rows // size,),
        in_specs=[pl.BlockSpec(memory_space=pltpu.SMEM)]
        + [pl.BlockSpec((size, width), lambda i: (i + first_row // size, 0))] * count,
        out_specs=pl.BlockSpec((size, count * width), lambda i: (i, 0)),
        out_shape=jax.ShapeDtypeStruct((rows, count * width), dtype),
        compiler_params=params(16 * 1024 * 1024),
        cost_estimate=cost(2),
        name="join",
    )(index, *blocks)


def join_norm_kernel(count, width, index_ref, gain_ref, *refs):
    blocks, normed_ref, scale_ref = refs[:count], refs[count], refs[count + 1]
    total = jnp.zeros((blocks[0].shape[0], 1), f32)
    for n in range(count):
        value = blocks[n][...].astype(f32)
        total = total + jnp.sum(value * value, axis=1, keepdims=True)
    scale = lax.rsqrt(total / (count * width) + epsilon)
    scale_ref[...] = jnp.broadcast_to(scale, scale_ref.shape)
    for n in range(count):
        here = pl.ds(pl.multiple_of((index_ref[0] ^ n) * width, LANES), width)
        normed_ref[:, here] = (blocks[n][...].astype(f32) * scale * gain_ref[:, here]).astype(bf16)


def join_norm(blocks, index, gain, rows, held=()):
    count = len(blocks)
    width = blocks[0].shape[1]
    size = 128
    block = pl.BlockSpec((size, width), lambda i: (i, 0))
    return call(
        partial(join_norm_kernel, count, width),
        held,
        grid=(rows // size,),
        in_specs=[pl.BlockSpec(memory_space=pltpu.SMEM), whole((1, count * width))] + [block] * count,
        out_specs=[
            pl.BlockSpec((size, count * width), lambda i: (i, 0)),
            pl.BlockSpec((size, LANES), lambda i: (i, 0)),
        ],
        out_shape=[
            jax.ShapeDtypeStruct((rows, count * width), bf16),
            jax.ShapeDtypeStruct((rows, LANES), f32),
        ],
        compiler_params=params(16 * 1024 * 1024),
        cost_estimate=cost(3),
        name="join_norm",
    )(index, gain, *blocks)


def input_side_kernel(count, width, own_ref, dots_ref, block_ref, grad_ref, scale_ref, gain_ref, *refs):
    sent, out_ref, norm_ref = refs[: count - 1], refs[count - 1], refs[count]
    normed_grad = own_ref[...]
    for piece in sent:
        normed_grad = normed_grad + piece[...].astype(f32)
    scale = scale_ref[:, 0:1]
    rows = scale.shape[0]
    mean = jnp.broadcast_to(dots_ref[0:1, :] / width, (LANES, rows)).T[:, 0:1]
    normed_x = block_ref[...].astype(f32) * scale
    grad = grad_ref[...].astype(f32) + scale * (gain_ref[...] * normed_grad - normed_x * mean)
    out_ref[...] = grad.astype(bf16)
    norm = jnp.sum(normed_grad * normed_x, axis=0, keepdims=True)

    @pl.when(pl.program_id(0) == 0)
    def _():
        norm_ref[...] = norm

    @pl.when(pl.program_id(0) > 0)
    def _():
        norm_ref[...] += norm


def input_gradient(own, sent, dots, block, grad, scale, gain, width, held=()):
    rows, cols = own.shape
    size = 128
    part = pl.BlockSpec((size, cols), lambda i: (i, 0))
    return call(
        partial(input_side_kernel, len(sent) + 1, float(width)),
        held,
        grid=(rows // size,),
        in_specs=[
            part, pl.BlockSpec((8, size), lambda i: (0, i)), part, part, pl.BlockSpec((size, LANES), lambda i: (i, 0)),
            whole((1, cols)),
        ]
        + [part] * len(sent),
        out_specs=[part, whole((1, cols))],
        out_shape=[jax.ShapeDtypeStruct((rows, cols), bf16), jax.ShapeDtypeStruct((1, cols), f32)],
        compiler_params=params(16 * 1024 * 1024),
        cost_estimate=cost(3),
        name="input_gradient",
    )(own, dots, block, grad, scale, gain, *sent)


def join_micro_kernel(count, width, held, places_ref, *refs):
    out_ref, refs = refs[-1], refs[held:]
    for n in range(count):
        start = pl.multiple_of((places_ref[0] ^ n) * width, LANES)
        out_ref[:, pl.ds(start, width)] = refs[n][...].astype(out_ref.dtype)


def join_micro(places, blocks, dtype, held=()):
    count = len(blocks)
    rows, width = blocks[0].shape
    size = rows // 4
    return pl.pallas_call(
        partial(join_micro_kernel, count, width, len(held)),
        grid_spec=pltpu.PrefetchScalarGridSpec(
            num_scalar_prefetch=1,
            grid=(4,),
            in_specs=[pl.BlockSpec(memory_space=pl.ANY)] * len(held)
            + [pl.BlockSpec((size, width), lambda i, places: (i, 0))] * count,
            out_specs=pl.BlockSpec((size, count * width), lambda i, places: (places[1] ^ i, 0)),
        ),
        out_shape=jax.ShapeDtypeStruct((rows, count * width), dtype),
        compiler_params=params(16 * 1024 * 1024),
        cost_estimate=cost(5),
        name="join_micro",
    )(places, *held, *blocks)


def join_gathered_kernel(count, width, held, places_ref, *refs):
    out_ref, blocks_ref = refs[-1], refs[held]
    for n in range(count):
        out_ref[:, n * width : (n + 1) * width] = blocks_ref[n].astype(out_ref.dtype)


def join_gathered(places, blocks, dtype, held=()):
    count, rows, width = blocks.shape
    size = rows // 4
    return pl.pallas_call(
        partial(join_gathered_kernel, count, width, len(held)),
        grid_spec=pltpu.PrefetchScalarGridSpec(
            num_scalar_prefetch=1,
            grid=(4,),
            in_specs=[pl.BlockSpec(memory_space=pl.ANY)] * len(held)
            + [pl.BlockSpec((count, size, width), lambda i, places: (0, i, 0))],
            out_specs=pl.BlockSpec((size, count * width), lambda i, places: (places[1] ^ i, 0)),
        ),
        out_shape=jax.ShapeDtypeStruct((rows, count * width), dtype),
        compiler_params=params(),
        cost_estimate=cost(5),
        name="join_gathered",
    )(places, *held, blocks)


def place_maps_kernel(count, places_ref, term_ref, normed_ref, *refs):
    pieces, out_ref = refs[:count], refs[count]
    rows = pieces[0].shape[0]
    total = jnp.zeros(out_ref.shape, f32)
    for n in range(count):
        here = pl.ds(pl.multiple_of((places_ref[0] ^ n) * rows, 16), rows)
        total = total + mm_tn(normed_ref[here, :], pieces[n][...])
    out_ref[...] = total.astype(bf16)


def place_maps(index, term, normed, pieces, first_column):
    count = len(pieces)
    rows, width = pieces[0].shape
    depth = normed.shape[1]
    return pl.pallas_call(
        partial(place_maps_kernel, count),
        grid=(width // LANES,),
        in_specs=[pl.BlockSpec(memory_space=pltpu.SMEM), pl.BlockSpec(memory_space=pl.ANY), whole(normed.shape)]
        + [pl.BlockSpec((rows, LANES), lambda i: (0, i))] * count,
        out_specs=pl.BlockSpec((depth, LANES), lambda i: (0, i + first_column // LANES)),
        out_shape=jax.ShapeDtypeStruct(term.shape, term.dtype),
        input_output_aliases={1: 0},
        compiler_params=params(16 * 1024 * 1024),
        cost_estimate=cost(3),
        name="place_maps",
    )(index, term, normed, *pieces)


def from_behind(block, axis, distance):
    devices = range(lax.axis_size(axis))
    route = [(i - distance, i) for i in devices if i - distance in devices]
    return lax.ppermute(block, axis, route)


def prefix(value, axis, join, neutral, backward):
    count, mine = (lax.axis_size(axis), lax.axis_index(axis))
    pieces = jax.tree.map(lambda part: lax.all_gather(part, axis), value)
    if backward:
        pieces = jax.tree.map(lambda part: part[::-1], pieces)
        mine = count - 1 - mine
    total = jax.tree.map(
        lambda part, zero: jnp.full_like(part, 0) + jnp.asarray(zero, part.dtype), value, neutral
    )

    def hop(position, total):
        longer = join(total, jax.tree.map(lambda part: part[position], pieces))
        return jax.tree.map(lambda new, old: jnp.where(position < mine, new, old), longer, total)

    return lax.fori_loop(0, count - 1, hop, total)


def block_step(decay_rate, carried, inputs):
    state_now, seg_before = carried
    x_block, rate_block, b_block, c_block, seg_block = inputs
    cumulative = jnp.cumsum(rate_block * decay_rate[None, :], axis=0)
    width_block = seg_block.shape[0]
    row_index = lax.broadcasted_iota(jnp.int32, (width_block, width_block), 0)
    col_index = lax.broadcasted_iota(jnp.int32, (width_block, width_block), 1)
    within = (row_index >= col_index) & (seg_block[:, None] == seg_block[None, :])
    within_heads = within[:, :, None]
    spread = cumulative[:, None, :] - cumulative[None, :, :]
    decay = jnp.where(within_heads, jnp.exp(jnp.where(within_heads, spread, 0.0)), 0.0)
    scores = jnp.dot(c_block, b_block.T, precision=precise)
    weights = scores[:, :, None] * decay * rate_block[None, :, :]
    output = jnp.einsum("tsh,shp->thp", weights, x_block, precision=precise)
    entering = jnp.exp(cumulative) * (seg_block == seg_before)[:, None].astype(jnp.float32)
    output = output + entering[:, :, None] * jnp.einsum(
        "tn,hpn->thp", c_block, state_now, precision=precise
    )
    leaving = (
        jnp.exp(cumulative[-1][None, :] - cumulative)
        * (seg_block == seg_block[-1])[:, None].astype(jnp.float32)
        * rate_block
    )
    state_next = entering[-1][:, None, None] * state_now + jnp.einsum(
        "sh,shp,sn->hpn", leaving, x_block, b_block, precision=precise
    )
    return ((state_next, seg_block[-1]), output)


def scan_blocks(x_heads, step_rate, b_part, c_part, seg_own, decay_rate, state_start, seg_start):
    blocks = x_heads.shape[0] // CH

    def to_blocks(value):
        return value.reshape((blocks, CH) + value.shape[1:])

    stepper = jax.checkpoint(partial(block_step, decay_rate))
    final_carry, output = lax.scan(
        stepper,
        (state_start, seg_start),
        (
            to_blocks(x_heads),
            to_blocks(step_rate),
            to_blocks(b_part),
            to_blocks(c_part),
            to_blocks(seg_own),
        ),
    )
    return (output.reshape(x_heads.shape), final_carry[0])


def causal_conv(padded_in, kernel, offset, seg_padded):
    own_rows = padded_in.shape[0] - (KC - 1)
    current = seg_padded[KC - 1 :]
    summed = jnp.zeros((own_rows, padded_in.shape[1]), jnp.float32) + offset[None, :]
    for tap_index in range(KC):
        shifted = padded_in[tap_index : tap_index + own_rows]
        same_doc = (seg_padded[tap_index : tap_index + own_rows] == current).astype(jnp.float32)
        summed = summed + kernel[tap_index][None, :] * shifted * same_doc[:, None]
    return summed


def chain_combine(earlier, later):
    return (earlier[0] * later[0], earlier[1] * later[0][:, None, None] + later[1])


def project_in(layer_in, gain_row, zx_full, bc_full, dt_full):
    inputs_f = layer_in.astype(jnp.float32)
    in_scale = lax.rsqrt(jnp.mean(inputs_f * inputs_f, axis=1) + epsilon)
    normed = (inputs_f * in_scale[:, None] * gain_row[None, :]).astype(jnp.bfloat16)
    model_width = zx_full.shape[0]
    inner_local = zx_full.shape[2]
    joined = jnp.dot(
        normed, zx_full.reshape(model_width, 2 * inner_local), preferred_element_type=jnp.float32
    )
    bc_pre = jnp.dot(normed, bc_full, preferred_element_type=jnp.float32)
    mixed_pre = jnp.concatenate([joined[:, inner_local:], bc_pre], axis=1).astype(jnp.bfloat16)
    step_pre = jnp.dot(normed, dt_full, preferred_element_type=jnp.float32)
    return (inputs_f, in_scale, normed, joined[:, :inner_local], mixed_pre, step_pre)


def mixer_parts(padded_in, step_pre, kernel, offset, bias_row, log_rate, seg_padded, heads_local):
    own_rows = step_pre.shape[0]
    inner_local = padded_in.shape[1] - 2 * N
    head_size = inner_local // heads_local
    conv_out = jax.nn.silu(causal_conv(padded_in, kernel, offset, seg_padded))
    x_heads = conv_out[:, :inner_local].reshape(own_rows, heads_local, head_size)
    b_part = conv_out[:, inner_local : inner_local + N]
    c_part = conv_out[:, inner_local + N :]
    step_rate = jax.nn.softplus(step_pre + bias_row[None, :])
    decay_rate = -jnp.exp(log_rate)
    seg_own = seg_padded[KC - 1 :]
    seg_start = seg_padded[KC - 2]
    local_out, local_state = scan_blocks(
        x_heads,
        step_rate,
        b_part,
        c_part,
        seg_own,
        decay_rate,
        jnp.zeros((heads_local, head_size, N), jnp.float32),
        seg_start,
    )
    carried = jnp.exp(jnp.cumsum(step_rate * decay_rate[None, :], axis=0)) * (seg_own == seg_start)[
        :, None
    ].astype(jnp.float32)
    return (x_heads, c_part, local_out, local_state, carried)


def mixer_tail(parts, state_in, gate_pre, skip_row):
    x_heads, c_part, local_out, local_state, carried = parts
    own_rows = gate_pre.shape[0]
    ssm_out = (
        local_out
        + carried[:, :, None] * jnp.einsum("tn,hpn->thp", c_part, state_in, precision=precise)
        + skip_row[None, :, None] * x_heads
    )
    gate_act = jax.nn.silu(gate_pre)
    gated = ssm_out.reshape(own_rows, gate_pre.shape[1]) * gate_act
    state_out = carried[-1][:, None, None] * state_in + local_state
    return ((gated, state_out), (carried, c_part, gate_act))


def select_batch(array_in, chosen):
    return lax.dynamic_index_in_dim(array_in, chosen, 0, keepdims=False)


def store_batch(buffer, value, chosen, valid):
    return jnp.where(valid, lax.dynamic_update_index_in_dim(buffer, value, chosen, 0), buffer)


def body(
    tokens,
    cotangent,
    seg_ids,
    norm_gain,
    in_zx,
    in_bc,
    in_dt,
    conv_x,
    conv_xb,
    conv_bc,
    conv_bcb,
    dt_bias,
    a_log,
    skip_gain,
    gate_gain,
    out_w,
):
    section_index = lax.axis_index("section")
    ctx_index = lax.axis_index("ctx")
    tensor_index = lax.axis_index("tensor")
    section_count = lax.axis_size("section")
    tensor_count = lax.axis_size("tensor")
    batches = tokens.shape[0]
    token_rows = tokens.shape[1]
    model_width = tokens.shape[2]
    zx_full, bc_full, dt_full, out_full = (
        lax.all_gather(in_zx[0], "ctx", axis=0, tiled=True),
        lax.all_gather(in_bc[0], "ctx", axis=0, tiled=True),
        lax.all_gather(in_dt[0], "ctx", axis=0, tiled=True),
        lax.all_gather(out_w[0], "ctx", axis=1, tiled=True),
    )
    inner_local = zx_full.shape[2]
    heads_local = dt_full.shape[1]
    head_size = inner_local // heads_local
    mixed_width = inner_local + 2 * N
    gain_row = norm_gain[0].astype(jnp.float32)
    kernel = jnp.concatenate([conv_x[0], conv_bc[0]], axis=1).astype(jnp.float32)
    offset = jnp.concatenate([conv_xb[0], conv_bcb[0]]).astype(jnp.float32)
    bias_row = dt_bias[0]
    log_rate = a_log[0]
    skip_row = skip_gain[0]
    gate_row = gate_gain[0].astype(jnp.float32)
    seg_lead = jnp.full((batches, KC - 1), -1, jnp.int32)
    seg_all = jnp.concatenate([seg_lead, seg_ids], axis=1)
    seg_local = lax.dynamic_slice_in_dim(seg_all, ctx_index * token_rows, token_rows + KC - 1, 1)
    chain_start = (
        jnp.ones((heads_local,), jnp.float32),
        jnp.zeros((heads_local, head_size, N), jnp.float32),
    )
    kept_inputs = jnp.zeros((batches, token_rows, model_width), jnp.bfloat16)
    kept_states = jnp.zeros((batches, heads_local, head_size, N), jnp.float32)
    kept_scales = jnp.zeros((batches, token_rows), jnp.float32)
    kept_edges = jnp.zeros((batches, KC - 1, mixed_width), jnp.bfloat16)
    section_store = jnp.zeros((batches, token_rows, model_width), jnp.bfloat16)
    received = jnp.zeros((token_rows, model_width), jnp.bfloat16)
    for tick_number in range(batches + section_count - 1):
        batch_index = tick_number - section_index
        valid = (batch_index >= 0) & (batch_index < batches)
        chosen = jnp.clip(batch_index, 0, batches - 1)
        layer_in = jnp.where(section_index == 0, select_batch(tokens, chosen), received)
        seg_padded = select_batch(seg_local, chosen)
        inputs_f, in_scale, normed, gate_pre, mixed_pre, step_pre = project_in(
            layer_in, gain_row, zx_full, bc_full, dt_full
        )
        edge_rows = from_behind(mixed_pre[token_rows - (KC - 1) :], "ctx", 1)
        padded_in = jnp.concatenate([edge_rows, mixed_pre], axis=0).astype(jnp.float32)
        parts = mixer_parts(
            padded_in, step_pre, kernel, offset, bias_row, log_rate, seg_padded, heads_local
        )
        state_in = prefix((parts[4][-1], parts[3]), "ctx", chain_combine, chain_start, False)[1]
        gated = mixer_tail(parts, state_in, gate_pre, skip_row)[0][0]
        squares = lax.psum(jnp.sum(gated * gated, axis=1), "tensor")
        gate_scale = lax.rsqrt(squares / DI + epsilon)
        gate_normed = (gated * gate_scale[:, None] * gate_row[None, :]).astype(jnp.bfloat16)
        projected = lax.psum(
            jnp.dot(gate_normed, out_full, preferred_element_type=jnp.float32), "tensor"
        )
        layer_out = (inputs_f + projected).astype(jnp.bfloat16)
        kept_inputs = store_batch(kept_inputs, layer_in, chosen, valid)
        kept_states = store_batch(kept_states, state_in, chosen, valid)
        kept_scales = store_batch(kept_scales, gate_scale, chosen, valid)
        kept_edges = store_batch(kept_edges, edge_rows, chosen, valid)
        section_store = store_batch(section_store, layer_out, chosen, valid)
        received = from_behind(layer_out, "section", 1)
    acc_zx = jnp.zeros((model_width, 2 * inner_local), jnp.float32)
    acc_dt = jnp.zeros((model_width, heads_local), jnp.float32)
    acc_out = jnp.zeros((inner_local, model_width), jnp.float32)
    acc_bc = jnp.zeros((model_width, 2 * N), jnp.float32)
    acc_gain = jnp.zeros((model_width,), jnp.float32)
    acc_kernel = jnp.zeros((KC, mixed_width), jnp.float32)
    acc_offset = jnp.zeros((mixed_width,), jnp.float32)
    acc_bias = jnp.zeros((heads_local,), jnp.float32)
    acc_log = jnp.zeros((heads_local,), jnp.float32)
    acc_skip = jnp.zeros((heads_local,), jnp.float32)
    acc_gate = jnp.zeros((inner_local,), jnp.float32)
    grad_store = jnp.zeros((batches, token_rows, model_width), jnp.float32)
    received_grad = jnp.zeros((token_rows, model_width), jnp.bfloat16)
    last_section = section_count - 1
    contract = (((0,), (0,)), ((), ()))
    for tick_number in range(batches + section_count - 1):
        batch_index = batches - 1 - tick_number + (last_section - section_index)
        valid = (batch_index >= 0) & (batch_index < batches)
        chosen = jnp.clip(batch_index, 0, batches - 1)
        out_grad = jnp.where(
            section_index == last_section, select_batch(cotangent, chosen), received_grad
        )
        seg_padded = select_batch(seg_local, chosen)
        inputs_f, in_scale, normed, gate_pre, mixed_pre, step_pre = project_in(
            select_batch(kept_inputs, chosen), gain_row, zx_full, bc_full, dt_full
        )
        padded_in = jnp.concatenate([select_batch(kept_edges, chosen), mixed_pre], axis=0).astype(
            jnp.float32
        )
        state_in = select_batch(kept_states, chosen)
        gate_scale = select_batch(kept_scales, chosen)

        def local_mixer(
            padded_arg,
            gate_arg,
            step_arg,
            state_arg,
            kernel_arg,
            offset_arg,
            bias_arg,
            log_arg,
            skip_arg,
        ):
            return mixer_tail(
                mixer_parts(
                    padded_arg,
                    step_arg,
                    kernel_arg,
                    offset_arg,
                    bias_arg,
                    log_arg,
                    seg_padded,
                    heads_local,
                ),
                state_arg,
                gate_arg,
                skip_arg,
            )

        outputs, pullback, extras = jax.vjp(
            local_mixer,
            padded_in,
            gate_pre,
            step_pre,
            state_in,
            kernel,
            offset,
            bias_row,
            log_rate,
            skip_row,
            has_aux=True,
        )
        gated = outputs[0]
        carried, c_part, gate_act = extras
        gate_normed = (gated * gate_scale[:, None] * gate_row[None, :]).astype(jnp.bfloat16)
        normed_gate_grad = jnp.dot(out_grad, out_full.T, preferred_element_type=jnp.float32)
        out_term = lax.dot_general(
            gate_normed, out_grad, contract, preferred_element_type=jnp.float32
        )
        gate_term = jnp.sum(normed_gate_grad * gated * gate_scale[:, None], axis=0)
        projection = lax.psum(
            jnp.sum(normed_gate_grad * gate_row[None, :] * gated, axis=1), "tensor"
        )
        gated_grad = (
            gate_scale[:, None] * gate_row[None, :] * normed_gate_grad
            - gated * (gate_scale**3 * projection / DI)[:, None]
        )
        out_heads = (gated_grad * gate_act).reshape(token_rows, heads_local, head_size)
        pull_state = jnp.einsum("th,thp,tn->hpn", carried, out_heads, c_part, precision=precise)
        state_after = prefix((carried[-1], pull_state), "ctx", chain_combine, chain_start, True)[1]
        (
            padded_grad,
            gate_grad,
            step_grad,
            unused_state,
            kernel_grad,
            offset_grad,
            bias_grad,
            log_grad,
            skip_grad,
        ) = pullback((gated_grad, state_after))
        edge_grad = from_behind(padded_grad[: KC - 1], "ctx", -1)
        mixed_grad = padded_grad[KC - 1 :].at[token_rows - (KC - 1) :].add(edge_grad)
        zx_grad = jnp.concatenate(
            [gate_grad.astype(jnp.bfloat16), mixed_grad[:, :inner_local].astype(jnp.bfloat16)],
            axis=1,
        )
        bc_grad = mixed_grad[:, inner_local:]
        step_low = step_grad.astype(jnp.bfloat16)
        normed_grad = jnp.dot(
            zx_grad,
            zx_full.reshape(model_width, 2 * inner_local).T,
            preferred_element_type=jnp.float32,
        )
        normed_grad = normed_grad + jnp.dot(step_low, dt_full.T, preferred_element_type=jnp.float32)
        normed_grad = normed_grad + jnp.dot(
            bc_grad, bc_full.astype(jnp.float32).T, precision=precise
        )
        zx_term = lax.dot_general(normed, zx_grad, contract, preferred_element_type=jnp.float32)
        dt_term = lax.dot_general(normed, step_low, contract, preferred_element_type=jnp.float32)
        bc_term = lax.dot_general(normed.astype(jnp.float32), bc_grad, contract, precision=precise)
        normed_grad = lax.psum(normed_grad.astype(jnp.bfloat16), "tensor").astype(jnp.float32)
        normed_x = inputs_f * in_scale[:, None]
        weighted = gain_row[None, :] * normed_grad
        input_grad = out_grad.astype(jnp.float32) + in_scale[:, None] * (
            weighted - normed_x * jnp.mean(weighted * normed_x, axis=1)[:, None]
        )
        norm_term = jnp.sum(normed_grad * normed_x, axis=0)
        sent_grad = input_grad.astype(jnp.bfloat16)
        grad_store = store_batch(
            grad_store,
            jnp.where(section_index == 0, input_grad, sent_grad.astype(jnp.float32)),
            chosen,
            valid,
        )
        acc_zx = jnp.where(valid, acc_zx + zx_term, acc_zx)
        acc_dt = jnp.where(valid, acc_dt + dt_term, acc_dt)
        acc_out = jnp.where(valid, acc_out + out_term, acc_out)
        acc_bc = jnp.where(valid, acc_bc + bc_term, acc_bc)
        acc_gain = jnp.where(valid, acc_gain + norm_term, acc_gain)
        acc_kernel = jnp.where(valid, acc_kernel + kernel_grad, acc_kernel)
        acc_offset = jnp.where(valid, acc_offset + offset_grad, acc_offset)
        acc_bias = jnp.where(valid, acc_bias + bias_grad, acc_bias)
        acc_log = jnp.where(valid, acc_log + log_grad, acc_log)
        acc_skip = jnp.where(valid, acc_skip + skip_grad, acc_skip)
        acc_gate = jnp.where(valid, acc_gate + gate_term, acc_gate)
        received_grad = from_behind(sent_grad, "section", -1)
    zx_sum, dt_sum, out_sum = (
        lax.psum_scatter(
            acc_zx.reshape(model_width, 2, inner_local).astype(jnp.bfloat16),
            "ctx",
            scatter_dimension=0,
            tiled=True,
        ).astype(jnp.float32),
        lax.psum_scatter(
            acc_dt.astype(jnp.bfloat16), "ctx", scatter_dimension=0, tiled=True
        ).astype(jnp.float32),
        lax.psum_scatter(
            acc_out.astype(jnp.bfloat16), "ctx", scatter_dimension=1, tiled=True
        ).astype(jnp.float32),
    )
    first_tensor = (tensor_index == 0).astype(jnp.float32)

    def widen(piece):
        full_shape = piece.shape[:-1] + (piece.shape[-1] * tensor_count,)
        return lax.dynamic_update_slice_in_dim(
            jnp.zeros(full_shape, jnp.float32),
            piece,
            tensor_index * piece.shape[-1],
            piece.ndim - 1,
        )

    def narrow(full_array):
        own_width = full_array.shape[-1] // tensor_count
        return lax.dynamic_slice_in_dim(
            full_array, tensor_index * own_width, own_width, full_array.ndim - 1
        )

    sums = lax.psum(
        (
            acc_bc,
            acc_gain * first_tensor,
            acc_kernel[:, inner_local:],
            acc_offset[inner_local:],
            widen(acc_kernel[:, :inner_local]),
            widen(acc_offset[:inner_local]),
            widen(acc_bias),
            widen(acc_log),
            widen(acc_skip),
            widen(acc_gate),
        ),
        ("ctx", "tensor"),
    )
    rows_own = in_bc.shape[1]
    bc_rows = lax.dynamic_slice_in_dim(sums[0], ctx_index * rows_own, rows_own, 0)
    return (
        section_store[None],
        grad_store[None],
        sums[1][None],
        zx_sum[None],
        bc_rows[None],
        dt_sum[None],
        narrow(sums[4])[None],
        narrow(sums[5])[None],
        sums[2][None],
        sums[3][None],
        narrow(sums[6])[None],
        narrow(sums[7])[None],
        narrow(sums[8])[None],
        narrow(sums[9])[None],
        out_sum[None],
    )


def swap_section(value):
    return lax.ppermute(value, "section", [(0, 1), (1, 0)])


def from_partner(value, distance):
    count = lax.axis_size("tensor")
    return lax.ppermute(value, "tensor", [(i, i ^ distance) for i in range(count)])


def with_partners(value):
    return [value] + [from_partner(value, k) for k in range(1, lax.axis_size("tensor"))]


def sum_over_tensor(value):
    return sum(with_partners(value)[1:], value)


def column_block(value, index, width):
    return lax.dynamic_slice_in_dim(value, index * width, width, value.ndim - 1)


def zero_of(value):
    return jnp.minimum(jnp.abs(value[(0,) * value.ndim].astype(f32)).astype(jnp.int32), 0)


def to_micro(value):
    section, ctx, tensor = (lax.axis_index(a) for a in ("section", "ctx", "tensor"))
    count = lax.axis_size("ctx")
    width = value.shape[2] // lax.axis_size("tensor")
    came = []
    for e in range(2):
        sent = 2 * section + ((ctx & 1) ^ e)
        piece = lax.dynamic_slice(value, (sent, 0, tensor * width), (1, value.shape[1], width))[0]
        route = [(s * count + c, (c >> 1) * count + 2 * s + ((c & 1) ^ e)) for s in range(2) for c in range(count)]
        came.append(lax.ppermute(piece, ("section", "ctx"), route))
    even = (ctx & 1) == 0
    return jnp.concatenate([jnp.where(even, came[0], came[1]), jnp.where(even, came[1], came[0])], axis=0)


def to_owners(blocks):
    section, ctx, count = lax.axis_index("section"), lax.axis_index("ctx"), lax.axis_size("ctx")
    rows = blocks[0].shape[0] // 2
    pieces = []
    for e in range(count):
        half, layer = (ctx ^ e) & 1, (ctx ^ e) >> 1
        piece = lax.dynamic_slice_in_dim(jnp.where(layer == 0, blocks[0], blocks[1]), half * rows, rows, 0)
        route = [
            (s * count + z, ((z ^ e) >> 1) * count + 2 * s + ((z ^ e) & 1)) for s in range(2) for z in range(count)
        ]
        pieces.append(lax.ppermute(piece, ("section", "ctx"), route))
    ordered = []
    for n in range(count):
        wanted = ctx ^ n
        e = ((wanted ^ ctx) & 1) | ((((wanted >> 1) ^ section) & 1) << 1)
        chosen = pieces[count - 1]
        for k in range(count - 1):
            chosen = jnp.where(e == k, pieces[k], chosen)
        ordered.append(chosen)
    return jnp.concatenate(ordered, axis=0)


def in_halves(own, section):
    half = own.shape[0] // 2
    keep = lax.dynamic_slice_in_dim(own, section * half, half, 0)
    came = swap_section(lax.dynamic_slice_in_dim(own, (1 - section) * half, half, 0))
    return [jnp.where(section == layer, keep, came) for layer in range(2)]


def own_layer(halves, section):
    keep = jnp.where(section == 0, halves[0], halves[1])
    came = swap_section(jnp.where(section == 0, halves[1], halves[0]))
    return jnp.concatenate([jnp.where(section == 0, keep, came), jnp.where(section == 0, came, keep)], axis=0)


def token_marks(seg_around, rows):
    own = seg_around[HALO : HALO + rows]
    columns = [seg_around[HALO - KC + 1 + k : HALO - KC + 1 + k + rows] == own for k in range(KC)]
    columns += [seg_around[HALO + KC - 1 - k : HALO + KC - 1 - k + rows] == own for k in range(KC)]
    chunks = rows // CH
    before = seg_around[HALO - 1 : HALO - 1 + rows].reshape(chunks, CH)[:, :1]
    last = own.reshape(chunks, CH)[:, -1:]
    columns.append((own.reshape(chunks, CH) == before).reshape(rows))
    columns.append((own.reshape(chunks, CH) == last).reshape(rows))
    columns = [column.astype(f32) for column in columns] + [own.astype(f32)]
    marks = jnp.pad(jnp.stack(columns, axis=1), ((0, 0), (0, LANES - len(columns))))
    return marks, jnp.broadcast_to(own.astype(f32)[None, :], (8, rows))


class Layer:
    pass


def lane_row(values):
    return jnp.pad(values, (0, LANES - values.shape[0]))[None, :]


def pair_rows(values, per):
    pairs = values.shape[0] // per
    padded = jnp.pad(values.reshape(pairs, per), ((0, 0), (0, 8 - per)))
    return jnp.broadcast_to(padded[:, :, None], (pairs, 8, LANES))


def from_pairs(values, per):
    return values[:, :per, 0].reshape(-1)


def unpack(pack, heads, head_size, inner, width):
    layer = Layer()
    layer.taps = jnp.concatenate([pack[: KC + 1, : inner + 2 * N], jnp.zeros((8 - KC - 1, inner + 2 * N), f32)], axis=0)
    layer.norm_gain = pack[KC + 1 : KC + 2, :width]
    layer.gate_gain = pack[KC + 2 : KC + 3, :inner]
    small = pack[KC + 3, : 3 * heads].reshape(3, heads)
    per = LANES // head_size
    decay = -jnp.exp(small[1])
    layer.bias_lanes, layer.decay_lanes = lane_row(small[0]), lane_row(decay)
    layer.bias_rows, layer.decay_rows = pair_rows(small[0], per), pair_rows(decay, per)
    layer.skip = jnp.repeat(small[2], head_size)[None, :]
    return layer


transposed = (((0,), (0,)), ((), ()))
across = (((1,), (1,)), ((), ()))


def project(layer, marks, seg_row, head_size, held=()):
    layer.pre = jnp.dot(layer.normed, layer.mix[:, LANES:], preferred_element_type=f32).astype(bf16)
    step = jnp.dot(layer.normed, layer.mix[:, :LANES], preferred_element_type=f32)
    layer.halo = lax.ppermute(layer.pre[-HALO:], "section", [(0, 1)])
    (layer.conv, layer.y, layer.own_state, last_state, layer.cum, layer.rate, layer.cum_rows, layer.step_rows) = scan_forward(
        layer.pre, layer.halo, layer.taps, marks, seg_row, step, layer.bias_lanes, layer.decay_lanes, head_size, held
    )
    layer.state_in = lax.ppermute(last_state, "section", [(0, 1)])


def gate(layer, marks, grad=None):
    layer.gate = jnp.dot(layer.normed, layer.gate_weight, preferred_element_type=f32)
    layer.ssm, layer.gained, layer.entering, sums = gate_forward(
        layer.y, layer.conv, layer.cum, marks, layer.own_state, layer.state_in, layer.gate, layer.skip, layer.gate_gain, grad
    )
    return sum_over_tensor(sums)


def gate_side(layer, grad, sums, marks, channels, held=()):
    (layer.out_grad, layer.gate_grad, layer.pulled, first, layer.gain_grad, layer.skip_grad, layer.gate_dots) = gate_backward(
        grad, layer.gate, layer.ssm, layer.conv, layer.cum, marks, sums, layer.gate_gain, channels, held
    )
    layer.after = lax.ppermute(first, "section", [(1, 0)])


def scan_side(layer, marks, seg_row, head_size, held_intra=(), held_scan=(), held_conv=(), after_intra=None, late_held=None):
    per = LANES // head_size
    scaled_grad, rate_rows, b_intra, c_intra = intra_backward(
        layer.out_grad, layer.conv, layer.cum, layer.rate, layer.cum_rows, marks, seg_row, head_size, held_intra
    )
    if after_intra is not None:
        held_conv = (*held_conv, *after_intra(rate_rows))
    conv_grad, layer.taps_grad, step_grad, log_grad, bias_grad = scan_backward(
        layer.out_grad, scaled_grad, layer.conv, layer.cum, layer.rate, rate_rows, layer.step_rows, layer.entering,
        layer.pulled, layer.after, layer.skip, layer.decay_rows, b_intra, c_intra, layer.pre, layer.halo,
        layer.taps, marks, head_size, held_scan,
    )
    next_grad = lax.ppermute(conv_grad[:8], "section", [(1, 0)])
    if late_held is not None:
        held_conv = (*held_conv, *late_held(conv_grad))
    layer.mix_grad, layer.map_grad, dots = conv_backward(
        conv_grad, next_grad, layer.taps, marks, layer.pre, layer.gate_dots, step_grad, layer.step_rows,
        layer.bias_rows, head_size, held_conv,
    )
    layer.dots = sum_over_tensor(dots)
    heads = layer.skip_grad.shape[1] // head_size
    layer.small = jnp.concatenate([
        from_pairs(bias_grad, per), from_pairs(log_grad, per), layer.skip_grad.reshape(heads, head_size).sum(axis=1)
    ])


def scatter_rows(term):
    return lax.psum_scatter(term, ("ctx", "section"), scatter_dimension=0, tiled=True)


def whole_micro_body(
    tokens, cotangent, seg_ids, norm_gain, in_zx, in_bc, in_dt, conv_x, conv_xb, conv_bc, conv_bcb, dt_bias, a_log,
    skip_gain, gate_gain, out_w,
):
    section, ctx, tensor = (lax.axis_index(a) for a in ("section", "ctx", "tensor"))
    tensors, ctxs = lax.axis_size("tensor"), lax.axis_size("ctx")
    width = tokens.shape[2]
    own_width = width // tensors
    inner = conv_x.shape[2]
    heads = dt_bias.shape[1]
    head_size = inner // heads
    mixed = inner + 2 * N
    channels = inner * tensors
    rows = seg_ids.shape[1] // 2
    index = tensor.astype(jnp.int32).reshape(1)

    def block_rows(weight, b):
        return lax.dynamic_slice_in_dim(weight, b * own_width, own_width, 0)

    def gather_rows(half):
        return lax.all_gather(half, ("ctx", "section"), axis=0, tiled=True)

    own_mix = jnp.concatenate([jnp.pad(in_dt[0], ((0, 0), (0, LANES - heads))), in_zx[0, :, 1], in_bc[0]], axis=1)
    mix_halves = in_halves(own_mix, section)
    mix_first = gather_rows(mix_halves[0])
    token_block = to_micro(tokens)
    rest_halves = in_halves(jnp.concatenate([in_zx[0, :, 0], out_w[0].T], axis=1), section)

    def line(values):
        return jnp.pad(values.astype(f32), (0, width - values.shape[0]))[None, :]

    own_pack = jnp.concatenate(
        [line(jnp.concatenate([conv_x[0, k], conv_bc[0, k]])) for k in range(KC)]
        + [
            line(jnp.concatenate([conv_xb[0], conv_bcb[0]])), line(norm_gain[0]), line(gate_gain[0]),
            line(jnp.concatenate([dt_bias[0], a_log[0], skip_gain[0]])),
        ],
        axis=0,
    )
    other_pack = swap_section(own_pack)
    first, second = (
        unpack(jnp.where(section == n, own_pack, other_pack), heads, head_size, inner, width) for n in range(2)
    )
    seg_mine = lax.dynamic_index_in_dim(seg_ids, ctx, 0, keepdims=False)
    seg_around = jnp.concatenate([jnp.full((HALO,), -1, jnp.int32), seg_mine, jnp.full((HALO,), -2, jnp.int32)])
    seg_around = lax.dynamic_slice_in_dim(seg_around, section * rows, rows + 2 * HALO, 0)
    marks, seg_row = token_marks(seg_around, rows)

    first.block = token_block
    first.gate_weight = gather_rows(ordered(rest_halves[0][:, :inner], token_block))
    first.normed, first.in_scale = join_norm(with_partners(first.block), index, first.norm_gain, rows)
    first.out_turned = gather_rows(ordered(rest_halves[0][:, inner:], first.normed))
    first.mix = mix_first
    project(first, marks, seg_row, head_size)
    second.mix = gather_rows(ordered(mix_halves[1], first.pre))
    rest_second = gather_rows(ordered(rest_halves[1], first.conv))
    second.gate_weight, second.out_turned = rest_second[:, :inner], rest_second[:, inner:]
    cot_block = to_micro(ordered(cotangent, first.pre))
    sums_first = gate(first, marks)

    def gate_low(layer, sums):
        layer.gated = (layer.gained * lax.rsqrt(sums[0] / channels + epsilon)[:, None]).astype(bf16)

    def blocks_of(total, dtype):
        parts = [column_block(total, tensor ^ n, own_width) for n in range(tensors)]
        return [parts[0]] + [part.astype(dtype) for part in parts[1:]]

    def out_terms(layer, dtype):
        return blocks_of(lax.dot_general(layer.gated, layer.out_turned, across, preferred_element_type=f32), dtype)

    gate_low(first, sums_first)
    terms = out_terms(first, f32)
    projected = sum([from_partner(terms[n], n) for n in range(1, tensors)], terms[0])
    second.block = (first.block.astype(f32) + projected).astype(bf16)

    second.normed, second.in_scale = join_norm(with_partners(second.block), index, second.norm_gain, rows)
    project(second, marks, seg_row, head_size)
    cot_full = join(with_partners(ordered(cot_block, second.pre)), index, bf16, 0)
    grad_second = jnp.dot(cot_full, second.out_turned, preferred_element_type=f32)
    sums_second = gate(second, marks, grad_second)

    def input_terms(layer):
        total = lax.dot_general(layer.gate_grad, layer.gate_weight, across, preferred_element_type=f32)
        total = total + lax.dot_general(layer.mix_grad, layer.mix, across, preferred_element_type=f32)
        rest = (layer.map_grad - layer.mix_grad[:, LANES + inner :].astype(f32)).astype(bf16)
        total = total + lax.dot_general(rest, layer.mix[:, LANES + inner :], across, preferred_element_type=f32)
        return blocks_of(total, bf16)

    def send_terms(layer, terms):
        return [from_partner(ordered(terms[n], layer.dots), n) for n in range(1, tensors)]

    def input_side(layer, own, sent, out_grad_block, held=()):
        return input_gradient(
            own, sent, layer.dots, layer.block, out_grad_block, layer.in_scale,
            column_block(layer.norm_gain, tensor, own_width), width, held,
        )

    def rest_term(layer, out_grad, *others):
        low = [
            lax.dot_general(layer.normed, ordered(layer.gate_grad, *others), transposed, preferred_element_type=f32).astype(bf16),
            lax.dot_general(out_grad, layer.gated, transposed, preferred_element_type=f32).astype(bf16),
        ]
        return jnp.concatenate(low, axis=1)

    def share(layer, *others):
        count = rows // tensors
        map_grad = ordered(layer.map_grad, *others)

        def part(b):
            return lax.dynamic_slice_in_dim(map_grad, b * count, count, 0)

        total = sum([from_partner(part(tensor ^ k), k) for k in range(1, tensors)], part(tensor))
        layer.map_share = total.astype(bf16)

    def mix_start(layer):
        return lax.dot_general(layer.normed, layer.mix_grad, transposed, preferred_element_type=f32).astype(bf16)

    def mix_term(layer, started, *others):
        pieces = [ordered(piece, *others) for piece in with_partners(layer.map_share)]
        return place_maps(index, started, layer.normed, pieces, LANES + inner)

    def small_pack(layer, norm_grad):
        def row(values):
            return jnp.pad(values, (0, mixed - values.shape[0]))[None, :]

        return jnp.concatenate(
            [layer.taps_grad, row(layer.gain_grad[0]), row(layer.small), row(norm_grad[0]), jnp.zeros((5, mixed), f32)], axis=0
        )

    gate_low(second, sums_second)
    out_second = lax.dot_general(second.gated, second.out_turned, across, preferred_element_type=f32).astype(bf16)
    result = lax.psum_scatter(out_second, "tensor", scatter_dimension=1, tiled=True)
    gate_side(second, grad_second, sums_second, marks, channels, (out_second,))
    rest_term_second = rest_term(second, cot_full)
    rest_sum_second = scatter_rows(rest_term_second)
    scan_side(second, marks, seg_row, head_size, held_scan=(rest_term_second,), held_conv=(result,))
    terms = input_terms(second)
    sent = send_terms(second, terms)
    middle_block, norm_second = input_side(second, terms[0], sent, cot_block)
    share(second, *sent)
    result = (second.block.astype(f32) + ordered(result, second.dots).astype(f32)).astype(bf16)
    output_pieces = to_owners([second.block, result])
    mix_started = mix_start(second)
    middle = join(with_partners(middle_block), index, bf16, 0, (mix_started, output_pieces))
    mix_term_second = mix_term(second, mix_started, rest_sum_second, middle)
    mix_sum_second = scatter_rows(mix_term_second)

    grad_first = jnp.dot(middle, first.out_turned, preferred_element_type=f32)
    crossed = jnp.sum(grad_first * first.gained, axis=1)
    crossed = sum_over_tensor(jnp.broadcast_to(crossed[None, :], (8, rows)))
    sums_first = jnp.concatenate([sums_first[:1], crossed[:1], sums_first[2:]], axis=0)
    gate_side(first, grad_first, sums_first, marks, channels)
    outputs = with_partners(ordered(output_pieces, first.out_grad))
    rest_terms = []

    def after_scan(conv_grad):
        rest_terms.append(rest_term(first, middle, conv_grad, *outputs[1:]))
        return rest_terms

    scan_side(
        first, marks, seg_row, head_size, held_intra=(mix_term_second,), held_conv=(rest_sum_second, mix_sum_second), late_held=after_scan,
    )
    rest_sum_first = scatter_rows(rest_terms[0])
    terms = input_terms(first)
    sent = send_terms(first, terms)
    share(first, first.dots)
    last_block, norm_first = input_side(first, terms[0], sent, middle_block)
    grad_pieces = to_owners([last_block, middle_block])
    grads = with_partners(grad_pieces)
    mix_sum_first = scatter_rows(mix_term(first, mix_start(first), rest_sum_first, grad_pieces))
    places = jnp.stack([tensor, ctx]).astype(jnp.int32)
    outputs = join_micro(places, outputs, bf16, (last_block,))

    rest_sum = own_layer([rest_sum_first, rest_sum_second], section).astype(f32)
    mix_sum = own_layer([mix_sum_first, mix_sum_second], section).astype(f32)
    bc_sum = mix_sum[:, LANES + inner :]
    pack_first, pack_second = ordered(small_pack(first, norm_first), grads[1]), small_pack(second, norm_second)
    pack = jnp.where(section == 0, pack_first, pack_second) + swap_section(
        jnp.where(section == 0, pack_second, pack_first)
    )
    pack = sum(
        [lax.ppermute(pack, "ctx", [(c, (c + d) % ctxs) for c in range(ctxs)]) for d in range(1, ctxs)], pack
    )
    shared = with_partners(jnp.concatenate([pack[:8, inner:], jnp.broadcast_to(pack[10:11, :own_width], (8, own_width))], axis=1))
    taps_bc = sum([piece[:, : 2 * N] for piece in shared[1:]], shared[0][:, : 2 * N])
    norm = join([piece[:, 2 * N :] for piece in shared], index, f32, 0)[0]
    small = pack[9, : 3 * heads].reshape(3, heads)
    zx_sum = jnp.stack([rest_sum[:, :inner], mix_sum[:, LANES : LANES + inner]], axis=1)
    out_sum = rest_sum[:, inner:].T
    input_grads = join_micro(places, grads, f32, (outputs,))
    return (
        outputs.reshape(1, ctxs, -1, width),
        input_grads.reshape(1, ctxs, -1, width),
        norm[None],
        zx_sum[None],
        bc_sum[None],
        mix_sum[:, :heads][None],
        pack[:KC, :inner][None],
        pack[KC, :inner][None],
        taps_bc[:KC][None],
        taps_bc[KC][None],
        small[0][None],
        small[1][None],
        small[2][None],
        pack[8, :inner][None],
        out_sum[None],
    )


def fits(shape, batches):
    return shape["ctx"] == batches == 4 and shape["section"] == 2 and shape["tensor"] & (shape["tensor"] - 1) == 0


def solution(mesh):
    def step(*args):
        chosen = whole_micro_body if fits(dict(mesh.shape), args[0].shape[0]) else body
        return jax.shard_map(
            chosen,
            mesh=mesh,
            in_specs=(
                P(None, "ctx", None),
                P(None, "ctx", None),
                P(),
                P("section", None),
                P("section", "ctx", None, "tensor"),
                P("section", "ctx", None),
                P("section", "ctx", "tensor"),
                P("section", None, "tensor"),
                P("section", "tensor"),
                P("section", None, None),
                P("section", None),
                P("section", "tensor"),
                P("section", "tensor"),
                P("section", "tensor"),
                P("section", "tensor"),
                P("section", "tensor", "ctx"),
            ),
            out_specs=(
                P("section", None, "ctx", None),
                P("section", None, "ctx", None),
                P("section", None),
                P("section", "ctx", None, "tensor"),
                P("section", "ctx", None),
                P("section", "ctx", "tensor"),
                P("section", None, "tensor"),
                P("section", "tensor"),
                P("section", None, None),
                P("section", None),
                P("section", "tensor"),
                P("section", "tensor"),
                P("section", "tensor"),
                P("section", "tensor"),
                P("section", "tensor", "ctx"),
            ),
            check_vma=False,
        )(*args)

    return step
```

```python
from functools import partial

import jax
import jax.numpy as jnp
from jax import lax
from jax.experimental import pallas as pl
from jax.experimental.pallas import tpu as pltpu
from jax.sharding import PartitionSpec as P

bf16 = jnp.bfloat16
f32 = jnp.float32
precise = lax.Precision.HIGHEST
epsilon = 1e-05
N = 128
KC = 4
CH = 256
DI = 3072
HALO = 16
LANES = 128
VMEM_BYTES = 60 * 1024 * 1024

M_FWD, M_BWD, M_ENTER, M_LEAVE, M_SEG = 0, 4, 8, 9, 10


def mm(a, b):
    return lax.dot_general(a, b, (((1,), (0,)), ((), ())), preferred_element_type=f32)


def mm_nt(a, b, precision=None):
    return lax.dot_general(a, b, (((1,), (1,)), ((), ())), preferred_element_type=f32, precision=precision)


def mm_tn(a, b):
    return lax.dot_general(a, b, (((0,), (0,)), ((), ())), preferred_element_type=f32)


def split(v):
    high = v.astype(bf16)
    return high, (v - high.astype(f32)).astype(bf16)


def rows_of(selector, values):
    high, low = split(values)
    return mm_nt(selector, high) + mm_nt(selector, low)


def times_mask(rows, mask):
    high, low = split(rows)
    return mm(high, mask) + mm(low, mask)


def left_parts(a):
    high, low = split(a)
    return jnp.concatenate([high, low, high], axis=1)


def right_parts(b, axis):
    high, low = split(b)
    return jnp.concatenate([high, high, low], axis=axis)


def thirds(v):
    high = v.astype(bf16)
    rest = v - high.astype(f32)
    middle = rest.astype(bf16)
    return high, middle, (rest - middle.astype(f32)).astype(bf16)


def left_exact(a):
    high, middle, low = thirds(a)
    return jnp.concatenate([high, middle, high, middle, low, high], axis=1)


def right_exact(b, axis):
    high, middle, low = thirds(b)
    return jnp.concatenate([high, high, middle, middle, high, low], axis=axis)


def precise_nt(a, b):
    return mm_nt(left_parts(a), right_parts(b, 1))


def precise_mm(a, b):
    return mm(left_parts(a), right_parts(b, 0))


def iota2(shape):
    return lax.broadcasted_iota(jnp.int32, shape, 0), lax.broadcasted_iota(jnp.int32, shape, 1)


def sigmoid(v):
    return 1.0 / (1.0 + jnp.exp(-v))


def softplus(v):
    return jnp.maximum(v, 0.0) + jnp.log1p(jnp.exp(-jnp.abs(v)))


def fill_padded(padded, halo_ref, pre_ref, rows):
    padded[pl.ds(0, HALO), :] = halo_ref[...].astype(f32)
    padded[pl.ds(HALO, rows), :] = pre_ref[...].astype(f32)


def spread_marks(wide, marks_ref, first):
    for k in range(KC - 1):
        wide[k] = jnp.broadcast_to(marks_ref[:, first + k : first + k + 1], wide.shape[1:])


def conv_tile(padded, taps_ref, marks, start, count):
    total = jnp.zeros((count, LANES), f32) + taps_ref[KC : KC + 1, :]
    for k in range(KC):
        shifted = padded[pl.ds(start + HALO - KC + 1 + k, count), :]
        if k == KC - 1:
            total = total + taps_ref[k : k + 1, :] * shifted
        else:
            total = total + taps_ref[k : k + 1, :] * (shifted * marks[k, pl.ds(start, count), :])
    return total


TILE = 128


def scan_forward_kernel(
    head_size, rows, pre_ref, halo_ref, taps_ref, marks_ref, seg_ref, step_ref, bias_ref, decay_ref,
    conv_ref, y_ref, own_state_ref, last_state_ref, cum_ref, rate_ref, cum_rows_ref, step_rows_ref,
    padded, b_all, b_turned, scores, cum_all, rate_all, step_all, cum_turned, step_turned, wide_marks,
):
    i = pl.program_id(0)
    chunks = rows // CH
    fill_padded(padded, halo_ref, pre_ref, rows)

    @pl.when(i == 0)
    def _():
        spread_marks(wide_marks, marks_ref, M_FWD)

    for start in range(0, rows, TILE):
        value = conv_tile(padded, taps_ref, wide_marks, start, TILE)
        conv_ref[pl.ds(start, TILE), :] = value / (1.0 + jnp.exp(-value))

    @pl.when(i == 0)
    def _():
        b_all[...] = conv_ref[...]
        b_turned[...] = conv_ref[...].T
        shifted = step_ref[...] + bias_ref[...]
        rate = softplus(shifted)
        step_all[...] = shifted
        rate_all[...] = rate
        r, c = iota2((CH, CH))
        tri = (r >= c).astype(f32)
        for n in range(chunks):
            part = rate[n * CH : (n + 1) * CH, :] * decay_ref[...]
            cum_all[pl.ds(n * CH, CH), :] = lax.dot_general(
                tri, part, (((1,), (0,)), ((), ())), preferred_element_type=f32, precision=precise
            )

    @pl.when(i == 1)
    def _():
        r, c = iota2((CH, CH))
        for n in range(chunks):
            here = pl.ds(n * CH, CH)
            same = marks_ref[here, M_SEG : M_SEG + 1] == seg_ref[0:1, here]
            value = mm_nt(left_exact(conv_ref[here, :]), right_exact(b_all[here, :], 1))
            scores[n] = jnp.where((r >= c) & same, value, 0.0)
        per = LANES // head_size
        for turned, values in ((cum_turned, cum_all), (step_turned, step_all)):
            rows_all = values[...].T
            for j in range(turned.shape[0]):
                turned[j, 0:per, :] = rows_all[per * j : per * (j + 1), :]

    @pl.when(i >= 2)
    def _():
        j = i - 2
        per = LANES // head_size
        row, lane = iota2((LANES, LANES))
        widen = (row == per * j + lane // head_size).astype(f32)
        cum = lax.dot_general(cum_all[...], widen, (((1,), (0,)), ((), ())), preferred_element_type=f32, precision=precise)
        rate = lax.dot_general(rate_all[...], widen, (((1,), (0,)), ((), ())), preferred_element_type=f32, precision=precise)
        cum_rows = cum_turned[j]
        cum_rows_ref[0] = cum_rows
        step_rows_ref[0] = step_turned[j]
        cum_ref[...] = cum
        rate_ref[...] = rate
        lane_c = lax.broadcasted_iota(jnp.int32, (CH, LANES), 1)
        states = []
        for n in range(chunks):
            here = pl.ds(n * CH, CH)
            span = slice(n * CH, (n + 1) * CH)
            scaled = rate[span] * conv_ref[here, :]
            out = jnp.zeros((CH, LANES), f32)
            for h in range(per):
                column = cum[span, h * head_size : h * head_size + 1]
                value = []
                for first, past in ((0, CH // 2), (CH // 2, CH)):
                    spread = column[first:past] - cum_rows[h : h + 1, n * CH : n * CH + past]
                    weights = scores[n, first:past, :past] * jnp.exp(jnp.minimum(spread, 0.0))
                    value.append(mm(left_exact(weights), right_exact(scaled[:past], 0)))
                value = jnp.concatenate(value, axis=0)
                out = value if per == 1 else jnp.where(lane_c // head_size == h, value, out)
            y_ref[here, :] = out
            leave = jnp.exp(cum[(n + 1) * CH - 1 : (n + 1) * CH, :] - cum[span]) * marks_ref[here, M_LEAVE : M_LEAVE + 1]
            state = mm(left_exact(b_turned[:, here]), right_exact(scaled * leave, 0))
            own_state_ref[n] = state
            states.append(state)
        total = states[0]
        for n in range(1, chunks):
            last = (n + 1) * CH - 1
            kept = jnp.exp(cum[last : last + 1, :]) * marks_ref[last : last + 1, M_ENTER : M_ENTER + 1]
            total = kept * total + states[n]
        last_state_ref[...] = total


def call(kernel, held, in_specs, **rest):
    count = len(held)

    def run(*refs):
        kernel(*refs[count:])

    made = pl.pallas_call(run, in_specs=[pl.BlockSpec(memory_space=pl.ANY)] * count + in_specs, **rest)
    return lambda *args: made(*held, *args)


def ordered(value, *others):
    anywhere = pl.BlockSpec(memory_space=pl.ANY)
    return pl.pallas_call(
        lambda *refs: None,
        in_specs=[anywhere] * (1 + len(others)),
        out_specs=anywhere,
        out_shape=jax.ShapeDtypeStruct(value.shape, value.dtype),
        input_output_aliases={0: 0},
        cost_estimate=cost(0),
        name="ordered",
    )(value, *others)


def whole(shape):
    return pl.BlockSpec(shape, lambda i: (0,) * len(shape))


def params(limit=VMEM_BYTES):
    return pltpu.CompilerParams(vmem_limit_bytes=limit, dimension_semantics=("arbitrary",))


def cost(microseconds):
    return pl.CostEstimate(flops=0, bytes_accessed=int(microseconds * 3e6), transcendentals=0)


def scan_forward(pre, halo, taps, marks, seg_row, step, bias, decay, head_size, held=()):
    rows, mixed = pre.shape
    inner = mixed - 2 * N
    pairs = inner // LANES
    chunks = rows // CH
    steps = pairs + 2
    column = lambda i: (0, (i + pairs) % steps)
    pair = lambda i: (0, jnp.maximum(i - 2, 0))
    return call(
        partial(scan_forward_kernel, head_size, rows),
        held,
        grid=(steps,),
        in_specs=[
            pl.BlockSpec((rows, LANES), column),
            pl.BlockSpec((HALO, LANES), column),
            pl.BlockSpec((8, LANES), column),
            whole((rows, LANES)),
            whole((8, rows)),
            whole((rows, LANES)),
            whole((1, LANES)),
            whole((1, LANES)),
        ],
        out_specs=[
            pl.BlockSpec((rows, LANES), column),
            pl.BlockSpec((rows, LANES), pair),
            pl.BlockSpec((chunks, N, LANES), lambda i: (0, 0, jnp.maximum(i - 2, 0))),
            pl.BlockSpec((N, LANES), pair),
            pl.BlockSpec((rows, LANES), pair),
            pl.BlockSpec((rows, LANES), pair),
            pl.BlockSpec((1, 8, rows), lambda i: (jnp.maximum(i - 2, 0), 0, 0)),
            pl.BlockSpec((1, 8, rows), lambda i: (jnp.maximum(i - 2, 0), 0, 0)),
        ],
        out_shape=[
            jax.ShapeDtypeStruct((rows, mixed), f32),
            jax.ShapeDtypeStruct((rows, inner), f32),
            jax.ShapeDtypeStruct((chunks, N, inner), f32),
            jax.ShapeDtypeStruct((N, inner), f32),
            jax.ShapeDtypeStruct((rows, inner), f32),
            jax.ShapeDtypeStruct((rows, inner), f32),
            jax.ShapeDtypeStruct((pairs, 8, rows), f32),
            jax.ShapeDtypeStruct((pairs, 8, rows), f32),
        ],
        scratch_shapes=[
            pltpu.VMEM((rows + HALO, LANES), f32),
            pltpu.VMEM((rows, LANES), f32),
            pltpu.VMEM((N, rows), f32),
            pltpu.VMEM((chunks, CH, CH), f32),
            pltpu.VMEM((rows, LANES), f32),
            pltpu.VMEM((rows, LANES), f32),
            pltpu.VMEM((rows, LANES), f32),
            pltpu.VMEM((pairs, 8, rows), f32),
            pltpu.VMEM((pairs, 8, rows), f32),
            pltpu.VMEM((KC - 1, rows, LANES), f32),
        ],
        compiler_params=params(),
        cost_estimate=cost(15),
        name="scan_forward",
    )(pre, halo, taps, marks, seg_row, step, bias, decay)


def gate_kernel(
    chunks, with_grad, y_ref, conv_ref, c_ref, cum_ref, marks_ref, own_state_ref, state_ref, gate_ref, skip_ref, gain_ref,
    *rest,
):
    if with_grad:
        grad_ref, ssm_ref, gated_ref, entering_ref, sums_ref, c_parts, squares, products = rest
    else:
        ssm_ref, gated_ref, entering_ref, sums_ref, c_parts, squares = rest
    i = pl.program_id(0)

    @pl.when(i == 0)
    def _():
        c_parts[...] = left_exact(c_ref[...])

    state = state_ref[...]
    for n in range(chunks):
        here = pl.ds(n * CH, CH)
        entering_ref[n] = state
        enter = jnp.exp(cum_ref[here, :]) * marks_ref[here, M_ENTER : M_ENTER + 1]
        ssm_ref[here, :] = (
            y_ref[here, :]
            + enter * mm(c_parts[here, :], right_exact(state, 0))
            + skip_ref[...] * conv_ref[here, :]
        )
        state = enter[CH - 1 : CH, :] * state + own_state_ref[n]
    gate = gate_ref[...]
    gated = ssm_ref[...] * (gate * sigmoid(gate))
    scaled = gated * gain_ref[...]
    gated_ref[...] = scaled
    totals = [(squares, gated * gated)] + ([(products, scaled * grad_ref[...])] if with_grad else [])

    @pl.when(i == 0)
    def _():
        for total, value in totals:
            total[...] = value

    @pl.when(i > 0)
    def _():
        for total, value in totals:
            total[...] += value

    @pl.when(i == pl.num_programs(0) - 1)
    def _():
        row = lax.broadcasted_iota(jnp.int32, (8, LANES), 0)
        sums = [rows_of((row == n).astype(bf16), total[...]) for n, (total, _) in enumerate(totals)]
        sums_ref[...] = sum(sums[1:], sums[0])


def gate_forward(y, conv, cum, marks, own_state, state_in, gate, skip, gain, grad=None, held=()):
    rows, inner = y.shape
    pairs = inner // LANES
    chunks = rows // CH
    block = pl.BlockSpec((rows, LANES), lambda i: (0, i))
    line = pl.BlockSpec((1, LANES), lambda i: (0, i))
    states = pl.BlockSpec((chunks, N, LANES), lambda i: (0, 0, i))
    last = conv.shape[1] // LANES - 1
    in_specs = [
        block, block, pl.BlockSpec((rows, LANES), lambda i: (0, last)), block, whole((rows, LANES)), states,
        pl.BlockSpec((N, LANES), lambda i: (0, i)), block, line, line,
    ]
    args = [y, conv, conv, cum, marks, own_state, state_in, gate, skip, gain]
    if grad is not None:
        in_specs.append(block)
        args.append(grad)
    return call(
        partial(gate_kernel, chunks, grad is not None),
        held,
        grid=(pairs,),
        in_specs=in_specs,
        out_specs=[block, block, states, whole((8, rows))],
        out_shape=[
            jax.ShapeDtypeStruct((rows, inner), f32),
            jax.ShapeDtypeStruct((rows, inner), f32),
            jax.ShapeDtypeStruct((chunks, N, inner), f32),
            jax.ShapeDtypeStruct((8, rows), f32),
        ],
        scratch_shapes=[pltpu.VMEM((rows, 6 * N), bf16)] + [pltpu.VMEM((rows, LANES), f32)] * (1 if grad is None else 2),
        compiler_params=params(48 * 1024 * 1024),
        cost_estimate=cost(6),
        name="gate_forward",
    )(*args)


def gate_backward_kernel(
    chunks, channels, grad_ref, gate_ref, ssm_ref, conv_ref, c_ref, cum_ref, marks_ref, sums_ref, gain_ref,
    out_grad_ref, gate_grad_ref, pulled_ref, first_ref, gain_grad_ref, skip_grad_ref, dots_ref,
    scale_all, shift_all, c_turned, products,
):
    i = pl.program_id(0)

    @pl.when(i == 0)
    def _():
        scale = lax.rsqrt(sums_ref[0:1, :] / channels + epsilon)
        shift = scale * scale * scale * sums_ref[1:2, :] / channels
        rows = scale.shape[1]
        scale_all[...] = jnp.broadcast_to(scale, (LANES, rows)).T
        shift_all[...] = jnp.broadcast_to(shift, (LANES, rows)).T
        for n in range(chunks):
            c_turned[n] = left_parts(c_ref[pl.ds(n * CH, CH), :].T)

    gate = gate_ref[...]
    sig = sigmoid(gate)
    act = gate * sig
    ssm = ssm_ref[...]
    gated = ssm * act
    grad = grad_ref[...]
    scale = scale_all[...]
    gated_grad = scale * gain_ref[...] * grad - gated * shift_all[...]
    gain_grad_ref[...] = jnp.sum(grad * gated * scale, axis=0, keepdims=True)
    out_grad = gated_grad * act
    out_grad_ref[...] = out_grad
    skip_grad_ref[...] = jnp.sum(out_grad * conv_ref[...], axis=0, keepdims=True)
    gate_grad = gated_grad * ssm * (sig * (1.0 + gate * (1.0 - sig)))
    gate_grad_ref[...] = gate_grad.astype(bf16)
    dots = gate_grad * gate
    kept = []
    for n in range(chunks):
        here = pl.ds(n * CH, CH)
        enter = jnp.exp(cum_ref[here, :]) * marks_ref[here, M_ENTER : M_ENTER + 1]
        pulled = mm(c_turned[n], right_parts(out_grad_ref[here, :] * enter, 0))
        pulled_ref[n] = pulled
        kept.append((enter[CH - 1 : CH, :], pulled))
    first = kept[-1][1]
    for last_enter, pulled in kept[-2::-1]:
        first = last_enter * first + pulled
    first_ref[...] = first

    @pl.when(i == 0)
    def _():
        products[...] = dots

    @pl.when(i > 0)
    def _():
        products[...] += dots

    @pl.when(i == pl.num_programs(0) - 1)
    def _():
        row = lax.broadcasted_iota(jnp.int32, (8, LANES), 0)
        dots_ref[...] = rows_of((row == 0).astype(bf16), products[...])


def gate_backward(grad, gate, ssm, conv, cum, marks, sums, gain, channels, held=()):
    rows, inner = ssm.shape
    pairs = inner // LANES
    chunks = rows // CH
    block = pl.BlockSpec((rows, LANES), lambda i: (0, i))
    line = pl.BlockSpec((1, LANES), lambda i: (0, i))
    states = pl.BlockSpec((chunks, N, LANES), lambda i: (0, 0, i))
    last = conv.shape[1] // LANES - 1
    return call(
        partial(gate_backward_kernel, chunks, float(channels)),
        held,
        grid=(pairs,),
        in_specs=[
            block, block, block, block, pl.BlockSpec((rows, LANES), lambda i: (0, last)), block,
            whole((rows, LANES)), whole((8, rows)), line,
        ],
        out_specs=[block, block, states, pl.BlockSpec((N, LANES), lambda i: (0, i)), line, line, whole((8, rows))],
        out_shape=[
            jax.ShapeDtypeStruct((rows, inner), f32),
            jax.ShapeDtypeStruct((rows, inner), bf16),
            jax.ShapeDtypeStruct((chunks, N, inner), f32),
            jax.ShapeDtypeStruct((N, inner), f32),
            jax.ShapeDtypeStruct((1, inner), f32),
            jax.ShapeDtypeStruct((1, inner), f32),
            jax.ShapeDtypeStruct((8, rows), f32),
        ],
        scratch_shapes=[
            pltpu.VMEM((rows, LANES), f32), pltpu.VMEM((rows, LANES), f32), pltpu.VMEM((chunks, N, 3 * CH), bf16),
            pltpu.VMEM((rows, LANES), f32),
        ],
        compiler_params=params(48 * 1024 * 1024),
        cost_estimate=cost(7),
        name="gate_backward",
    )(grad, gate, ssm, conv, conv, cum, marks, sums, gain)


def intra_backward_kernel(
    head_size, chunks, out_grad_ref, conv_ref, b_ref, c_ref, cum_ref, rate_ref, cum_rows_ref, marks_ref, seg_ref,
    scaled_grad_ref, rate_rows_ref, b_grad_ref, c_grad_ref,
    scores, scores_grad,
):
    i = pl.program_id(0)
    per = LANES // head_size
    r, c = iota2((CH, CH))

    @pl.when(i == 0)
    def _():
        for n in range(chunks):
            here = pl.ds(n * CH, CH)
            same = marks_ref[here, M_SEG : M_SEG + 1] == seg_ref[0:1, here]
            value = precise_nt(b_ref[here, :], c_ref[here, :])
            scores[n] = jnp.where((r <= c) & same, value, 0.0)
            scores_grad[n] = jnp.zeros((CH, CH), f32)

    from_row = (r >= c).astype(bf16)
    from_row = jnp.concatenate([from_row, from_row], axis=0)
    lane_c = lax.broadcasted_iota(jnp.int32, (CH, LANES), 1)
    rate_rows_ref[...] = jnp.zeros(rate_rows_ref.shape, f32)
    for n in range(chunks):
        here = pl.ds(n * CH, CH)
        scaled = rate_ref[here, :] * conv_ref[here, :]
        grad_parts = right_parts(out_grad_ref[here, :], 1)
        grad_low = grad_parts[:, :LANES]
        out = jnp.zeros((CH, LANES), f32)
        for h in range(per):
            mine = lane_c // head_size == h
            spread = cum_rows_ref[0, h : h + 1, here] - cum_ref[here, h * head_size : h * head_size + 1]
            decay = jnp.exp(jnp.minimum(spread, 0.0))
            weights = scores[n] * decay
            value = mm(weights.astype(bf16), grad_low)
            out = jnp.where(mine, value, out)
            weights_grad = mm_nt(left_parts(jnp.where(mine, scaled, 0.0)), grad_parts)
            scores_grad[n] += decay * weights_grad
            flow = mm(jnp.concatenate(split(weights * weights_grad), axis=1), from_row)
            rate_rows_ref[0, h : h + 1, here] = jnp.sum(jnp.where(r < c, flow, 0.0), axis=0, keepdims=True)
        scaled_grad_ref[here, :] = out

    @pl.when(i == pl.num_programs(0) - 1)
    def _():
        for n in range(chunks):
            here = pl.ds(n * CH, CH)
            same = marks_ref[here, M_SEG : M_SEG + 1] == seg_ref[0:1, here]
            total = jnp.where((r <= c) & same, scores_grad[n], 0.0)
            b_grad_ref[here, :] = precise_mm(total, c_ref[here, :])
            c_grad_ref[here, :] = precise_mm(total.T, b_ref[here, :])


def intra_backward(out_grad, conv, cum, rate, cum_rows, marks, seg_row, head_size, held=()):
    rows, inner = out_grad.shape
    pairs = inner // LANES
    chunks = rows // CH
    block = pl.BlockSpec((rows, LANES), lambda i: (0, i))
    heads = pl.BlockSpec((1, 8, rows), lambda i: (i, 0, 0))
    return call(
        partial(intra_backward_kernel, head_size, chunks),
        held,
        grid=(pairs,),
        in_specs=[
            block, block, pl.BlockSpec((rows, LANES), lambda i: (0, pairs)),
            pl.BlockSpec((rows, LANES), lambda i: (0, pairs + 1)), block, block, heads,
            whole((rows, LANES)), whole((8, rows)),
        ],
        out_specs=[block, heads, whole((rows, N)), whole((rows, N))],
        out_shape=[
            jax.ShapeDtypeStruct((rows, inner), f32),
            jax.ShapeDtypeStruct((pairs, 8, rows), f32),
            jax.ShapeDtypeStruct((rows, N), f32),
            jax.ShapeDtypeStruct((rows, N), f32),
        ],
        scratch_shapes=[pltpu.VMEM((chunks, CH, CH), f32), pltpu.VMEM((chunks, CH, CH), f32)],
        compiler_params=params(),
        cost_estimate=cost(3),
        name="intra_backward",
    )(out_grad, conv, conv, conv, cum, rate, cum_rows, marks, seg_row)


def scan_backward_kernel(
    head_size, rows, pairs, out_grad_ref, scaled_grad_ref, conv_ref, b_ref, c_ref, cum_ref, rate_ref, rate_rows_ref, step_rows_ref,
    entering_ref, pulled_ref, after_ref, skip_ref, decay_ref, b_intra_ref, c_intra_ref, pre_ref, halo_ref, taps_ref, marks_ref,
    conv_grad_ref, taps_grad_ref, step_grad_ref, log_grad_ref, bias_grad_ref,
    padded, b_total, c_total, current, head_sums, wide_marks,
):
    i = pl.program_id(0)
    chunks = rows // CH
    fill_padded(padded, halo_ref, pre_ref, rows)

    per = LANES // head_size

    @pl.when(i == 0)
    def _():
        b_total[...] = b_intra_ref[...]
        c_total[...] = c_intra_ref[...]
        head_sums[...] = jnp.zeros(head_sums.shape, f32)
        spread_marks(wide_marks, marks_ref, M_FWD)

    @pl.when(i < pairs)
    def _():
        after = after_ref[...]
        row, lane = iota2((6 * LANES, LANES))
        quantity = (row // LANES) % 3
        selector = (lane == 8 * i + per * quantity + (row % LANES) // head_size).astype(bf16)
        last_row = lax.broadcasted_iota(jnp.int32, (CH, LANES), 0) == CH - 1
        for n in reversed(range(chunks)):
            here = pl.ds(n * CH, CH)
            last = (n + 1) * CH - 1
            mark_enter = marks_ref[here, M_ENTER : M_ENTER + 1]
            mark_leave = marks_ref[here, M_LEAVE : M_LEAVE + 1]
            cum = cum_ref[here, :]
            enter = jnp.exp(cum) * mark_enter
            leave = jnp.exp(cum_ref[last : last + 1, :] - cum) * mark_leave
            conv = conv_ref[here, :]
            rate = rate_ref[here, :]
            scaled = rate * conv
            out_grad = out_grad_ref[here, :]
            state = entering_ref[n]
            left = leave * precise_mm(b_ref[here, :], after)
            scaled_grad = scaled_grad_ref[here, :] + left
            b_total[here, :] += precise_nt(scaled * leave, after)
            entered = out_grad * enter
            c_total[here, :] += precise_nt(entered, state)
            kept = enter[CH - 1 : CH, :]
            through = jnp.sum(kept * (state * after), axis=0, keepdims=True)
            came = entered * precise_mm(c_ref[here, :], state) + jnp.where(last_row, through, 0.0)
            parts = [split(value) for value in (came, scaled * left, conv * scaled_grad)]
            stacked = jnp.concatenate([high for high, _ in parts] + [low for _, low in parts], axis=1)
            head_sums[here, :] += mm(stacked, selector)
            current[here, :] = rate * scaled_grad + skip_ref[...] * out_grad
            after = kept * after + pulled_ref[n]

    @pl.when(i == pairs)
    def _():
        current[...] = b_total[...]
        r, c = iota2((CH, CH))
        from_row = (r >= c).astype(bf16)
        before = (r < c).astype(bf16)
        totals = [(jnp.zeros((per, 1), f32), jnp.zeros((per, 1), f32)) for _ in range(pairs)]
        for n in range(chunks):
            here = pl.ds(n * CH, CH)
            turned = head_sums[here, :].T
            came, gone = times_mask(turned, from_row), times_mask(turned, before)
            for j in range(pairs):
                first = 8 * j
                log_rate_grad = (
                    rate_rows_ref[j, 0:per, here] + came[first : first + per] + gone[first + per : first + 2 * per]
                )
                direct = turned[first + 2 * per : first + 3 * per]
                shifted = step_rows_ref[j, 0:per, here]
                decay = decay_ref[j, 0:per, 0:1]
                step_grad = (direct + log_rate_grad * decay) * sigmoid(shifted)
                step_grad_ref[j, 0:per, here] = step_grad
                log_total, bias_total = totals[j]
                totals[j] = (
                    log_total + jnp.sum(log_rate_grad * softplus(shifted), axis=1, keepdims=True) * decay,
                    bias_total + jnp.sum(step_grad, axis=1, keepdims=True),
                )
        for j, (log_total, bias_total) in enumerate(totals):
            log_grad_ref[j, 0:per, :] = jnp.broadcast_to(log_total, (per, LANES))
            bias_grad_ref[j, 0:per, :] = jnp.broadcast_to(bias_total, (per, LANES))

    @pl.when(i == pairs + 1)
    def _():
        current[...] = c_total[...]

    sums = [jnp.zeros((1, LANES), f32) for _ in range(KC + 1)]
    for start in range(0, rows, TILE):
        value = conv_tile(padded, taps_ref, wide_marks, start, TILE)
        sig = sigmoid(value)
        grad = current[pl.ds(start, TILE), :] * (sig * (1.0 + value * (1.0 - sig)))
        conv_grad_ref[pl.ds(start, TILE), :] = grad
        for k in range(KC):
            shifted = padded[pl.ds(start + HALO - KC + 1 + k, TILE), :]
            if k < KC - 1:
                shifted = shifted * wide_marks[k, pl.ds(start, TILE), :]
            sums[k] = sums[k] + jnp.sum(grad * shifted, axis=0, keepdims=True)
        sums[KC] = sums[KC] + jnp.sum(grad, axis=0, keepdims=True)
    taps_grad_ref[...] = jnp.concatenate(sums + [jnp.zeros((8 - KC - 1, LANES), f32)], axis=0)


def scan_backward(
    out_grad, scaled_grad, conv, cum, rate, rate_rows, step_rows, entering, pulled, after, skip, decay_rows,
    b_intra, c_intra, pre, halo, taps, marks, head_size, held=(),
):
    rows, inner = out_grad.shape
    mixed = pre.shape[1]
    pairs = inner // LANES
    chunks = rows // CH
    steps = pairs + 2
    own = lambda i: jnp.minimum(i, pairs - 1)
    block = pl.BlockSpec((rows, LANES), lambda i: (0, own(i)))
    column = lambda i: (0, i)
    heads, few = whole((pairs, 8, rows)), whole((pairs, 8, LANES))
    states = pl.BlockSpec((chunks, N, LANES), lambda i: (0, 0, own(i)))
    return call(
        partial(scan_backward_kernel, head_size, rows, pairs),
        held,
        grid=(steps,),
        in_specs=[
            block, block, block, pl.BlockSpec((rows, LANES), lambda i: (0, pairs)),
            pl.BlockSpec((rows, LANES), lambda i: (0, pairs + 1)), block, block, heads, heads, states, states,
            pl.BlockSpec((N, LANES), lambda i: (0, own(i))), pl.BlockSpec((1, LANES), lambda i: (0, own(i))), few,
            whole((rows, N)), whole((rows, N)), pl.BlockSpec((rows, LANES), column), pl.BlockSpec((HALO, LANES), column),
            pl.BlockSpec((8, LANES), column), whole((rows, LANES)),
        ],
        out_specs=[pl.BlockSpec((rows, LANES), column), pl.BlockSpec((8, LANES), column), heads, few, few],
        out_shape=[
            jax.ShapeDtypeStruct((rows, mixed), f32),
            jax.ShapeDtypeStruct((8, mixed), f32),
            jax.ShapeDtypeStruct((pairs, 8, rows), f32),
            jax.ShapeDtypeStruct((pairs, 8, LANES), f32),
            jax.ShapeDtypeStruct((pairs, 8, LANES), f32),
        ],
        scratch_shapes=[
            pltpu.VMEM((rows + HALO, LANES), f32),
            pltpu.VMEM((rows, N), f32),
            pltpu.VMEM((rows, N), f32),
            pltpu.VMEM((rows, LANES), f32),
            pltpu.VMEM((rows, LANES), f32),
            pltpu.VMEM((KC - 1, rows, LANES), f32),
        ],
        compiler_params=params(),
        cost_estimate=cost(3),
        name="scan_backward",
    )(
        out_grad, scaled_grad, conv, conv, conv, cum, rate, rate_rows, step_rows, entering, pulled, after, skip, decay_rows,
        b_intra, c_intra, pre, halo, taps, marks,
    )


def conv_backward_kernel(
    rows, pairs, per, conv_grad_ref, next_ref, taps_ref, marks_ref, pre_ref, gate_dots_ref, step_grad_ref, step_rows_ref,
    bias_ref, out_ref, map_grad_ref, dots_ref, padded, products, wide_marks,
):
    i = pl.program_id(0)
    row = lax.broadcasted_iota(jnp.int32, (8, LANES), 0)

    @pl.when(i == 0)
    def _():
        dots_ref[...] = gate_dots_ref[...]
        products[...] = jnp.zeros(products.shape, f32)
        spread_marks(wide_marks, marks_ref, M_BWD)

    @pl.when(i > 0)
    def _():
        padded[pl.ds(0, rows), :] = conv_grad_ref[...]
        padded[pl.ds(rows, 8), :] = next_ref[...]
        for start in range(0, rows, TILE):
            total = taps_ref[KC - 1 : KC, :] * padded[pl.ds(start, TILE), :]
            for k in range(KC - 1):
                shifted = padded[pl.ds(start + KC - 1 - k, TILE), :]
                total = total + taps_ref[k : k + 1, :] * (
                    shifted * wide_marks[k, pl.ds(start, TILE), :]
                )
            out_ref[pl.ds(start, TILE), :] = total.astype(bf16)
            map_grad_ref[pl.ds(start, TILE), :] = total
            products[pl.ds(start, TILE), :] += total * pre_ref[pl.ds(start, TILE), :].astype(f32)

    @pl.when(i == 0)
    def _():
        grads = [step_grad_ref[j, 0:per, :] for j in range(pairs)]
        grads = jnp.concatenate(grads + [jnp.zeros((LANES - per * pairs, rows), f32)], axis=0)
        out_ref[...] = grads.T.astype(bf16)
        total = jnp.zeros((1, rows), f32)
        for j in range(pairs):
            total = total + jnp.sum(
                step_grad_ref[j, 0:per, :] * (step_rows_ref[j, 0:per, :] - bias_ref[j, 0:per, 0:1]), axis=0, keepdims=True
            )
        dots_ref[0:1, :] += total

    @pl.when(i == pl.num_programs(0) - 1)
    def _():
        dots_ref[...] += rows_of((row == 0).astype(bf16), products[...])


def conv_backward(conv_grad, next_grad, taps, marks, pre, gate_dots, step_grad, step_rows, bias_rows, head_size, held=()):
    rows, mixed = pre.shape
    pairs = (mixed - 2 * N) // LANES
    steps = pairs + 3
    column = lambda i: (0, jnp.clip(i - 1, 0, pairs + 1))
    return call(
        partial(conv_backward_kernel, rows, pairs, LANES // head_size),
        held,
        grid=(steps,),
        in_specs=[
            pl.BlockSpec((rows, LANES), column), pl.BlockSpec((8, LANES), column), pl.BlockSpec((8, LANES), column),
            whole((rows, LANES)), pl.BlockSpec((rows, LANES), column),
            whole((8, rows)),
            whole((pairs, 8, rows)), whole((pairs, 8, rows)), whole((pairs, 8, LANES)),
        ],
        out_specs=[
            pl.BlockSpec((rows, LANES), lambda i: (0, i)),
            pl.BlockSpec((rows, LANES), lambda i: (0, jnp.clip(i - pairs - 1, 0, 1))),
            whole((8, rows)),
        ],
        out_shape=[
            jax.ShapeDtypeStruct((rows, steps * LANES), bf16),
            jax.ShapeDtypeStruct((rows, 2 * N), f32),
            jax.ShapeDtypeStruct((8, rows), f32),
        ],
        scratch_shapes=[
            pltpu.VMEM((rows + 8, LANES), f32), pltpu.VMEM((rows, LANES), f32), pltpu.VMEM((KC - 1, rows, LANES), f32),
        ],
        compiler_params=params(32 * 1024 * 1024),
        cost_estimate=cost(6),
        name="conv_backward",
    )(conv_grad, next_grad, taps, marks, pre, gate_dots, step_grad, step_rows, bias_rows)


def join_kernel(count, width, index_ref, *refs):
    blocks, out_ref = refs[:count], refs[count]
    for n in range(count):
        start = pl.multiple_of((index_ref[0] ^ n) * width, LANES)
        out_ref[:, pl.ds(start, width)] = blocks[n][...].astype(out_ref.dtype)


def join(blocks, index, dtype, first_row, held=()):
    count = len(blocks)
    rows, width = blocks[0].shape
    rows -= first_row
    size = min(rows, 256)
    return call(
        partial(join_kernel, count, width),
        held,
        grid=(rows // size,),
        in_specs=[pl.BlockSpec(memory_space=pltpu.SMEM)]
        + [pl.BlockSpec((size, width), lambda i: (i + first_row // size, 0))] * count,
        out_specs=pl.BlockSpec((size, count * width), lambda i: (i, 0)),
        out_shape=jax.ShapeDtypeStruct((rows, count * width), dtype),
        compiler_params=params(16 * 1024 * 1024),
        cost_estimate=cost(2),
        name="join",
    )(index, *blocks)


def join_norm_kernel(count, width, index_ref, gain_ref, *refs):
    blocks, normed_ref, scale_ref = refs[:count], refs[count], refs[count + 1]
    total = jnp.zeros((blocks[0].shape[0], 1), f32)
    for n in range(count):
        value = blocks[n][...].astype(f32)
        total = total + jnp.sum(value * value, axis=1, keepdims=True)
    scale = lax.rsqrt(total / (count * width) + epsilon)
    scale_ref[...] = jnp.broadcast_to(scale, scale_ref.shape)
    for n in range(count):
        here = pl.ds(pl.multiple_of((index_ref[0] ^ n) * width, LANES), width)
        normed_ref[:, here] = (blocks[n][...].astype(f32) * scale * gain_ref[:, here]).astype(bf16)


def join_norm(blocks, index, gain, rows, held=()):
    count = len(blocks)
    width = blocks[0].shape[1]
    size = 128
    block = pl.BlockSpec((size, width), lambda i: (i, 0))
    return call(
        partial(join_norm_kernel, count, width),
        held,
        grid=(rows // size,),
        in_specs=[pl.BlockSpec(memory_space=pltpu.SMEM), whole((1, count * width))] + [block] * count,
        out_specs=[
            pl.BlockSpec((size, count * width), lambda i: (i, 0)),
            pl.BlockSpec((size, LANES), lambda i: (i, 0)),
        ],
        out_shape=[
            jax.ShapeDtypeStruct((rows, count * width), bf16),
            jax.ShapeDtypeStruct((rows, LANES), f32),
        ],
        compiler_params=params(16 * 1024 * 1024),
        cost_estimate=cost(3),
        name="join_norm",
    )(index, gain, *blocks)


def input_side_kernel(count, width, own_ref, dots_ref, block_ref, grad_ref, scale_ref, gain_ref, *refs):
    sent, out_ref, norm_ref = refs[: count - 1], refs[count - 1], refs[count]
    normed_grad = own_ref[...]
    for piece in sent:
        normed_grad = normed_grad + piece[...].astype(f32)
    scale = scale_ref[:, 0:1]
    rows = scale.shape[0]
    mean = jnp.broadcast_to(dots_ref[0:1, :] / width, (LANES, rows)).T[:, 0:1]
    normed_x = block_ref[...].astype(f32) * scale
    grad = grad_ref[...].astype(f32) + scale * (gain_ref[...] * normed_grad - normed_x * mean)
    out_ref[...] = grad.astype(bf16)
    norm = jnp.sum(normed_grad * normed_x, axis=0, keepdims=True)

    @pl.when(pl.program_id(0) == 0)
    def _():
        norm_ref[...] = norm

    @pl.when(pl.program_id(0) > 0)
    def _():
        norm_ref[...] += norm


def input_gradient(own, sent, dots, block, grad, scale, gain, width, held=()):
    rows, cols = own.shape
    size = 128
    part = pl.BlockSpec((size, cols), lambda i: (i, 0))
    return call(
        partial(input_side_kernel, len(sent) + 1, float(width)),
        held,
        grid=(rows // size,),
        in_specs=[
            part, pl.BlockSpec((8, size), lambda i: (0, i)), part, part, pl.BlockSpec((size, LANES), lambda i: (i, 0)),
            whole((1, cols)),
        ]
        + [part] * len(sent),
        out_specs=[part, whole((1, cols))],
        out_shape=[jax.ShapeDtypeStruct((rows, cols), bf16), jax.ShapeDtypeStruct((1, cols), f32)],
        compiler_params=params(16 * 1024 * 1024),
        cost_estimate=cost(3),
        name="input_gradient",
    )(own, dots, block, grad, scale, gain, *sent)


def join_micro_kernel(count, width, held, places_ref, *refs):
    out_ref, refs = refs[-1], refs[held:]
    for n in range(count):
        start = pl.multiple_of((places_ref[0] ^ n) * width, LANES)
        out_ref[:, pl.ds(start, width)] = refs[n][...].astype(out_ref.dtype)


def join_micro(places, blocks, dtype, held=()):
    count = len(blocks)
    rows, width = blocks[0].shape
    size = rows // 4
    return pl.pallas_call(
        partial(join_micro_kernel, count, width, len(held)),
        grid_spec=pltpu.PrefetchScalarGridSpec(
            num_scalar_prefetch=1,
            grid=(4,),
            in_specs=[pl.BlockSpec(memory_space=pl.ANY)] * len(held)
            + [pl.BlockSpec((size, width), lambda i, places: (i, 0))] * count,
            out_specs=pl.BlockSpec((size, count * width), lambda i, places: (places[1] ^ i, 0)),
        ),
        out_shape=jax.ShapeDtypeStruct((rows, count * width), dtype),
        compiler_params=params(16 * 1024 * 1024),
        cost_estimate=cost(5),
        name="join_micro",
    )(places, *held, *blocks)


def join_gathered_kernel(count, width, held, places_ref, *refs):
    out_ref, blocks_ref = refs[-1], refs[held]
    for n in range(count):
        out_ref[:, n * width : (n + 1) * width] = blocks_ref[n].astype(out_ref.dtype)


def join_gathered(places, blocks, dtype, held=()):
    count, rows, width = blocks.shape
    size = rows // 4
    return pl.pallas_call(
        partial(join_gathered_kernel, count, width, len(held)),
        grid_spec=pltpu.PrefetchScalarGridSpec(
            num_scalar_prefetch=1,
            grid=(4,),
            in_specs=[pl.BlockSpec(memory_space=pl.ANY)] * len(held)
            + [pl.BlockSpec((count, size, width), lambda i, places: (0, i, 0))],
            out_specs=pl.BlockSpec((size, count * width), lambda i, places: (places[1] ^ i, 0)),
        ),
        out_shape=jax.ShapeDtypeStruct((rows, count * width), dtype),
        compiler_params=params(),
        cost_estimate=cost(5),
        name="join_gathered",
    )(places, *held, blocks)


def place_maps_kernel(count, places_ref, term_ref, normed_ref, *refs):
    pieces, out_ref = refs[:count], refs[count]
    rows = pieces[0].shape[0]
    total = jnp.zeros(out_ref.shape, f32)
    for n in range(count):
        here = pl.ds(pl.multiple_of((places_ref[0] ^ n) * rows, 16), rows)
        total = total + mm_tn(normed_ref[here, :], pieces[n][...])
    out_ref[...] = total.astype(bf16)


def place_maps(index, term, normed, pieces, first_column):
    count = len(pieces)
    rows, width = pieces[0].shape
    depth = normed.shape[1]
    return pl.pallas_call(
        partial(place_maps_kernel, count),
        grid=(width // LANES,),
        in_specs=[pl.BlockSpec(memory_space=pltpu.SMEM), pl.BlockSpec(memory_space=pl.ANY), whole(normed.shape)]
        + [pl.BlockSpec((rows, LANES), lambda i: (0, i))] * count,
        out_specs=pl.BlockSpec((depth, LANES), lambda i: (0, i + first_column // LANES)),
        out_shape=jax.ShapeDtypeStruct(term.shape, term.dtype),
        input_output_aliases={1: 0},
        compiler_params=params(16 * 1024 * 1024),
        cost_estimate=cost(3),
        name="place_maps",
    )(index, term, normed, *pieces)


def from_behind(block, axis, distance):
    devices = range(lax.axis_size(axis))
    route = [(i - distance, i) for i in devices if i - distance in devices]
    return lax.ppermute(block, axis, route)


def prefix(value, axis, join, neutral, backward):
    count, mine = (lax.axis_size(axis), lax.axis_index(axis))
    pieces = jax.tree.map(lambda part: lax.all_gather(part, axis), value)
    if backward:
        pieces = jax.tree.map(lambda part: part[::-1], pieces)
        mine = count - 1 - mine
    total = jax.tree.map(
        lambda part, zero: jnp.full_like(part, 0) + jnp.asarray(zero, part.dtype), value, neutral
    )

    def hop(position, total):
        longer = join(total, jax.tree.map(lambda part: part[position], pieces))
        return jax.tree.map(lambda new, old: jnp.where(position < mine, new, old), longer, total)

    return lax.fori_loop(0, count - 1, hop, total)


def block_step(decay_rate, carried, inputs):
    state_now, seg_before = carried
    x_block, rate_block, b_block, c_block, seg_block = inputs
    cumulative = jnp.cumsum(rate_block * decay_rate[None, :], axis=0)
    width_block = seg_block.shape[0]
    row_index = lax.broadcasted_iota(jnp.int32, (width_block, width_block), 0)
    col_index = lax.broadcasted_iota(jnp.int32, (width_block, width_block), 1)
    within = (row_index >= col_index) & (seg_block[:, None] == seg_block[None, :])
    within_heads = within[:, :, None]
    spread = cumulative[:, None, :] - cumulative[None, :, :]
    decay = jnp.where(within_heads, jnp.exp(jnp.where(within_heads, spread, 0.0)), 0.0)
    scores = jnp.dot(c_block, b_block.T, precision=precise)
    weights = scores[:, :, None] * decay * rate_block[None, :, :]
    output = jnp.einsum("tsh,shp->thp", weights, x_block, precision=precise)
    entering = jnp.exp(cumulative) * (seg_block == seg_before)[:, None].astype(jnp.float32)
    output = output + entering[:, :, None] * jnp.einsum(
        "tn,hpn->thp", c_block, state_now, precision=precise
    )
    leaving = (
        jnp.exp(cumulative[-1][None, :] - cumulative)
        * (seg_block == seg_block[-1])[:, None].astype(jnp.float32)
        * rate_block
    )
    state_next = entering[-1][:, None, None] * state_now + jnp.einsum(
        "sh,shp,sn->hpn", leaving, x_block, b_block, precision=precise
    )
    return ((state_next, seg_block[-1]), output)


def scan_blocks(x_heads, step_rate, b_part, c_part, seg_own, decay_rate, state_start, seg_start):
    blocks = x_heads.shape[0] // CH

    def to_blocks(value):
        return value.reshape((blocks, CH) + value.shape[1:])

    stepper = jax.checkpoint(partial(block_step, decay_rate))
    final_carry, output = lax.scan(
        stepper,
        (state_start, seg_start),
        (
            to_blocks(x_heads),
            to_blocks(step_rate),
            to_blocks(b_part),
            to_blocks(c_part),
            to_blocks(seg_own),
        ),
    )
    return (output.reshape(x_heads.shape), final_carry[0])


def causal_conv(padded_in, kernel, offset, seg_padded):
    own_rows = padded_in.shape[0] - (KC - 1)
    current = seg_padded[KC - 1 :]
    summed = jnp.zeros((own_rows, padded_in.shape[1]), jnp.float32) + offset[None, :]
    for tap_index in range(KC):
        shifted = padded_in[tap_index : tap_index + own_rows]
        same_doc = (seg_padded[tap_index : tap_index + own_rows] == current).astype(jnp.float32)
        summed = summed + kernel[tap_index][None, :] * shifted * same_doc[:, None]
    return summed


def chain_combine(earlier, later):
    return (earlier[0] * later[0], earlier[1] * later[0][:, None, None] + later[1])


def project_in(layer_in, gain_row, zx_full, bc_full, dt_full):
    inputs_f = layer_in.astype(jnp.float32)
    in_scale = lax.rsqrt(jnp.mean(inputs_f * inputs_f, axis=1) + epsilon)
    normed = (inputs_f * in_scale[:, None] * gain_row[None, :]).astype(jnp.bfloat16)
    model_width = zx_full.shape[0]
    inner_local = zx_full.shape[2]
    joined = jnp.dot(
        normed, zx_full.reshape(model_width, 2 * inner_local), preferred_element_type=jnp.float32
    )
    bc_pre = jnp.dot(normed, bc_full, preferred_element_type=jnp.float32)
    mixed_pre = jnp.concatenate([joined[:, inner_local:], bc_pre], axis=1).astype(jnp.bfloat16)
    step_pre = jnp.dot(normed, dt_full, preferred_element_type=jnp.float32)
    return (inputs_f, in_scale, normed, joined[:, :inner_local], mixed_pre, step_pre)


def mixer_parts(padded_in, step_pre, kernel, offset, bias_row, log_rate, seg_padded, heads_local):
    own_rows = step_pre.shape[0]
    inner_local = padded_in.shape[1] - 2 * N
    head_size = inner_local // heads_local
    conv_out = jax.nn.silu(causal_conv(padded_in, kernel, offset, seg_padded))
    x_heads = conv_out[:, :inner_local].reshape(own_rows, heads_local, head_size)
    b_part = conv_out[:, inner_local : inner_local + N]
    c_part = conv_out[:, inner_local + N :]
    step_rate = jax.nn.softplus(step_pre + bias_row[None, :])
    decay_rate = -jnp.exp(log_rate)
    seg_own = seg_padded[KC - 1 :]
    seg_start = seg_padded[KC - 2]
    local_out, local_state = scan_blocks(
        x_heads,
        step_rate,
        b_part,
        c_part,
        seg_own,
        decay_rate,
        jnp.zeros((heads_local, head_size, N), jnp.float32),
        seg_start,
    )
    carried = jnp.exp(jnp.cumsum(step_rate * decay_rate[None, :], axis=0)) * (seg_own == seg_start)[
        :, None
    ].astype(jnp.float32)
    return (x_heads, c_part, local_out, local_state, carried)


def mixer_tail(parts, state_in, gate_pre, skip_row):
    x_heads, c_part, local_out, local_state, carried = parts
    own_rows = gate_pre.shape[0]
    ssm_out = (
        local_out
        + carried[:, :, None] * jnp.einsum("tn,hpn->thp", c_part, state_in, precision=precise)
        + skip_row[None, :, None] * x_heads
    )
    gate_act = jax.nn.silu(gate_pre)
    gated = ssm_out.reshape(own_rows, gate_pre.shape[1]) * gate_act
    state_out = carried[-1][:, None, None] * state_in + local_state
    return ((gated, state_out), (carried, c_part, gate_act))


def select_batch(array_in, chosen):
    return lax.dynamic_index_in_dim(array_in, chosen, 0, keepdims=False)


def store_batch(buffer, value, chosen, valid):
    return jnp.where(valid, lax.dynamic_update_index_in_dim(buffer, value, chosen, 0), buffer)


def body(
    tokens,
    cotangent,
    seg_ids,
    norm_gain,
    in_zx,
    in_bc,
    in_dt,
    conv_x,
    conv_xb,
    conv_bc,
    conv_bcb,
    dt_bias,
    a_log,
    skip_gain,
    gate_gain,
    out_w,
):
    section_index = lax.axis_index("section")
    ctx_index = lax.axis_index("ctx")
    tensor_index = lax.axis_index("tensor")
    section_count = lax.axis_size("section")
    tensor_count = lax.axis_size("tensor")
    batches = tokens.shape[0]
    token_rows = tokens.shape[1]
    model_width = tokens.shape[2]
    zx_full, bc_full, dt_full, out_full = (
        lax.all_gather(in_zx[0], "ctx", axis=0, tiled=True),
        lax.all_gather(in_bc[0], "ctx", axis=0, tiled=True),
        lax.all_gather(in_dt[0], "ctx", axis=0, tiled=True),
        lax.all_gather(out_w[0], "ctx", axis=1, tiled=True),
    )
    inner_local = zx_full.shape[2]
    heads_local = dt_full.shape[1]
    head_size = inner_local // heads_local
    mixed_width = inner_local + 2 * N
    gain_row = norm_gain[0].astype(jnp.float32)
    kernel = jnp.concatenate([conv_x[0], conv_bc[0]], axis=1).astype(jnp.float32)
    offset = jnp.concatenate([conv_xb[0], conv_bcb[0]]).astype(jnp.float32)
    bias_row = dt_bias[0]
    log_rate = a_log[0]
    skip_row = skip_gain[0]
    gate_row = gate_gain[0].astype(jnp.float32)
    seg_lead = jnp.full((batches, KC - 1), -1, jnp.int32)
    seg_all = jnp.concatenate([seg_lead, seg_ids], axis=1)
    seg_local = lax.dynamic_slice_in_dim(seg_all, ctx_index * token_rows, token_rows + KC - 1, 1)
    chain_start = (
        jnp.ones((heads_local,), jnp.float32),
        jnp.zeros((heads_local, head_size, N), jnp.float32),
    )
    kept_inputs = jnp.zeros((batches, token_rows, model_width), jnp.bfloat16)
    kept_states = jnp.zeros((batches, heads_local, head_size, N), jnp.float32)
    kept_scales = jnp.zeros((batches, token_rows), jnp.float32)
    kept_edges = jnp.zeros((batches, KC - 1, mixed_width), jnp.bfloat16)
    section_store = jnp.zeros((batches, token_rows, model_width), jnp.bfloat16)
    received = jnp.zeros((token_rows, model_width), jnp.bfloat16)
    for tick_number in range(batches + section_count - 1):
        batch_index = tick_number - section_index
        valid = (batch_index >= 0) & (batch_index < batches)
        chosen = jnp.clip(batch_index, 0, batches - 1)
        layer_in = jnp.where(section_index == 0, select_batch(tokens, chosen), received)
        seg_padded = select_batch(seg_local, chosen)
        inputs_f, in_scale, normed, gate_pre, mixed_pre, step_pre = project_in(
            layer_in, gain_row, zx_full, bc_full, dt_full
        )
        edge_rows = from_behind(mixed_pre[token_rows - (KC - 1) :], "ctx", 1)
        padded_in = jnp.concatenate([edge_rows, mixed_pre], axis=0).astype(jnp.float32)
        parts = mixer_parts(
            padded_in, step_pre, kernel, offset, bias_row, log_rate, seg_padded, heads_local
        )
        state_in = prefix((parts[4][-1], parts[3]), "ctx", chain_combine, chain_start, False)[1]
        gated = mixer_tail(parts, state_in, gate_pre, skip_row)[0][0]
        squares = lax.psum(jnp.sum(gated * gated, axis=1), "tensor")
        gate_scale = lax.rsqrt(squares / DI + epsilon)
        gate_normed = (gated * gate_scale[:, None] * gate_row[None, :]).astype(jnp.bfloat16)
        projected = lax.psum(
            jnp.dot(gate_normed, out_full, preferred_element_type=jnp.float32), "tensor"
        )
        layer_out = (inputs_f + projected).astype(jnp.bfloat16)
        kept_inputs = store_batch(kept_inputs, layer_in, chosen, valid)
        kept_states = store_batch(kept_states, state_in, chosen, valid)
        kept_scales = store_batch(kept_scales, gate_scale, chosen, valid)
        kept_edges = store_batch(kept_edges, edge_rows, chosen, valid)
        section_store = store_batch(section_store, layer_out, chosen, valid)
        received = from_behind(layer_out, "section", 1)
    acc_zx = jnp.zeros((model_width, 2 * inner_local), jnp.float32)
    acc_dt = jnp.zeros((model_width, heads_local), jnp.float32)
    acc_out = jnp.zeros((inner_local, model_width), jnp.float32)
    acc_bc = jnp.zeros((model_width, 2 * N), jnp.float32)
    acc_gain = jnp.zeros((model_width,), jnp.float32)
    acc_kernel = jnp.zeros((KC, mixed_width), jnp.float32)
    acc_offset = jnp.zeros((mixed_width,), jnp.float32)
    acc_bias = jnp.zeros((heads_local,), jnp.float32)
    acc_log = jnp.zeros((heads_local,), jnp.float32)
    acc_skip = jnp.zeros((heads_local,), jnp.float32)
    acc_gate = jnp.zeros((inner_local,), jnp.float32)
    grad_store = jnp.zeros((batches, token_rows, model_width), jnp.float32)
    received_grad = jnp.zeros((token_rows, model_width), jnp.bfloat16)
    last_section = section_count - 1
    contract = (((0,), (0,)), ((), ()))
    for tick_number in range(batches + section_count - 1):
        batch_index = batches - 1 - tick_number + (last_section - section_index)
        valid = (batch_index >= 0) & (batch_index < batches)
        chosen = jnp.clip(batch_index, 0, batches - 1)
        out_grad = jnp.where(
            section_index == last_section, select_batch(cotangent, chosen), received_grad
        )
        seg_padded = select_batch(seg_local, chosen)
        inputs_f, in_scale, normed, gate_pre, mixed_pre, step_pre = project_in(
            select_batch(kept_inputs, chosen), gain_row, zx_full, bc_full, dt_full
        )
        padded_in = jnp.concatenate([select_batch(kept_edges, chosen), mixed_pre], axis=0).astype(
            jnp.float32
        )
        state_in = select_batch(kept_states, chosen)
        gate_scale = select_batch(kept_scales, chosen)

        def local_mixer(
            padded_arg,
            gate_arg,
            step_arg,
            state_arg,
            kernel_arg,
            offset_arg,
            bias_arg,
            log_arg,
            skip_arg,
        ):
            return mixer_tail(
                mixer_parts(
                    padded_arg,
                    step_arg,
                    kernel_arg,
                    offset_arg,
                    bias_arg,
                    log_arg,
                    seg_padded,
                    heads_local,
                ),
                state_arg,
                gate_arg,
                skip_arg,
            )

        outputs, pullback, extras = jax.vjp(
            local_mixer,
            padded_in,
            gate_pre,
            step_pre,
            state_in,
            kernel,
            offset,
            bias_row,
            log_rate,
            skip_row,
            has_aux=True,
        )
        gated = outputs[0]
        carried, c_part, gate_act = extras
        gate_normed = (gated * gate_scale[:, None] * gate_row[None, :]).astype(jnp.bfloat16)
        normed_gate_grad = jnp.dot(out_grad, out_full.T, preferred_element_type=jnp.float32)
        out_term = lax.dot_general(
            gate_normed, out_grad, contract, preferred_element_type=jnp.float32
        )
        gate_term = jnp.sum(normed_gate_grad * gated * gate_scale[:, None], axis=0)
        projection = lax.psum(
            jnp.sum(normed_gate_grad * gate_row[None, :] * gated, axis=1), "tensor"
        )
        gated_grad = (
            gate_scale[:, None] * gate_row[None, :] * normed_gate_grad
            - gated * (gate_scale**3 * projection / DI)[:, None]
        )
        out_heads = (gated_grad * gate_act).reshape(token_rows, heads_local, head_size)
        pull_state = jnp.einsum("th,thp,tn->hpn", carried, out_heads, c_part, precision=precise)
        state_after = prefix((carried[-1], pull_state), "ctx", chain_combine, chain_start, True)[1]
        (
            padded_grad,
            gate_grad,
            step_grad,
            unused_state,
            kernel_grad,
            offset_grad,
            bias_grad,
            log_grad,
            skip_grad,
        ) = pullback((gated_grad, state_after))
        edge_grad = from_behind(padded_grad[: KC - 1], "ctx", -1)
        mixed_grad = padded_grad[KC - 1 :].at[token_rows - (KC - 1) :].add(edge_grad)
        zx_grad = jnp.concatenate(
            [gate_grad.astype(jnp.bfloat16), mixed_grad[:, :inner_local].astype(jnp.bfloat16)],
            axis=1,
        )
        bc_grad = mixed_grad[:, inner_local:]
        step_low = step_grad.astype(jnp.bfloat16)
        normed_grad = jnp.dot(
            zx_grad,
            zx_full.reshape(model_width, 2 * inner_local).T,
            preferred_element_type=jnp.float32,
        )
        normed_grad = normed_grad + jnp.dot(step_low, dt_full.T, preferred_element_type=jnp.float32)
        normed_grad = normed_grad + jnp.dot(
            bc_grad, bc_full.astype(jnp.float32).T, precision=precise
        )
        zx_term = lax.dot_general(normed, zx_grad, contract, preferred_element_type=jnp.float32)
        dt_term = lax.dot_general(normed, step_low, contract, preferred_element_type=jnp.float32)
        bc_term = lax.dot_general(normed.astype(jnp.float32), bc_grad, contract, precision=precise)
        normed_grad = lax.psum(normed_grad.astype(jnp.bfloat16), "tensor").astype(jnp.float32)
        normed_x = inputs_f * in_scale[:, None]
        weighted = gain_row[None, :] * normed_grad
        input_grad = out_grad.astype(jnp.float32) + in_scale[:, None] * (
            weighted - normed_x * jnp.mean(weighted * normed_x, axis=1)[:, None]
        )
        norm_term = jnp.sum(normed_grad * normed_x, axis=0)
        sent_grad = input_grad.astype(jnp.bfloat16)
        grad_store = store_batch(
            grad_store,
            jnp.where(section_index == 0, input_grad, sent_grad.astype(jnp.float32)),
            chosen,
            valid,
        )
        acc_zx = jnp.where(valid, acc_zx + zx_term, acc_zx)
        acc_dt = jnp.where(valid, acc_dt + dt_term, acc_dt)
        acc_out = jnp.where(valid, acc_out + out_term, acc_out)
        acc_bc = jnp.where(valid, acc_bc + bc_term, acc_bc)
        acc_gain = jnp.where(valid, acc_gain + norm_term, acc_gain)
        acc_kernel = jnp.where(valid, acc_kernel + kernel_grad, acc_kernel)
        acc_offset = jnp.where(valid, acc_offset + offset_grad, acc_offset)
        acc_bias = jnp.where(valid, acc_bias + bias_grad, acc_bias)
        acc_log = jnp.where(valid, acc_log + log_grad, acc_log)
        acc_skip = jnp.where(valid, acc_skip + skip_grad, acc_skip)
        acc_gate = jnp.where(valid, acc_gate + gate_term, acc_gate)
        received_grad = from_behind(sent_grad, "section", -1)
    zx_sum, dt_sum, out_sum = (
        lax.psum_scatter(
            acc_zx.reshape(model_width, 2, inner_local).astype(jnp.bfloat16),
            "ctx",
            scatter_dimension=0,
            tiled=True,
        ).astype(jnp.float32),
        lax.psum_scatter(
            acc_dt.astype(jnp.bfloat16), "ctx", scatter_dimension=0, tiled=True
        ).astype(jnp.float32),
        lax.psum_scatter(
            acc_out.astype(jnp.bfloat16), "ctx", scatter_dimension=1, tiled=True
        ).astype(jnp.float32),
    )
    first_tensor = (tensor_index == 0).astype(jnp.float32)

    def widen(piece):
        full_shape = piece.shape[:-1] + (piece.shape[-1] * tensor_count,)
        return lax.dynamic_update_slice_in_dim(
            jnp.zeros(full_shape, jnp.float32),
            piece,
            tensor_index * piece.shape[-1],
            piece.ndim - 1,
        )

    def narrow(full_array):
        own_width = full_array.shape[-1] // tensor_count
        return lax.dynamic_slice_in_dim(
            full_array, tensor_index * own_width, own_width, full_array.ndim - 1
        )

    sums = lax.psum(
        (
            acc_bc,
            acc_gain * first_tensor,
            acc_kernel[:, inner_local:],
            acc_offset[inner_local:],
            widen(acc_kernel[:, :inner_local]),
            widen(acc_offset[:inner_local]),
            widen(acc_bias),
            widen(acc_log),
            widen(acc_skip),
            widen(acc_gate),
        ),
        ("ctx", "tensor"),
    )
    rows_own = in_bc.shape[1]
    bc_rows = lax.dynamic_slice_in_dim(sums[0], ctx_index * rows_own, rows_own, 0)
    return (
        section_store[None],
        grad_store[None],
        sums[1][None],
        zx_sum[None],
        bc_rows[None],
        dt_sum[None],
        narrow(sums[4])[None],
        narrow(sums[5])[None],
        sums[2][None],
        sums[3][None],
        narrow(sums[6])[None],
        narrow(sums[7])[None],
        narrow(sums[8])[None],
        narrow(sums[9])[None],
        out_sum[None],
    )


def swap_section(value):
    return lax.ppermute(value, "section", [(0, 1), (1, 0)])


def from_partner(value, distance):
    count = lax.axis_size("tensor")
    return lax.ppermute(value, "tensor", [(i, i ^ distance) for i in range(count)])


def with_partners(value):
    return [value] + [from_partner(value, k) for k in range(1, lax.axis_size("tensor"))]


def sum_over_tensor(value):
    return sum(with_partners(value)[1:], value)


def column_block(value, index, width):
    return lax.dynamic_slice_in_dim(value, index * width, width, value.ndim - 1)


def zero_of(value):
    return jnp.minimum(jnp.abs(value[(0,) * value.ndim].astype(f32)).astype(jnp.int32), 0)


def to_micro(value):
    section, ctx, tensor = (lax.axis_index(a) for a in ("section", "ctx", "tensor"))
    count = lax.axis_size("ctx")
    width = value.shape[2] // lax.axis_size("tensor")
    came = []
    for e in range(2):
        sent = 2 * section + ((ctx & 1) ^ e)
        piece = lax.dynamic_slice(value, (sent, 0, tensor * width), (1, value.shape[1], width))[0]
        route = [(s * count + c, (c >> 1) * count + 2 * s + ((c & 1) ^ e)) for s in range(2) for c in range(count)]
        came.append(lax.ppermute(piece, ("section", "ctx"), route))
    even = (ctx & 1) == 0
    return jnp.concatenate([jnp.where(even, came[0], came[1]), jnp.where(even, came[1], came[0])], axis=0)


def to_owners(blocks):
    section, ctx, count = lax.axis_index("section"), lax.axis_index("ctx"), lax.axis_size("ctx")
    rows = blocks[0].shape[0] // 2
    pieces = []
    for e in range(count):
        half, layer = (ctx ^ e) & 1, (ctx ^ e) >> 1
        piece = lax.dynamic_slice_in_dim(jnp.where(layer == 0, blocks[0], blocks[1]), half * rows, rows, 0)
        route = [
            (s * count + z, ((z ^ e) >> 1) * count + 2 * s + ((z ^ e) & 1)) for s in range(2) for z in range(count)
        ]
        pieces.append(lax.ppermute(piece, ("section", "ctx"), route))
    ordered = []
    for n in range(count):
        wanted = ctx ^ n
        e = ((wanted ^ ctx) & 1) | ((((wanted >> 1) ^ section) & 1) << 1)
        chosen = pieces[count - 1]
        for k in range(count - 1):
            chosen = jnp.where(e == k, pieces[k], chosen)
        ordered.append(chosen)
    return jnp.concatenate(ordered, axis=0)


def in_halves(own, section):
    half = own.shape[0] // 2
    keep = lax.dynamic_slice_in_dim(own, section * half, half, 0)
    came = swap_section(lax.dynamic_slice_in_dim(own, (1 - section) * half, half, 0))
    return [jnp.where(section == layer, keep, came) for layer in range(2)]


def own_layer(halves, section):
    keep = jnp.where(section == 0, halves[0], halves[1])
    came = swap_section(jnp.where(section == 0, halves[1], halves[0]))
    return jnp.concatenate([jnp.where(section == 0, keep, came), jnp.where(section == 0, came, keep)], axis=0)


def token_marks(seg_around, rows):
    own = seg_around[HALO : HALO + rows]
    columns = [seg_around[HALO - KC + 1 + k : HALO - KC + 1 + k + rows] == own for k in range(KC)]
    columns += [seg_around[HALO + KC - 1 - k : HALO + KC - 1 - k + rows] == own for k in range(KC)]
    chunks = rows // CH
    before = seg_around[HALO - 1 : HALO - 1 + rows].reshape(chunks, CH)[:, :1]
    last = own.reshape(chunks, CH)[:, -1:]
    columns.append((own.reshape(chunks, CH) == before).reshape(rows))
    columns.append((own.reshape(chunks, CH) == last).reshape(rows))
    columns = [column.astype(f32) for column in columns] + [own.astype(f32)]
    marks = jnp.pad(jnp.stack(columns, axis=1), ((0, 0), (0, LANES - len(columns))))
    return marks, jnp.broadcast_to(own.astype(f32)[None, :], (8, rows))


class Layer:
    pass


def lane_row(values):
    return jnp.pad(values, (0, LANES - values.shape[0]))[None, :]


def pair_rows(values, per):
    pairs = values.shape[0] // per
    padded = jnp.pad(values.reshape(pairs, per), ((0, 0), (0, 8 - per)))
    return jnp.broadcast_to(padded[:, :, None], (pairs, 8, LANES))


def from_pairs(values, per):
    return values[:, :per, 0].reshape(-1)


def unpack(pack, heads, head_size, inner, width):
    layer = Layer()
    layer.taps = jnp.concatenate([pack[: KC + 1, : inner + 2 * N], jnp.zeros((8 - KC - 1, inner + 2 * N), f32)], axis=0)
    layer.norm_gain = pack[KC + 1 : KC + 2, :width]
    layer.gate_gain = pack[KC + 2 : KC + 3, :inner]
    small = pack[KC + 3, : 3 * heads].reshape(3, heads)
    per = LANES // head_size
    decay = -jnp.exp(small[1])
    layer.bias_lanes, layer.decay_lanes = lane_row(small[0]), lane_row(decay)
    layer.bias_rows, layer.decay_rows = pair_rows(small[0], per), pair_rows(decay, per)
    layer.skip = jnp.repeat(small[2], head_size)[None, :]
    return layer


transposed = (((0,), (0,)), ((), ()))
across = (((1,), (1,)), ((), ()))


def project(layer, marks, seg_row, head_size, held=()):
    layer.pre = jnp.dot(layer.normed, layer.mix[:, LANES:], preferred_element_type=f32).astype(bf16)
    step = jnp.dot(layer.normed, layer.mix[:, :LANES], preferred_element_type=f32)
    layer.halo = lax.ppermute(layer.pre[-HALO:], "section", [(0, 1)])
    (layer.conv, layer.y, layer.own_state, last_state, layer.cum, layer.rate, layer.cum_rows, layer.step_rows) = scan_forward(
        layer.pre, layer.halo, layer.taps, marks, seg_row, step, layer.bias_lanes, layer.decay_lanes, head_size, held
    )
    layer.state_in = lax.ppermute(last_state, "section", [(0, 1)])


def gate(layer, marks, grad=None):
    layer.gate = jnp.dot(layer.normed, layer.gate_weight, preferred_element_type=f32)
    layer.ssm, layer.gained, layer.entering, sums = gate_forward(
        layer.y, layer.conv, layer.cum, marks, layer.own_state, layer.state_in, layer.gate, layer.skip, layer.gate_gain, grad
    )
    return sum_over_tensor(sums)


def gate_side(layer, grad, sums, marks, channels, held=()):
    (layer.out_grad, layer.gate_grad, layer.pulled, first, layer.gain_grad, layer.skip_grad, layer.gate_dots) = gate_backward(
        grad, layer.gate, layer.ssm, layer.conv, layer.cum, marks, sums, layer.gate_gain, channels, held
    )
    layer.after = lax.ppermute(first, "section", [(1, 0)])


def scan_side(layer, marks, seg_row, head_size, held_intra=(), held_scan=(), held_conv=(), after_intra=None, late_held=None):
    per = LANES // head_size
    scaled_grad, rate_rows, b_intra, c_intra = intra_backward(
        layer.out_grad, layer.conv, layer.cum, layer.rate, layer.cum_rows, marks, seg_row, head_size, held_intra
    )
    if after_intra is not None:
        held_conv = (*held_conv, *after_intra(rate_rows))
    conv_grad, layer.taps_grad, step_grad, log_grad, bias_grad = scan_backward(
        layer.out_grad, scaled_grad, layer.conv, layer.cum, layer.rate, rate_rows, layer.step_rows, layer.entering,
        layer.pulled, layer.after, layer.skip, layer.decay_rows, b_intra, c_intra, layer.pre, layer.halo,
        layer.taps, marks, head_size, held_scan,
    )
    next_grad = lax.ppermute(conv_grad[:8], "section", [(1, 0)])
    if late_held is not None:
        held_conv = (*held_conv, *late_held(conv_grad))
    layer.mix_grad, layer.map_grad, dots = conv_backward(
        conv_grad, next_grad, layer.taps, marks, layer.pre, layer.gate_dots, step_grad, layer.step_rows,
        layer.bias_rows, head_size, held_conv,
    )
    layer.dots = sum_over_tensor(dots)
    heads = layer.skip_grad.shape[1] // head_size
    layer.small = jnp.concatenate([
        from_pairs(bias_grad, per), from_pairs(log_grad, per), layer.skip_grad.reshape(heads, head_size).sum(axis=1)
    ])


def scatter_rows(term):
    return lax.psum_scatter(term, ("ctx", "section"), scatter_dimension=0, tiled=True)


def whole_micro_body(
    tokens, cotangent, seg_ids, norm_gain, in_zx, in_bc, in_dt, conv_x, conv_xb, conv_bc, conv_bcb, dt_bias, a_log,
    skip_gain, gate_gain, out_w,
):
    section, ctx, tensor = (lax.axis_index(a) for a in ("section", "ctx", "tensor"))
    tensors, ctxs = lax.axis_size("tensor"), lax.axis_size("ctx")
    width = tokens.shape[2]
    own_width = width // tensors
    inner = conv_x.shape[2]
    heads = dt_bias.shape[1]
    head_size = inner // heads
    mixed = inner + 2 * N
    channels = inner * tensors
    rows = seg_ids.shape[1] // 2
    index = tensor.astype(jnp.int32).reshape(1)

    def block_rows(weight, b):
        return lax.dynamic_slice_in_dim(weight, b * own_width, own_width, 0)

    def gather_rows(half):
        return lax.all_gather(half, ("ctx", "section"), axis=0, tiled=True)

    own_mix = jnp.concatenate([jnp.pad(in_dt[0], ((0, 0), (0, LANES - heads))), in_zx[0, :, 1], in_bc[0]], axis=1)
    mix_halves = in_halves(own_mix, section)
    mix_first = gather_rows(mix_halves[0])
    token_block = to_micro(tokens)
    rest_halves = in_halves(jnp.concatenate([in_zx[0, :, 0], out_w[0].T], axis=1), section)

    def line(values):
        return jnp.pad(values.astype(f32), (0, width - values.shape[0]))[None, :]

    own_pack = jnp.concatenate(
        [line(jnp.concatenate([conv_x[0, k], conv_bc[0, k]])) for k in range(KC)]
        + [
            line(jnp.concatenate([conv_xb[0], conv_bcb[0]])), line(norm_gain[0]), line(gate_gain[0]),
            line(jnp.concatenate([dt_bias[0], a_log[0], skip_gain[0]])),
        ],
        axis=0,
    )
    other_pack = swap_section(own_pack)
    first, second = (
        unpack(jnp.where(section == n, own_pack, other_pack), heads, head_size, inner, width) for n in range(2)
    )
    seg_mine = lax.dynamic_index_in_dim(seg_ids, ctx, 0, keepdims=False)
    seg_around = jnp.concatenate([jnp.full((HALO,), -1, jnp.int32), seg_mine, jnp.full((HALO,), -2, jnp.int32)])
    seg_around = lax.dynamic_slice_in_dim(seg_around, section * rows, rows + 2 * HALO, 0)
    marks, seg_row = token_marks(seg_around, rows)

    first.block = token_block
    first.gate_weight = gather_rows(ordered(rest_halves[0][:, :inner], token_block))
    first.normed, first.in_scale = join_norm(with_partners(first.block), index, first.norm_gain, rows)
    first.out_turned = gather_rows(ordered(rest_halves[0][:, inner:], first.normed))
    first.mix = mix_first
    project(first, marks, seg_row, head_size)
    second.mix = gather_rows(ordered(mix_halves[1], first.pre))
    rest_second = gather_rows(ordered(rest_halves[1], first.conv))
    second.gate_weight, second.out_turned = rest_second[:, :inner], rest_second[:, inner:]
    cot_block = to_micro(ordered(cotangent, first.pre))
    sums_first = gate(first, marks)

    def gate_low(layer, sums):
        layer.gated = (layer.gained * lax.rsqrt(sums[0] / channels + epsilon)[:, None]).astype(bf16)

    def blocks_of(total, dtype):
        parts = [column_block(total, tensor ^ n, own_width) for n in range(tensors)]
        return [parts[0]] + [part.astype(dtype) for part in parts[1:]]

    def out_terms(layer, dtype):
        return blocks_of(lax.dot_general(layer.gated, layer.out_turned, across, preferred_element_type=f32), dtype)

    gate_low(first, sums_first)
    terms = out_terms(first, f32)
    projected = sum([from_partner(terms[n], n) for n in range(1, tensors)], terms[0])
    second.block = (first.block.astype(f32) + projected).astype(bf16)

    second.normed, second.in_scale = join_norm(with_partners(second.block), index, second.norm_gain, rows)
    project(second, marks, seg_row, head_size)
    cot_full = join(with_partners(ordered(cot_block, second.pre)), index, bf16, 0)
    grad_second = jnp.dot(cot_full, second.out_turned, preferred_element_type=f32)
    sums_second = gate(second, marks, grad_second)

    def input_terms(layer):
        total = lax.dot_general(layer.gate_grad, layer.gate_weight, across, preferred_element_type=f32)
        total = total + lax.dot_general(layer.mix_grad, layer.mix, across, preferred_element_type=f32)
        rest = (layer.map_grad - layer.mix_grad[:, LANES + inner :].astype(f32)).astype(bf16)
        total = total + lax.dot_general(rest, layer.mix[:, LANES + inner :], across, preferred_element_type=f32)
        return blocks_of(total, bf16)

    def send_terms(layer, terms):
        return [from_partner(ordered(terms[n], layer.dots), n) for n in range(1, tensors)]

    def input_side(layer, own, sent, out_grad_block, held=()):
        return input_gradient(
            own, sent, layer.dots, layer.block, out_grad_block, layer.in_scale,
            column_block(layer.norm_gain, tensor, own_width), width, held,
        )

    def rest_term(layer, out_grad, *others):
        low = [
            lax.dot_general(layer.normed, ordered(layer.gate_grad, *others), transposed, preferred_element_type=f32).astype(bf16),
            lax.dot_general(out_grad, layer.gated, transposed, preferred_element_type=f32).astype(bf16),
        ]
        return jnp.concatenate(low, axis=1)

    def share(layer, *others):
        count = rows // tensors
        map_grad = ordered(layer.map_grad, *others)

        def part(b):
            return lax.dynamic_slice_in_dim(map_grad, b * count, count, 0)

        total = sum([from_partner(part(tensor ^ k), k) for k in range(1, tensors)], part(tensor))
        layer.map_share = total.astype(bf16)

    def mix_start(layer):
        return lax.dot_general(layer.normed, layer.mix_grad, transposed, preferred_element_type=f32).astype(bf16)

    def mix_term(layer, started, *others):
        pieces = [ordered(piece, *others) for piece in with_partners(layer.map_share)]
        return place_maps(index, started, layer.normed, pieces, LANES + inner)

    def small_pack(layer, norm_grad):
        def row(values):
            return jnp.pad(values, (0, mixed - values.shape[0]))[None, :]

        return jnp.concatenate(
            [layer.taps_grad, row(layer.gain_grad[0]), row(layer.small), row(norm_grad[0]), jnp.zeros((5, mixed), f32)], axis=0
        )

    gate_low(second, sums_second)
    out_second = lax.dot_general(second.gated, second.out_turned, across, preferred_element_type=f32).astype(bf16)
    result = lax.psum_scatter(out_second, "tensor", scatter_dimension=1, tiled=True)
    gate_side(second, grad_second, sums_second, marks, channels, (out_second,))
    rest_term_second = rest_term(second, cot_full)
    rest_sum_second = scatter_rows(rest_term_second)
    scan_side(second, marks, seg_row, head_size, held_scan=(rest_term_second,), held_conv=(result,))
    terms = input_terms(second)
    sent = send_terms(second, terms)
    middle_block, norm_second = input_side(second, terms[0], sent, cot_block)
    share(second, *sent)
    result = (second.block.astype(f32) + ordered(result, second.dots).astype(f32)).astype(bf16)
    output_pieces = to_owners([second.block, result])
    mix_started = mix_start(second)
    middle = join(with_partners(middle_block), index, bf16, 0, (mix_started, output_pieces))
    mix_term_second = mix_term(second, mix_started, rest_sum_second, middle)
    mix_sum_second = scatter_rows(mix_term_second)

    grad_first = jnp.dot(middle, first.out_turned, preferred_element_type=f32)
    crossed = jnp.sum(grad_first * first.gained, axis=1)
    crossed = sum_over_tensor(jnp.broadcast_to(crossed[None, :], (8, rows)))
    sums_first = jnp.concatenate([sums_first[:1], crossed[:1], sums_first[2:]], axis=0)
    gate_side(first, grad_first, sums_first, marks, channels)
    outputs = with_partners(ordered(output_pieces, first.out_grad))
    rest_terms = []

    def after_scan(conv_grad):
        rest_terms.append(rest_term(first, middle, conv_grad, *outputs[1:]))
        return rest_terms

    scan_side(
        first, marks, seg_row, head_size, held_intra=(mix_term_second,), held_conv=(rest_sum_second, mix_sum_second), late_held=after_scan,
    )
    rest_sum_first = scatter_rows(rest_terms[0])
    terms = input_terms(first)
    sent = send_terms(first, terms)
    share(first, first.dots)
    last_block, norm_first = input_side(first, terms[0], sent, middle_block)
    grad_pieces = to_owners([last_block, middle_block])
    grads = with_partners(grad_pieces)
    mix_sum_first = scatter_rows(mix_term(first, mix_start(first), rest_sum_first, grad_pieces))
    places = jnp.stack([tensor, ctx]).astype(jnp.int32)
    outputs = join_micro(places, outputs, bf16, (last_block,))

    rest_sum = own_layer([rest_sum_first, rest_sum_second], section).astype(f32)
    mix_sum = own_layer([mix_sum_first, mix_sum_second], section).astype(f32)
    bc_sum = mix_sum[:, LANES + inner :]
    pack_first, pack_second = ordered(small_pack(first, norm_first), grads[1]), small_pack(second, norm_second)
    pack = jnp.where(section == 0, pack_first, pack_second) + swap_section(
        jnp.where(section == 0, pack_second, pack_first)
    )
    pack = sum(
        [lax.ppermute(pack, "ctx", [(c, (c + d) % ctxs) for c in range(ctxs)]) for d in range(1, ctxs)], pack
    )
    shared = with_partners(jnp.concatenate([pack[:8, inner:], jnp.broadcast_to(pack[10:11, :own_width], (8, own_width))], axis=1))
    taps_bc = sum([piece[:, : 2 * N] for piece in shared[1:]], shared[0][:, : 2 * N])
    norm = join([piece[:, 2 * N :] for piece in shared], index, f32, 0)[0]
    small = pack[9, : 3 * heads].reshape(3, heads)
    zx_sum = jnp.stack([rest_sum[:, :inner], mix_sum[:, LANES : LANES + inner]], axis=1)
    out_sum = rest_sum[:, inner:].T
    input_grads = join_micro(places, grads, f32, (outputs,))
    return (
        outputs.reshape(1, ctxs, -1, width),
        input_grads.reshape(1, ctxs, -1, width),
        norm[None],
        zx_sum[None],
        bc_sum[None],
        mix_sum[:, :heads][None],
        pack[:KC, :inner][None],
        pack[KC, :inner][None],
        taps_bc[:KC][None],
        taps_bc[KC][None],
        small[0][None],
        small[1][None],
        small[2][None],
        pack[8, :inner][None],
        out_sum[None],
    )


def fits(shape, batches):
    return shape["ctx"] == batches == 4 and shape["section"] == 2 and shape["tensor"] & (shape["tensor"] - 1) == 0


def solution(mesh):
    def step(*args):
        chosen = whole_micro_body if fits(dict(mesh.shape), args[0].shape[0]) else body
        return jax.shard_map(
            chosen,
            mesh=mesh,
            in_specs=(
                P(None, "ctx", None),
                P(None, "ctx", None),
                P(),
                P("section", None),
                P("section", "ctx", None, "tensor"),
                P("section", "ctx", None),
                P("section", "ctx", "tensor"),
                P("section", None, "tensor"),
                P("section", "tensor"),
                P("section", None, None),
                P("section", None),
                P("section", "tensor"),
                P("section", "tensor"),
                P("section", "tensor"),
                P("section", "tensor"),
                P("section", "tensor", "ctx"),
            ),
            out_specs=(
                P("section", None, "ctx", None),
                P("section", None, "ctx", None),
                P("section", None),
                P("section", "ctx", None, "tensor"),
                P("section", "ctx", None),
                P("section", "ctx", "tensor"),
                P("section", None, "tensor"),
                P("section", "tensor"),
                P("section", None, None),
                P("section", None),
                P("section", "tensor"),
                P("section", "tensor"),
                P("section", "tensor"),
                P("section", "tensor"),
                P("section", "tensor", "ctx"),
            ),
            check_vma=False,
        )(*args)

    return step
```
